32 devices in a mesh: clip: 8 (over z, core), row: 4 (over y, x).
Axes of the slice: x: 2, y: 2, z: 4, core: 2. Of those that a mesh axis runs over, the one named last changes fastest.
Arguments:
- latents: float32 [8, 9, 8, 16, 128], P('clip', None, 'row'), may hold values from -6 to 6
- noise: float32 [8, 9, 8, 16, 128], P('clip', None, 'row'), may hold values from -6 to 6
- levels: int32 [8, 9], P('clip'), may hold values from 0 to 999
- w_patch: float32 [128, 1024], P('clip'), may hold values from -0.5 to 0.5
- w_level: float32 [256, 1024], P('clip', 'row'), may hold values from -0.375 to 0.375
- w_adapt: float32 [1024, 8192], P('row', 'clip'), may hold values from -0.1875 to 0.1875
- w_project: float32 [1024, 3, 1024], P('clip', None, 'row'), may hold values from -0.1875 to 0.1875
- w_output: float32 [1024, 1024], P('row', 'clip'), may hold values from -1.5 to 1.5
- w_gateup: float32 [1024, 2, 4096], P('clip', None, 'row'), may hold values from -0.1875 to 0.1875
- w_down: float32 [4096, 1024], P('row', 'clip'), may hold values from -0.09375 to 0.09375
- w_head: float32 [1024, 128], P('clip'), may hold values from -0.1875 to 0.1875
- first_patch: float32 [128, 1024], P('clip'), may hold values from -2.3841858e-07 to 2.3841858e-07
- first_level: float32 [256, 1024], P('clip', 'row'), may hold values from -2.3841858e-07 to 2.3841858e-07
- first_adapt: float32 [1024, 8192], P('row', 'clip'), may hold values from -2.3841858e-07 to 2.3841858e-07
- first_project: float32 [1024, 3, 1024], P('clip', None, 'row'), may hold values from -2.3841858e-07 to 2.3841858e-07
- first_output: float32 [1024, 1024], P('row', 'clip'), may hold values from -2.3841858e-07 to 2.3841858e-07
- first_gateup: float32 [1024, 2, 4096], P('clip', None, 'row'), may hold values from -2.3841858e-07 to 2.3841858e-07
- first_down: float32 [4096, 1024], P('row', 'clip'), may hold values from -2.3841858e-07 to 2.3841858e-07
- first_head: float32 [1024, 128], P('clip'), may hold values from -2.3841858e-07 to 2.3841858e-07
- second_patch: float32 [128, 1024], P('clip'), may hold values from 8.189922e-15 to 3.2759687e-14
- second_level: float32 [256, 1024], P('clip', 'row'), may hold values from 8.189922e-15 to 3.2759687e-14
- second_adapt: float32 [1024, 8192], P('row', 'clip'), may hold values from 8.189922e-15 to 3.2759687e-14
- second_project: float32 [1024, 3, 1024], P('clip', None, 'row'), may hold values from 8.189922e-15 to 3.2759687e-14
- second_output: float32 [1024, 1024], P('row', 'clip'), may hold values from 8.189922e-15 to 3.2759687e-14
- second_gateup: float32 [1024, 2, 4096], P('clip', None, 'row'), may hold values from 1.0276328e-15 to 4.094961e-15
- second_down: float32 [4096, 1024], P('row', 'clip'), may hold values from 8.189922e-15 to 3.2759687e-14
- second_head: float32 [1024, 128], P('clip'), may hold values from 8.189922e-15 to 3.2759687e-14
Outputs:
- loss_sum: float32 [], replicated
- weight_sum: float32 [], replicated
- grad_norm: float32 [], replicated
- new_patch: float32 [128, 1024], P('clip')
- new_level: float32 [256, 1024], P('clip', 'row')
- new_adapt: float32 [1024, 8192], P('row', 'clip')
- new_project: float32 [1024, 3, 1024], P('clip', None, 'row')
- new_output: float32 [1024, 1024], P('row', 'clip')
- new_gateup: float32 [1024, 2, 4096], P('clip', None, 'row')
- new_down: float32 [4096, 1024], P('row', 'clip')
- new_head: float32 [1024, 128], P('clip')
- mean_patch: float32 [128, 1024], P('clip')
- mean_level: float32 [256, 1024], P('clip', 'row')
- mean_adapt: float32 [1024, 8192], P('row', 'clip')
- mean_project: float32 [1024, 3, 1024], P('clip', None, 'row')
- mean_output: float32 [1024, 1024], P('row', 'clip')
- mean_gateup: float32 [1024, 2, 4096], P('clip', None, 'row')
- mean_down: float32 [4096, 1024], P('row', 'clip')
- mean_head: float32 [1024, 128], P('clip')
- square_patch: float32 [128, 1024], P('clip')
- square_level: float32 [256, 1024], P('clip', 'row')
- square_adapt: float32 [1024, 8192], P('row', 'clip')
- square_project: float32 [1024, 3, 1024], P('clip', None, 'row')
- square_output: float32 [1024, 1024], P('row', 'clip')
- square_gateup: float32 [1024, 2, 4096], P('clip', None, 'row')
- square_down: float32 [4096, 1024], P('row', 'clip')
- square_head: float32 [1024, 128], P('clip')
The draws below stay inside these ranges and needn't reach their ends.
All inputs are finite; a program needn't handle non-finite values.
Results may differ from the reference program's by a relative error of at most 0.0094.
Values may be sent and summed in bfloat16 or wider, within the bound.
A program may use at most 192 MiB of HBM per device.

```python
import math
import jax
import jax.numpy as jnp
from jax import lax

D = 1024
HEADS = 16
HSIZE = 64
FF = 4096
PF = 128
TF = 256
FRAMES = 9
PCOLS = 16
LEVELS = 1000
STEP = 3
CLIPS = 8
PROWS = 8
PARAMS = 25690112


def place_ends(values, key, low, high):
    shape = values.shape
    place = [jax.random.randint(jax.random.fold_in(key, axis), (), 0, shape[axis]) for axis in range(len(shape))]
    values = values.at[tuple(place)].set(low)
    longest = shape.index(max(shape))
    place[longest] = (place[longest] + 1) % shape[longest]
    return values.at[tuple(place)].set(high)


def block_levels(own_key, dims, shards, low, high):
    gain = 1.0
    for position, parts in shards:
        steps = jax.random.uniform(jax.random.fold_in(jax.random.fold_in(own_key, 6), position), (parts,), jnp.float32, low / len(shards), high / len(shards))
        gain = gain * jnp.repeat(jnp.exp(steps), dims[position] // parts).reshape((-1,) + (1,) * (len(dims) - 1 - position))
    return gain


def centred(own_key, dims, scale, limit, pieces=(), kind=jnp.bfloat16):
    loudness = block_levels(own_key, dims, pieces, -0.22, 0.18) if pieces else 1.0
    entries = jax.random.normal(own_key, dims, jnp.float32) * scale * loudness
    return jnp.minimum(jnp.maximum(entries, -limit), limit).astype(kind)


def setup_inputs(seed: int = 0) -> dict:
    streams_of = jax.random.split(jax.random.key(seed), 28)
    return {
        "latents": centred(streams_of[0], (CLIPS, FRAMES, PROWS, PCOLS, PF), 1.0, 6.0, ((0, 8), (2, 4)), jnp.float32),
        "noise": centred(streams_of[1], (CLIPS, FRAMES, PROWS, PCOLS, PF), 1.0, 6.0, ((0, 8), (2, 4)), jnp.float32),
        "levels": place_ends(jax.random.randint(streams_of[2], (CLIPS, FRAMES), 0, LEVELS), jax.random.fold_in(streams_of[2], 1), 0, LEVELS - 1).astype(jnp.int32),
        "w_patch": centred(streams_of[3], (PF, D), PF ** -0.5, 0.5, ((0, 8),), jnp.float32),
        "w_level": centred(streams_of[4], (TF, D), TF ** -0.5, 0.375, ((0, 8), (1, 4)), jnp.float32),
        "w_adapt": centred(streams_of[5], (D, 8 * D), D ** -0.5, 0.1875, ((0, 4), (1, 8)), jnp.float32),
        "w_project": centred(streams_of[6], (D, 3, D), D ** -0.5, 0.1875, ((0, 8), (2, 4)), jnp.float32),
        "w_output": centred(streams_of[7], (D, D), (D // 64) ** -0.5, 1.5, ((0, 4), (1, 8)), jnp.float32),
        "w_gateup": centred(streams_of[8], (D, 2, FF), D ** -0.5, 0.1875, ((0, 8), (2, 4)), jnp.float32),
        "w_down": centred(streams_of[9], (FF, D), FF ** -0.5, 0.09375, ((0, 4), (1, 8)), jnp.float32),
        "w_head": centred(streams_of[10], (D, PF), D ** -0.5, 0.1875, ((0, 8),), jnp.float32),
        "first_patch": centred(streams_of[11], (PF, D), (0.111 * 0.002 * PARAMS ** -0.5), 2.384185791015625e-07, ((0, 8),), jnp.float32),
        "first_level": centred(streams_of[12], (TF, D), (0.111 * 0.002 * PARAMS ** -0.5), 2.384185791015625e-07, ((0, 8), (1, 4)), jnp.float32),
        "first_adapt": centred(streams_of[13], (D, 8 * D), (0.111 * 0.002 * PARAMS ** -0.5), 2.384185791015625e-07, ((0, 4), (1, 8)), jnp.float32),
        "first_project": centred(streams_of[14], (D, 3, D), (0.111 * 0.002 * PARAMS ** -0.5), 2.384185791015625e-07, ((0, 8), (2, 4)), jnp.float32),
        "first_output": centred(streams_of[15], (D, D), (0.111 * 0.002 * PARAMS ** -0.5), 2.384185791015625e-07, ((0, 4), (1, 8)), jnp.float32),
        "first_gateup": centred(streams_of[16], (D, 2, FF), (0.111 * 0.002 * PARAMS ** -0.5), 2.384185791015625e-07, ((0, 8), (2, 4)), jnp.float32),
        "first_down": centred(streams_of[17], (FF, D), (0.111 * 0.002 * PARAMS ** -0.5), 2.384185791015625e-07, ((0, 4), (1, 8)), jnp.float32),
        "first_head": centred(streams_of[18], (D, PF), (0.111 * 0.002 * PARAMS ** -0.5), 2.384185791015625e-07, ((0, 8),), jnp.float32),
        "second_patch": jnp.clip(jnp.exp(math.log(3.2759687025813236e-14) - 1.3862944 * jax.random.uniform(streams_of[19], (PF, D), jnp.float32) ** block_levels(streams_of[19], (PF, D), ((0, 8),), -0.2, 0.2)), 8.189921756453309e-15, 3.2759687025813236e-14),
        "second_level": jnp.clip(jnp.exp(math.log(3.2759687025813236e-14) - 1.3862944 * jax.random.uniform(streams_of[20], (TF, D), jnp.float32) ** block_levels(streams_of[20], (TF, D), ((0, 8), (1, 4)), -0.2, 0.2)), 8.189921756453309e-15, 3.2759687025813236e-14),
        "second_adapt": jnp.clip(jnp.exp(math.log(3.2759687025813236e-14) - 1.3862944 * jax.random.uniform(streams_of[21], (D, 8 * D), jnp.float32) ** block_levels(streams_of[21], (D, 8 * D), ((0, 4), (1, 8)), -0.2, 0.2)), 8.189921756453309e-15, 3.2759687025813236e-14),
        "second_project": jnp.clip(jnp.exp(math.log(3.2759687025813236e-14) - 1.3862944 * jax.random.uniform(streams_of[22], (D, 3, D), jnp.float32) ** block_levels(streams_of[22], (D, 3, D), ((0, 8), (2, 4)), -0.2, 0.2)), 8.189921756453309e-15, 3.2759687025813236e-14),
        "second_output": jnp.clip(jnp.exp(math.log(3.2759687025813236e-14) - 1.3862944 * jax.random.uniform(streams_of[23], (D, D), jnp.float32) ** block_levels(streams_of[23], (D, D), ((0, 4), (1, 8)), -0.2, 0.2)), 8.189921756453309e-15, 3.2759687025813236e-14),
        "second_gateup": jnp.clip(jnp.exp(math.log(4.0949608782266545e-15) - 1.3824993 * jax.random.uniform(streams_of[24], (D, 2, FF), jnp.float32) ** block_levels(streams_of[24], (D, 2, FF), ((0, 8), (2, 4)), -0.2, 0.2)), 1.0276327594657708e-15, 4.0949608782266545e-15),
        "second_down": jnp.clip(jnp.exp(math.log(3.2759687025813236e-14) - 1.3862944 * jax.random.uniform(streams_of[25], (FF, D), jnp.float32) ** block_levels(streams_of[25], (FF, D), ((0, 4), (1, 8)), -0.2, 0.2)), 8.189921756453309e-15, 3.2759687025813236e-14),
        "second_head": jnp.clip(jnp.exp(math.log(3.2759687025813236e-14) - 1.3862944 * jax.random.uniform(streams_of[26], (D, PF), jnp.float32) ** block_levels(streams_of[26], (D, PF), ((0, 8),), -0.2, 0.2)), 8.189921756453309e-15, 3.2759687025813236e-14),
    }


@jax.custom_vjp
def low(v):
    return lax.optimization_barrier(v.astype(jnp.bfloat16)).astype(jnp.float32)

@jax.custom_vjp
def low_back(v):
    return v

def low_keep(v):
    return (low(v), None)

def low_pass(kept, grad):
    return (grad,)

def back_keep(v):
    return (v, None)

def back_low(kept, grad):
    return (low(grad),)
low.defvjp(low_keep, low_pass)
low_back.defvjp(back_keep, back_low)
norm_eps = 1e-06
clip_level = 0.002
learn_rate = 0.03
beta_one = 0.9
beta_two = 0.95
decay_rate = 0.1
adam_eps = 1e-08

def matmul(left, right):
    return jnp.dot(left, right, precision=lax.Precision.HIGHEST)

def frequencies(number):
    return jnp.exp(-math.log(10000.0) * jnp.arange(number, dtype=jnp.float32) / number)

def rotary_tables(frames, row_count, col_count, row_offset, half):
    frame_part = half // 4
    row_part = 3 * half // 8
    col_part = half - frame_part - row_part
    frame_pos = jnp.arange(frames, dtype=jnp.float32)
    row_pos = jnp.arange(row_count, dtype=jnp.float32) + row_offset
    col_pos = jnp.arange(col_count, dtype=jnp.float32)
    shape = (frames, row_count, col_count)
    angle = jnp.concatenate([jnp.broadcast_to(frame_pos[:, None, None, None] * frequencies(frame_part), shape + (frame_part,)), jnp.broadcast_to(row_pos[None, :, None, None] * frequencies(row_part), shape + (row_part,)), jnp.broadcast_to(col_pos[None, None, :, None] * frequencies(col_part), shape + (col_part,))], -1)
    angle = angle.reshape(frames, row_count * col_count, 1, half)
    return (jnp.cos(angle), jnp.sin(angle))

def rotate(values, cosine, sine):
    half = values.shape[-1] // 2
    first_half = values[..., :half]
    second_half = values[..., half:]
    return jnp.concatenate([first_half * cosine - second_half * sine, first_half * sine + second_half * cosine], -1)

def modulate(stream, shift, scale):
    centre = stream - lax.optimization_barrier(jnp.mean(stream, -1, keepdims=True))
    spread = lax.optimization_barrier(jnp.mean(centre * centre, -1, keepdims=True))
    return centre * lax.rsqrt(spread + norm_eps) * (1.0 + scale) + shift

def noise_plan(levels):
    ratio = levels.astype(jnp.float32) / LEVELS
    alpha_bar = jnp.cos((ratio + 0.008) / 1.008 * (math.pi / 2)) ** 2
    weight = jnp.minimum(1.0, 5.0 * (1.0 - alpha_bar) / alpha_bar)
    return (alpha_bar, weight)

def level_embedding(levels, half):
    angle = levels.astype(jnp.float32)[..., None] * frequencies(half)
    return jnp.concatenate([jnp.cos(angle), jnp.sin(angle)], -1)

def attention_ref(query, key, value):
    per_frame = PROWS * PCOLS
    key_frame = jnp.arange(FRAMES * per_frame, dtype=jnp.int32) // per_frame

    def block(frame):
        query_block = lax.dynamic_slice_in_dim(query, (frame * per_frame).astype(jnp.int32), per_frame, 0)
        scores = low_back(jnp.einsum('qhe,khe->hqk', query_block, key, precision=lax.Precision.HIGHEST))
        allowed = (key_frame <= frame)[None, None, :]
        scores = jnp.where(allowed, scores, -1e+30)
        row_max = lax.optimization_barrier(jnp.max(scores, -1, keepdims=True))
        exponent = jnp.where(allowed, jnp.exp(scores - row_max), 0.0)
        row_total = lax.optimization_barrier(jnp.sum(exponent, -1))
        mixed = jnp.einsum('hqk,khe->qhe', low(exponent), value, precision=lax.Precision.HIGHEST)
        return mixed / jnp.transpose(row_total)[:, :, None]
    result = lax.map(jax.checkpoint(block), jnp.arange(FRAMES, dtype=jnp.int32))
    return result.reshape(FRAMES * per_frame, HEADS * HSIZE)

def forward(params, latent_clip, noise_clip, level_clip):
    w_patch, w_level, w_adapt, w_project, w_output, w_gateup, w_down, w_head = [low(weight) for weight in params]
    w_project = w_project.reshape(D, 3 * D)
    w_gateup = w_gateup.reshape(D, 2 * FF)
    per_frame = PROWS * PCOLS
    tokens = FRAMES * per_frame
    alpha_bar, weight = noise_plan(level_clip)
    noisy = jnp.sqrt(alpha_bar)[:, None, None] * latent_clip + jnp.sqrt(1.0 - alpha_bar)[:, None, None] * noise_clip
    inputs = low(noisy).reshape(tokens, PF)
    embedded = low(level_embedding(level_clip, TF // 2))
    level_pre = low_back(matmul(embedded, w_level))
    condition = low(jax.nn.silu(level_pre))
    adapt = low_back(matmul(condition, w_adapt)).reshape(FRAMES, 8, 1, D)
    stream = low_back(matmul(inputs, w_patch)).reshape(FRAMES, per_frame, D)
    normed_one = low(modulate(stream, adapt[:, 0], adapt[:, 1])).reshape(tokens, D)
    projected = low_back(matmul(normed_one, w_project)).reshape(FRAMES, per_frame, 3, HEADS, HSIZE)
    cosine, sine = rotary_tables(FRAMES, PROWS, PCOLS, 0.0, HSIZE // 2)
    query = low(rotate(projected[:, :, 0], cosine, sine) * HSIZE ** (-0.5)).reshape(tokens, HEADS, HSIZE)
    key = low(rotate(projected[:, :, 1], cosine, sine)).reshape(tokens, HEADS, HSIZE)
    value = low(projected[:, :, 2]).reshape(tokens, HEADS, HSIZE)
    attended = low_back(low(attention_ref(query, key, value)))
    branch = low_back(matmul(attended, w_output)).reshape(FRAMES, per_frame, D)
    stream_mid = stream + adapt[:, 2] * branch
    normed_two = low(modulate(stream_mid, adapt[:, 3], adapt[:, 4])).reshape(tokens, D)
    gate_up = low_back(matmul(normed_two, w_gateup))
    active = low(jax.nn.gelu(gate_up[:, :FF]) * gate_up[:, FF:])
    feed = low_back(matmul(active, w_down)).reshape(FRAMES, per_frame, D)
    stream_top = stream_mid + adapt[:, 5] * feed
    normed_end = low(modulate(stream_top, adapt[:, 6], adapt[:, 7])).reshape(tokens, D)
    predicted = low_back(matmul(normed_end, w_head)).reshape(FRAMES, per_frame, PF)
    missed = predicted - noise_clip
    return jnp.sum(weight[:, None] * lax.optimization_barrier(jnp.mean(missed * missed, -1)))

def adam_update(master, first, second, grad):
    first_new = beta_one * first + (1.0 - beta_one) * grad
    second_new = beta_two * second + (1.0 - beta_two) * grad * grad
    first_hat = first_new / (1.0 - beta_one ** STEP)
    second_hat = second_new / (1.0 - beta_two ** STEP)
    master_new = master - learn_rate * (first_hat / (jnp.sqrt(second_hat) + adam_eps) + decay_rate * master)
    return (master_new, first_new, second_new)

def reference(latents, noise, levels, w_patch, w_level, w_adapt, w_project, w_output, w_gateup, w_down, w_head, first_patch, first_level, first_adapt, first_project, first_output, first_gateup, first_down, first_head, second_patch, second_level, second_adapt, second_project, second_output, second_gateup, second_down, second_head):
    params = (w_patch, w_level, w_adapt, w_project, w_output, w_gateup, w_down, w_head)
    firsts = (first_patch, first_level, first_adapt, first_project, first_output, first_gateup, first_down, first_head)
    seconds = (second_patch, second_level, second_adapt, second_project, second_output, second_gateup, second_down, second_head)
    per_frame = PROWS * PCOLS

    def clip_step(running, inputs):
        latent_clip, noise_clip, level_clip = inputs
        latent_flat = latent_clip.reshape(FRAMES, per_frame, PF)
        noise_flat = noise_clip.reshape(FRAMES, per_frame, PF)
        value, pull = jax.vjp(lambda weights: forward(weights, latent_flat, noise_flat, level_clip), params)
        grads = pull(jnp.ones_like(value))[0]
        return ((running[0] + value, jax.tree.map(jnp.add, running[1], grads)), None)
    initial = (jnp.zeros((), jnp.float32), jax.tree.map(jnp.zeros_like, params))
    (loss_sum, grads), unused = lax.scan(clip_step, initial, (latents, noise, levels))
    weight_sum = jnp.sum(noise_plan(levels)[1]) * per_frame
    grads = [grad / weight_sum for grad in grads]
    grad_norm = jnp.sqrt(sum((jnp.sum(grad * grad) for grad in grads)))
    factor = jnp.minimum(1.0, clip_level / (grad_norm + 1e-06))
    results = [adam_update(master, first, second, grad * factor) for master, first, second, grad in zip(params, firsts, seconds, grads)]
    news = [item[0] for item in results]
    means = [item[1] for item in results]
    squares = [item[2] for item in results]
    return (loss_sum, weight_sum, grad_norm, news[0], news[1], news[2], news[3], news[4], news[5], news[6], news[7], means[0], means[1], means[2], means[3], means[4], means[5], means[6], means[7], squares[0], squares[1], squares[2], squares[3], squares[4], squares[5], squares[6], squares[7])
```

```python
import functools
import math
import types

import jax
import jax.numpy as jnp
import numpy as np
from jax import lax
from jax.experimental import pallas as pl
from jax.experimental.pallas import tpu as pltpu
from jax.sharding import PartitionSpec as P

D = 1024
HEADS = 16
HSIZE = 64
TF = 256
LEVELS = 1000
STEP = 3
VECTORS = 8
PAD = 16

norm_eps = 1e-06
clip_level = 0.002
learn_rate = 0.03
beta_one = 0.9
beta_two = 0.95
decay_rate = 0.1
adam_eps = 1e-08

MESH = pl.DeviceIdType.MESH
f32 = jnp.float32
bf16 = jnp.bfloat16


def dot_nn(left, right):
    return jnp.dot(left, right, preferred_element_type=f32)


def dot_nt(left, right):
    return lax.dot_general(left, right, (((1,), (1,)), ((), ())), preferred_element_type=f32)


def dot_tn(left, right):
    return lax.dot_general(left, right, (((0,), (0,)), ((), ())), preferred_element_type=f32)


def frequencies(number):
    return jnp.exp(-math.log(10000.0) * jnp.arange(number, dtype=f32) / number)


def noise_plan(levels):
    ratio = levels.astype(f32) / LEVELS
    alpha_bar = jnp.cos((ratio + 0.008) / 1.008 * (math.pi / 2)) ** 2
    weight = jnp.minimum(1.0, 5.0 * (1.0 - alpha_bar) / alpha_bar)
    return (alpha_bar, weight)


def level_embedding(levels, half):
    angle = levels.astype(f32)[..., None] * frequencies(half)
    return jnp.concatenate([jnp.cos(angle), jnp.sin(angle)], -1)


def sizes_of(latents, clips, parts):
    z = types.SimpleNamespace()
    z.C, z.R = clips, parts
    z.F = latents.shape[1]
    z.rows, z.cols, z.PF = latents.shape[2], latents.shape[3], latents.shape[4]
    z.LT = z.rows * z.cols
    z.N = 3 if z.F % 3 == 0 else 1
    z.CF = z.F // z.N
    z.CT = z.CF * z.LT
    z.W = z.R * z.CT
    z.T = z.F * z.LT
    z.HD = HEADS // parts
    z.HW = z.HD * HSIZE
    z.FH = 4 * D // parts
    z.DR = D // clips
    z.LR = TF // clips
    z.LW = D // parts
    z.AW = VECTORS * D // clips
    z.aw = z.AW // parts
    return z


def rotary_consts(z):
    half = HSIZE // 2
    fp = half // 4
    rp = 3 * half // 8
    cp = half - fp - rp

    def freq(n):
        return np.exp(-math.log(10000.0) * np.arange(n, dtype=np.float32) / np.float32(n)).astype(np.float32)

    shape = (z.N, z.R, z.CF, z.rows, z.cols)
    frame = (np.arange(z.N)[:, None] * z.CF + np.arange(z.CF)[None, :]).astype(np.float32)
    frame = np.broadcast_to(frame[:, None, :, None, None], shape)
    prow = (np.arange(z.R)[:, None] * z.rows + np.arange(z.rows)[None, :]).astype(np.float32)
    prow = np.broadcast_to(prow[None, :, None, :, None], shape)
    pcol = np.broadcast_to(np.arange(z.cols, dtype=np.float32), shape)
    angle = np.concatenate(
        [frame[..., None] * freq(fp), prow[..., None] * freq(rp), pcol[..., None] * freq(cp)], -1
    ).astype(np.float32)
    angle = angle.reshape(z.N, z.W, half)
    cos, sin = np.cos(angle), np.sin(angle)
    return np.concatenate([cos, cos, sin, sin], -1).astype(np.float32)


def remote(src, dst, send_sem, recv_sem, device):
    return pltpu.make_async_remote_copy(
        src_ref=src, dst_ref=dst, send_sem=send_sem, recv_sem=recv_sem, device_id=device, device_id_type=MESH
    )


def place(n, z):
    n.clip = lax.axis_index("clip")
    n.row = lax.axis_index("row")
    n.sib = n.clip + 1 - 2 * (n.clip % 2)
    n.row_peer = [(n.row + k) % z.R for k in range(1, z.R)]
    n.clip_peer = [(n.clip + k) % z.C for k in range(1, z.C)]
    n.square = z.R == 4
    n.far = (n.row + 1 - 2 * (n.row % 2) + 2) % z.R
    n.x = (n.clip, n.row + 1 - 2 * (n.row % 2))
    n.y = (n.clip, (n.row + 2) % z.R)
    n.arrivals = 2 if n.square else z.R - 1
    n.line = z.C == 8
    place = n.clip // 2
    n.inner = jnp.logical_or(place == 1, place == 2)
    n.far_end = jnp.where(n.inner, n.clip + 4 - 8 * (place // 2), n.clip)
    n.near_end = jnp.where(n.inner, n.clip - 2 + 4 * (place // 2), n.clip)
    n.core_peer = [(n.clip + 2 * k) % z.C for k in range(1, z.C // 2)]


def enter(n, z):
    barrier = pltpu.get_barrier_semaphore()
    for p in n.row_peer:
        pl.semaphore_signal(barrier, inc=1, device_id=(n.clip, p), device_id_type=MESH)
    for p in n.clip_peer:
        pl.semaphore_signal(barrier, inc=1, device_id=(p, n.row), device_id_type=MESH)
    pl.semaphore_wait(barrier, z.R + z.C - 2)


def send(src, dst, sems, slot, land, device):
    remote(src, dst, sems.at[(0,) + slot], sems.at[(1,) + land], device).start()


def sent(ref, sems, slot, device):
    remote(ref, ref, sems.at[(0,) + slot], sems.at[(1,) + slot], device).wait_send()


def got(ref, sems, slot, device):
    remote(ref, ref, sems.at[(0,) + slot], sems.at[(1,) + slot], device).wait_recv()


def halves(n, ref, c, p):
    rows = ref.shape[2] // 2
    return ref.at[c, p, :rows], ref.at[c, p, rows:]


def gather_row(n, full, sems, c):
    mine = full.at[c, n.row]
    if n.square:
        send(mine, mine, sems, (c, 0), (c, 0), n.x)
        send(mine, mine, sems, (c, 1), (c, 1), n.y)
        return
    for k, p in enumerate(n.row_peer):
        back = len(n.row_peer) - 1 - k
        send(mine, mine, sems, (c, k), (c, back), (n.clip, p))


def gather_more(n, full, sems, c):
    if n.square:
        got(full.at[c, n.x[1]], sems, (c, 0), n.x)
        block = halves(n, full, c, n.x[1])[0]
        send(block, block, sems, (c, 2), (c, 2), n.y)
        got(full.at[c, n.y[1]], sems, (c, 1), n.y)
        block = halves(n, full, c, n.y[1])[1]
        send(block, block, sems, (c, 3), (c, 3), n.x)


def gather_row_wait(n, full, sems, c):
    if n.square:
        low, high = halves(n, full, c, n.far)
        got(low, sems, (c, 2), n.y)
        got(high, sems, (c, 3), n.x)
        mine = full.at[c, n.row]
        sent(mine, sems, (c, 0), n.x)
        sent(mine, sems, (c, 1), n.y)
        sent(low, sems, (c, 2), n.y)
        sent(high, sems, (c, 3), n.x)
        return
    for k, p in enumerate(n.row_peer):
        block = full.at[c, p]
        got(block, sems, (c, k), (n.clip, p))
        sent(block, sems, (c, k), (n.clip, p))


def scatter_row(n, parts, landed, sems, c):
    if n.square:
        (xl, _), (_, yh), (fl, fh) = (halves(n, parts, c, p) for p in (n.x[1], n.y[1], n.far))
        send(fl, halves(n, landed, c, 2)[0], sems, (c, 0), (c, 0), n.x)
        send(fh, halves(n, landed, c, 2)[1], sems, (c, 1), (c, 1), n.y)
        send(xl, halves(n, landed, c, 0)[0], sems, (c, 2), (c, 2), n.x)
        send(yh, halves(n, landed, c, 1)[1], sems, (c, 3), (c, 3), n.y)
        return
    for k, p in enumerate(n.row_peer):
        back = len(n.row_peer) - 1 - k
        send(parts.at[c, p], landed.at[c, back], sems, (c, k), (c, back), (n.clip, p))


def scatter_more(n, parts, landed, sems, c):
    if n.square:
        rows = parts.shape[2] // 2
        low, high = halves(n, landed, c, 2)
        got(low, sems, (c, 0), n.x)
        parts[c, n.y[1], :rows] = (parts[c, n.y[1], :rows].astype(f32) + low[...].astype(f32)).astype(bf16)
        send(halves(n, parts, c, n.y[1])[0], halves(n, landed, c, 1)[0], sems, (c, 5), (c, 5), n.y)
        got(high, sems, (c, 1), n.y)
        parts[c, n.x[1], rows:] = (parts[c, n.x[1], rows:].astype(f32) + high[...].astype(f32)).astype(bf16)
        send(halves(n, parts, c, n.x[1])[1], halves(n, landed, c, 0)[1], sems, (c, 4), (c, 4), n.x)


def scatter_row_wait(n, parts, landed, sems, c):
    if n.square:
        (xl, xh), (yl, yh) = (halves(n, landed, c, k) for k in range(2))
        for slot, ref, peer in ((2, xl, n.x), (3, yh, n.y), (4, xh, n.x), (5, yl, n.y)):
            got(ref, sems, (c, slot), peer)
        for slot in range(6):
            sent(xl, sems, (c, slot), n.x)
        return
    for k, p in enumerate(n.row_peer):
        got(landed.at[c, k], sems, (c, k), (n.clip, p))
        sent(landed.at[c, k], sems, (c, k), (n.clip, p))


def share_row(n, buf, sems):
    for k, p in enumerate(n.row_peer):
        mine = buf.at[n.row]
        remote(mine, mine, sems.at[0, k], sems.at[1, n.row], (n.clip, p)).start()


def share_row_wait(n, buf, sems):
    for k, p in enumerate(n.row_peer):
        block = buf.at[p]
        remote(block, block, sems.at[0, k], sems.at[1, p], (n.clip, p)).wait()


def swap_row(n, src, dst, sems):
    for k, p in enumerate(n.row_peer):
        remote(src.at[p], dst.at[n.row], sems.at[0, k], sems.at[1, n.row], (n.clip, p)).start()


def swap_row_wait(n, src, dst, sems):
    for k, p in enumerate(n.row_peer):
        remote(src.at[p], dst.at[p], sems.at[0, k], sems.at[1, p], (n.clip, p)).wait()


def share_clip(n, buf, sems):
    for k, p in enumerate(n.clip_peer):
        mine = buf.at[n.clip]
        remote(mine, mine, sems.at[0, k], sems.at[1, n.clip], (p, n.row)).start()


def share_clip_wait(n, buf, sems):
    for k, p in enumerate(n.clip_peer):
        block = buf.at[p]
        remote(block, block, sems.at[0, k], sems.at[1, p], (p, n.row)).wait()


def swap_clip(n, src, dst, sems):
    for k, p in enumerate(n.clip_peer):
        remote(src.at[p], dst.at[n.clip], sems.at[0, k], sems.at[1, n.clip], (p, n.row)).start()


def swap_clip_wait(n, src, dst, sems):
    for k, p in enumerate(n.clip_peer):
        remote(src.at[p], dst.at[p], sems.at[0, k], sems.at[1, p], (p, n.row)).wait()


def skipped(n, z, p, relayed):
    if not relayed or not n.line:
        return None
    return jnp.logical_and(n.clip // 2 + p // 2 == 3, jnp.logical_not(n.inner))


def unless(skip, work):
    if skip is None:
        work()
    else:
        pl.when(jnp.logical_not(skip))(work)


def weight_send(n, z, buf, sems, relayed=False):
    mine = buf.at[n.clip]
    remote(mine, mine, sems.at[0, 0], sems.at[1, n.clip], (n.sib, n.row)).start()
    for k, p in enumerate(n.core_peer):
        copy = remote(mine, mine, sems.at[0, 1 + k], sems.at[1, n.clip], (p, n.row))
        unless(skipped(n, z, p, relayed), copy.start)


def weight_relay(n, z, buf, sems):
    if n.line:

        @pl.when(n.inner)
        def _():
            block = buf.at[n.far_end]
            remote(block, block, sems.at[0, 0], sems.at[1, n.far_end], (n.far_end, n.row)).wait_recv()
            remote(block, block, sems.at[0, z.C - 1], sems.at[1, n.far_end], (n.near_end, n.row)).start()


def weight_forward(n, z, buf, sems, relayed=False):
    for k, p in enumerate(n.core_peer):
        block = buf.at[p]
        known = jnp.logical_and(n.inner, p == n.far_end) if relayed and n.line else None
        unless(known, remote(block, block, sems.at[0, 1 + k], sems.at[1, p], (p, n.row)).wait_recv)
        remote(block, block, sems.at[0, z.C // 2 + k], sems.at[1, p], (n.sib, n.row)).start()


def weight_wait(n, z, buf, sems, relayed=False):
    block = buf.at[n.sib]
    remote(block, block, sems.at[0, 0], sems.at[1, n.sib], (n.sib, n.row)).wait()
    for k, p in enumerate(n.core_peer):
        j = (p // 2) * 2 + n.sib % 2
        block = buf.at[j]
        remote(block, block, sems.at[0, 1 + k], sems.at[1, j], (n.sib, n.row)).wait_recv()
        unless(skipped(n, z, p, relayed), remote(block, block, sems.at[0, 1 + k], sems.at[1, j], (n.sib, n.row)).wait_send)
        remote(block, block, sems.at[0, z.C // 2 + k], sems.at[1, j], (n.sib, n.row)).wait_send()
    if relayed and n.line:
        pl.when(n.inner)(remote(block, block, sems.at[0, z.C - 1], sems.at[1, n.sib], (n.sib, n.row)).wait_send)


def flat(x):
    return x.reshape((-1, x.shape[-1]))


def normed(x):
    centre = x - jnp.mean(x, -1, keepdims=True)
    rstd = lax.rsqrt(jnp.mean(centre * centre, -1, keepdims=True) + norm_eps)
    return centre * rstd, rstd


def norm_pull(n_hat, rstd, scale, grad):
    d_shift = jnp.sum(grad, 0, keepdims=True)
    d_scale = jnp.sum(grad * n_hat, 0, keepdims=True)
    dn = grad * (1.0 + scale)
    dx = rstd * (dn - jnp.mean(dn, -1, keepdims=True) - n_hat * jnp.mean(dn * n_hat, -1, keepdims=True))
    return dx, d_shift, d_scale


def vec(n, which, frame):
    return n.mod[which, pl.ds(frame, 1), :]


def frame_rows(z, c, i):
    return pl.ds(pl.multiple_of((c * z.CF + i) * z.LT, z.LT), z.LT)


def tables(n, c):
    x = n.tab[c]
    lane = lax.broadcasted_iota(jnp.int32, x.shape, 1)
    y = pltpu.roll(x, 64, 1)
    sin = jnp.where(lane < 64, y, x)
    return jnp.where(lane < 64, x, y), jnp.where(lane % HSIZE < HSIZE // 2, -sin, sin)


def turn(x, cos, sin):
    lane = lax.broadcasted_iota(jnp.int32, x.shape, 1)
    other = jnp.where(lane % HSIZE < HSIZE // 2, pltpu.roll(x, 128 - HSIZE // 2, 1), pltpu.roll(x, HSIZE // 2, 1))
    return x * cos + other * sin


def gelu_parts(x):
    k = math.sqrt(2.0 / math.pi)
    t = jnp.tanh(k * (x + 0.044715 * (x * x * x)))
    value = 0.5 * x * (1.0 + t)
    slope = 0.5 * (1.0 + t) + 0.5 * x * (1.0 - t * t) * (k * (1.0 + 3 * 0.044715 * (x * x)))
    return value, slope


def causal(z):
    a = (lax.broadcasted_iota(jnp.int32, (z.W, z.W), 0) % z.CT) // z.LT
    b = (lax.broadcasted_iota(jnp.int32, (z.W, z.W), 1) % z.CT) // z.LT
    return a, b


def after(z, c, more):
    if z.N > 1:
        pl.when(c > 0)(lambda: more(c - 1))


def last(z, c, more):
    if z.N > 1:
        pl.when(c == 0)(lambda: more(z.N - 1))


def phase_level(n, z):
    n.lv[n.clip] = n.w_level[...].astype(bf16)
    n.ea[n.clip] = n.emb[...]
    n.pt[n.clip] = n.w_patch[...]
    n.Wh[n.clip] = n.w_head[...].astype(bf16)
    enter(n, z)
    share_clip(n, n.ea, n.ea_s)
    share_clip(n, n.lv, n.lv_s)
    share_clip(n, n.pt, n.pt_s)
    for k in range(3):
        n.Wp[n.clip, :, k * z.HW : (k + 1) * z.HW] = n.wp[k].astype(bf16)
    n.Wo[n.clip] = jnp.transpose(n.wo[...]).astype(bf16)
    tiles = z.FH // 128
    for t in range(tiles):
        for k in range(2):
            at = k * z.FH + t * 128
            n.Wg[n.clip, :, at : at + 128] = n.wg[pl.ds(2 * t + k, z.DR, stride=2 * tiles), :].astype(bf16)
    n.Wd[n.clip] = jnp.transpose(n.wd[...]).astype(bf16)
    share_clip_wait(n, n.ea, n.ea_s)
    share_clip_wait(n, n.lv, n.lv_s)
    pre = dot_nn(flat(n.ea[...]), flat(n.lv[...]))
    n.pre[...] = pre
    cond = (pre * (1.0 / (1.0 + jnp.exp(-pre)))).astype(bf16)
    n.cond[...] = cond
    part = dot_nn(cond, n.w_adapt[...].astype(bf16))
    for p in range(z.R):
        n.pa[p] = part[:, p * z.aw : (p + 1) * z.aw]
    swap_row(n, n.pa, n.ra, n.ra_s)
    share_clip_wait(n, n.pt, n.pt_s)
    patch = flat(n.pt[...]).astype(bf16)
    for c in range(z.N):
        rows = slice(c * z.CT, (c + 1) * z.CT)
        n.stream[rows, :] = dot_nn(n.inputs[rows, :], patch)
    swap_row_wait(n, n.pa, n.ra, n.ra_s)
    total = n.pa[n.row]
    for p in n.row_peer:
        total = total + n.ra[p]
    n.rs[...] = total.reshape(z.C, PAD, z.aw)
    n.rb[n.clip] = n.rs[n.clip]
    swap_clip(n, n.rs, n.rb, n.rb_s)
    weight_send(n, z, n.Wp, n.Wp_s)
    swap_clip_wait(n, n.rs, n.rb, n.rb_s)
    n.ab[n.row] = n.rb[...]
    share_row(n, n.ab, n.ab_s)
    weight_send(n, z, n.Wo, n.Wo_s)
    share_clip(n, n.Wh, n.Wh_s)
    weight_send(n, z, n.Wg, n.Wg_s, True)
    weight_send(n, z, n.Wd, n.Wd_s)
    share_row_wait(n, n.ab, n.ab_s)
    for i in range(z.C):
        for r in range(z.R):
            col = i * z.AW + r * z.aw
            n.mod[col // D, :, col % D : col % D + z.aw] = n.ab[r, i]


def phase_one(n, z):
    def chunk(c, _):
        def frame(i, _):
            f = c * z.CF + i
            hat, unused = normed(n.stream[frame_rows(z, c, i), :])
            y = hat * (1.0 + vec(n, 1, f)) + vec(n, 0, f)
            n.one[c, n.row, pl.ds(pl.multiple_of(i * z.LT, z.LT), z.LT), :] = y.astype(bf16)
            return 0

        lax.fori_loop(0, z.CF, frame, 0)
        gather_row(n, n.one, n.one_s, c)
        after(z, c, lambda d: gather_more(n, n.one, n.one_s, d))
        return 0

    lax.fori_loop(0, z.N, chunk, 0)


def phase_attend(n, z):
    weight_forward(n, z, n.Wp, n.Wp_s)
    weight_wait(n, z, n.Wp, n.Wp_s)

    def chunk(c, _):
        if z.N == 1:
            gather_more(n, n.one, n.one_s, c)
        gather_row_wait(n, n.one, n.one_s, c)
        x = flat(n.one[c])
        pr = dot_nn(x, flat(n.Wp[...]))
        cos, sin = tables(n, c)
        for which in range(3):
            dest = (n.q, n.k, n.v)[which]
            for g in range(z.HW // 128):
                at = which * z.HW + g * 128
                y = pr[:, at : at + 128]
                if which < 2:
                    y = turn(y, cos, sin)
                if which == 0:
                    y = y * HSIZE**-0.5
                y = y.astype(bf16)
                for s in range(128 // HSIZE):
                    dest[g * (128 // HSIZE) + s, c] = y[:, s * HSIZE : (s + 1) * HSIZE]

        def head(h, _):
            q = n.q[h, c]
            a, b = causal(z)
            s = jnp.where(b <= a, dot_nt(q, n.k[h, c]), -1e30)
            m = jnp.max(s, -1, keepdims=True)
            e = jnp.exp(s - m)
            total = jnp.sum(e, -1, keepdims=True)
            o = dot_nn(e.astype(bf16), n.v[h, c])

            def more(j, carry):
                m, total, o = carry
                s = dot_nt(q, n.k[h, j])
                m2 = jnp.maximum(m, jnp.max(s, -1, keepdims=True))
                keep = jnp.exp(m - m2)
                e = jnp.exp(s - m2)
                total = total * keep + jnp.sum(e, -1, keepdims=True)
                o = o * keep + dot_nn(e.astype(bf16), n.v[h, j])
                return m2, total, o

            m, total, o = lax.fori_loop(0, c, more, (m, total, o))
            n.oh[h] = o / total
            lse = jnp.broadcast_to(m + jnp.log(total), (z.W, 128))
            n.lse[h, c] = jnp.transpose(lse)[:8]
            return 0

        lax.fori_loop(0, z.HD, head, 0)

        @pl.when(c == 0)
        def _():
            weight_forward(n, z, n.Wo, n.Wo_s)
            weight_wait(n, z, n.Wo, n.Wo_s)

        att = jnp.concatenate([n.oh[h] for h in range(z.HD)], -1)
        n.att[c] = att
        n.sb[c] = dot_nt(att.astype(bf16), flat(n.Wo[...])).astype(bf16).reshape(z.R, z.CT, D)
        last(z, c, lambda d: gather_more(n, n.one, n.one_s, d))
        scatter_row(n, n.sb, n.rsr, n.br_s, c)
        pl.when(c == (z.N - 1) // 2)(lambda: weight_relay(n, z, n.Wg, n.Wg_s))
        after(z, c, lambda d: scatter_more(n, n.sb, n.rsr, n.br_s, d))
        return 0

    lax.fori_loop(0, z.N, chunk, 0)


def summed(n, z, c, i):
    rows = pl.ds(pl.multiple_of(i * z.LT, z.LT), z.LT)
    total = n.sb[c, n.row, rows, :].astype(f32)
    for k in range(n.arrivals):
        total = total + n.rsr[c, k, rows, :].astype(f32)
    return total


def phase_two(n, z):
    def chunk(c, _):
        if z.N == 1:
            scatter_more(n, n.sb, n.rsr, n.br_s, c)
        scatter_row_wait(n, n.sb, n.rsr, n.br_s, c)

        def frame(i, _):
            f = c * z.CF + i
            rows = frame_rows(z, c, i)
            branch = summed(n, z, c, i)
            n.branch[rows, :] = branch
            mid = n.stream[rows, :] + vec(n, 2, f) * branch
            hat, unused = normed(mid)
            y = hat * (1.0 + vec(n, 4, f)) + vec(n, 3, f)
            n.two[c, n.row, pl.ds(pl.multiple_of(i * z.LT, z.LT), z.LT), :] = y.astype(bf16)
            return 0

        lax.fori_loop(0, z.CF, frame, 0)
        last(z, c, lambda d: scatter_more(n, n.sb, n.rsr, n.br_s, d))
        gather_row(n, n.two, n.two_s, c)
        after(z, c, lambda d: gather_more(n, n.two, n.two_s, d))
        return 0

    lax.fori_loop(0, z.N, chunk, 0)


def phase_feed(n, z):
    weight_forward(n, z, n.Wg, n.Wg_s, True)
    weight_wait(n, z, n.Wg, n.Wg_s, True)
    tile = 256

    def chunk(c, _):
        if z.N == 1:
            gather_more(n, n.two, n.two_s, c)
        gather_row_wait(n, n.two, n.two_s, c)

        def column(t, _):
            at = pl.ds(pl.multiple_of(t * tile, tile), tile)
            up_at = pl.ds(pl.multiple_of(z.FH + t * tile, tile), tile)
            x = flat(n.two[c])
            gate = dot_nn(x, flat(n.Wg[:, :, at]))
            up = dot_nn(x, flat(n.Wg[:, :, up_at]))
            value, unused = gelu_parts(gate)
            n.act[c, :, at] = (value * up).astype(bf16)
            n.gu[c, :, at] = gate.astype(bf16)
            n.gu[c, :, up_at] = up.astype(bf16)
            return 0

        lax.fori_loop(0, z.FH // tile, column, 0)

        @pl.when(c == 0)
        def _():
            weight_forward(n, z, n.Wd, n.Wd_s)
            weight_wait(n, z, n.Wd, n.Wd_s)

        slabs = tile // z.DR

        def output(t, _):
            y = dot_nt(n.act[c], flat(n.Wd[pl.ds(t * slabs, slabs)]))
            at = pl.ds(pl.multiple_of(t * tile, tile), tile)
            n.sb[c, :, :, at] = y.astype(bf16).reshape(z.R, z.CT, tile)
            return 0

        lax.fori_loop(0, D // tile, output, 0)
        last(z, c, lambda d: gather_more(n, n.two, n.two_s, d))
        scatter_row(n, n.sb, n.rsr, n.fd_s, c)
        after(z, c, lambda d: scatter_more(n, n.sb, n.rsr, n.fd_s, d))
        return 0

    lax.fori_loop(0, z.N, chunk, 0)


def phase_top(n, z):
    share_clip_wait(n, n.Wh, n.Wh_s)
    n.ghead[...] = jnp.zeros_like(n.ghead)
    n.loss[...] = jnp.zeros_like(n.loss)
    n.gad[...] = jnp.zeros_like(n.gad)

    def chunk(c, _):
        if z.N == 1:
            scatter_more(n, n.sb, n.rsr, n.fd_s, c)
        scatter_row_wait(n, n.sb, n.rsr, n.fd_s, c)

        def ahead(i, _):
            f = c * z.CF + i
            rows = frame_rows(z, c, i)
            here = pl.ds(pl.multiple_of(i * z.LT, z.LT), z.LT)
            feed = summed(n, z, c, i)
            mid = n.stream[rows, :] + vec(n, 2, f) * n.branch[rows, :]
            n.feed[here, :] = feed
            hat, rstd = normed(mid + vec(n, 5, f) * feed)
            n.hat[here, :] = hat
            n.rstd[here, :] = jnp.broadcast_to(rstd, (z.LT, 128))
            n.end[here, :] = (hat * (1.0 + vec(n, 7, f)) + vec(n, 6, f)).astype(bf16)
            return 0

        lax.fori_loop(0, z.CF, ahead, 0)
        rows = pl.ds(pl.multiple_of(c * z.CT, z.CT), z.CT)
        missed = dot_nn(n.end[...], flat(n.Wh[...])) - n.noise[rows, :]
        weight = n.fw[rows, :]
        n.loss[...] += jnp.sum((weight * (missed * missed)).reshape(z.CT // 8, 8, z.PF), 0)
        gp = ((2.0 / z.PF) * weight * missed).astype(bf16)
        n.ghead[...] += dot_tn(n.end[...], gp)
        n.gend[...] = dot_nt(gp, flat(n.Wh[...]))

        def back(i, _):
            f = c * z.CF + i
            rows = frame_rows(z, c, i)
            here = pl.ds(pl.multiple_of(i * z.LT, z.LT), z.LT)
            dx, d_shift, d_scale = norm_pull(n.hat[here, :], n.rstd[here, :1], vec(n, 7, f), n.gend[here, :])
            n.gad[6, pl.ds(f, 1), :] = d_shift
            n.gad[7, pl.ds(f, 1), :] = d_scale
            n.gad[5, pl.ds(f, 1), :] = jnp.sum(dx * n.feed[here, :], 0, keepdims=True)
            n.gmid[rows, :] = dx
            n.gf[c, n.row, here, :] = (dx * vec(n, 5, f)).astype(bf16)
            return 0

        lax.fori_loop(0, z.CF, back, 0)
        last(z, c, lambda d: scatter_more(n, n.sb, n.rsr, n.fd_s, d))
        gather_row(n, n.gf, n.gf_s, c)
        after(z, c, lambda d: gather_more(n, n.gf, n.gf_s, d))
        return 0

    lax.fori_loop(0, z.N, chunk, 0)


def run(body, z, cid, ins, anys, outs, scratch, export, vmem):
    names = list(ins) + list(anys) + list(outs) + list(scratch)

    def kernel(*refs):
        n = types.SimpleNamespace(**dict(zip(names, refs)))
        place(n, z)
        body(n, z)

    result = pl.pallas_call(
        kernel,
        out_shape=[jax.ShapeDtypeStruct(s, d) for s, d in outs.values()],
        in_specs=[pl.BlockSpec(memory_space=pltpu.VMEM)] * len(ins) + [pl.BlockSpec(memory_space=pl.ANY)] * len(anys),
        out_specs=[pl.BlockSpec(memory_space=pl.ANY if k in export else pltpu.VMEM) for k in outs],
        scratch_shapes=list(scratch.values()),
        compiler_params=pltpu.CompilerParams(collective_id=cid, has_side_effects=True, vmem_limit_bytes=vmem),
    )(*ins.values(), *anys.values())
    return dict(zip(outs, result))


KEPT = ("one", "two", "gf", "Wp", "Wo", "Wg", "Wd", "q", "k", "v", "att", "lse", "gu", "act", "stream", "branch", "gmid", "mod")


def forward_body(n, z):
    def export(*names):
        for name in names:
            i = KEPT.index(name)
            pltpu.make_async_copy(getattr(n, name), getattr(n, name + "_o"), n.ex_s.at[i]).start()

    phase_level(n, z)
    phase_one(n, z)
    export("mod", "stream")
    phase_attend(n, z)
    export("one", "Wp", "Wo", "q", "k", "v", "att", "lse")
    phase_two(n, z)
    export("branch")
    phase_feed(n, z)
    export("two", "Wg", "Wd", "gu", "act")
    phase_top(n, z)
    export("gmid")
    gather_more(n, n.gf, n.gf_s, z.N - 1)
    for c in range(z.N):
        gather_row_wait(n, n.gf, n.gf_s, c)
    export("gf")
    for i, name in enumerate(KEPT):
        pltpu.make_async_copy(getattr(n, name), getattr(n, name + "_o"), n.ex_s.at[i]).wait()


def shapes_of(z):
    rowed = (z.N, z.R, z.CT, D)
    return {
        "one": (rowed, bf16),
        "two": (rowed, bf16),
        "gf": (rowed, bf16),
        "gb": (rowed, bf16),
        "sb": (rowed, bf16),
        "rsr": ((z.N, z.R - 1, z.CT, D), bf16),
        "Wp": ((z.C, z.DR, 3 * z.HW), bf16),
        "Wo": ((z.C, z.DR, z.HW), bf16),
        "Wg": ((z.C, z.DR, 2 * z.FH), bf16),
        "Wd": ((z.C, z.DR, z.FH), bf16),
        "Wh": ((z.C, z.DR, z.PF), bf16),
        "q": ((z.HD, z.N, z.W, HSIZE), bf16),
        "k": ((z.HD, z.N, z.W, HSIZE), bf16),
        "v": ((z.HD, z.N, z.W, HSIZE), bf16),
        "att": ((z.N, z.W, z.HW), f32),
        "oh": ((z.HD, z.W, HSIZE), f32),
        "lse": ((z.HD, z.N, 8, z.W), f32),
        "gu": ((z.N, z.W, 2 * z.FH), bf16),
        "act": ((z.N, z.W, z.FH), bf16),
        "stream": ((z.T, D), f32),
        "branch": ((z.T, D), f32),
        "gmid": ((z.T, D), f32),
        "mod": ((VECTORS, PAD, D), f32),
        "gad": ((VECTORS, PAD, D), f32),
        "ghead": ((D, z.PF), f32),
        "loss": ((8, z.PF), f32),
        "pre": ((z.C * PAD, z.LW), f32),
        "cond": ((z.C * PAD, z.LW), bf16),
        "lv": ((z.C, z.LR, z.LW), bf16),
        "ea": ((z.C, PAD, TF), bf16),
        "pt": ((z.C, z.PF // z.C, D), f32),
        "pa": ((z.R, z.C * PAD, z.aw), f32),
        "ra": ((z.R, z.C * PAD, z.aw), f32),
        "rs": ((z.C, PAD, z.aw), f32),
        "rb": ((z.C, PAD, z.aw), f32),
        "ab": ((z.R, z.C, PAD, z.aw), f32),
        "feed": ((z.CT, D), f32),
        "hat": ((z.CT, D), f32),
        "rstd": ((z.CT, 128), f32),
        "end": ((z.CT, D), bf16),
        "gend": ((z.CT, D), f32),
    }


def vm(shapes, names):
    return {k: pltpu.VMEM(*shapes[k]) for k in names}


def forward_call(z, ins):
    sh = shapes_of(z)
    direct = ("gad", "ghead", "loss", "pre", "cond", "ea")
    outs = {k: sh[k] for k in direct}
    outs.update({k + "_o": sh[k] for k in KEPT})
    rest = ["Wh", "oh", "sb", "rsr", "lv", "pt", "pa", "ra", "rs", "rb", "ab", "feed", "hat", "rstd", "end", "gend"]
    scratch = vm(sh, list(KEPT) + rest)
    dma = pltpu.SemaphoreType.DMA
    for k in ("ea_s", "lv_s", "pt_s", "rb_s", "Wh_s", "Wp_s", "Wo_s", "Wg_s", "Wd_s"):
        scratch[k] = dma((2, z.C))
    for k in ("ra_s", "ab_s"):
        scratch[k] = dma((2, z.R))
    for k in ("one_s", "br_s", "two_s", "fd_s", "gf_s"):
        scratch[k] = dma((2, z.N, max(6, z.R)))
    scratch["ex_s"] = dma((len(KEPT),))
    got = run(forward_body, z, 0, ins, {}, outs, scratch, [k + "_o" for k in KEPT], 60 << 20)
    return {(k[:-2] if k.endswith("_o") else k): v for k, v in got.items()}


def forward_inputs(z, a):
    alpha_bar, frame_weight = noise_plan(a["levels"])
    latents = a["latents"].reshape(z.F, z.LT, z.PF)
    noise = a["noise"].reshape(z.F, z.LT, z.PF)
    noisy = jnp.sqrt(alpha_bar)[0, :, None, None] * latents + jnp.sqrt(1.0 - alpha_bar)[0, :, None, None] * noise
    emb = level_embedding(a["levels"][0], TF // 2).astype(bf16)
    return {
        "emb": jnp.pad(emb, ((0, PAD - z.F), (0, 0))),
        "w_level": a["w_level"],
        "w_patch": a["w_patch"],
        "w_head": a["w_head"],
        "w_adapt": a["w_adapt"],
        "wp": jnp.transpose(a["w_project"], (1, 0, 2)),
        "wo": a["w_output"],
        "wg": packed(a["w_gateup"]),
        "wd": a["w_down"],
        "inputs": noisy.astype(bf16).reshape(z.T, z.PF),
        "noise": noise.reshape(z.T, z.PF),
        "fw": jnp.broadcast_to(frame_weight[0][:, None, None], (z.F, z.LT, z.PF)).reshape(z.T, z.PF),
        "tab": jnp.asarray(rotary_consts(z)),
    }, frame_weight


def fetch(n, name):
    i = LOADED.index(name)
    return pltpu.make_async_copy(getattr(n, name + "_i"), getattr(n, name), n.in_s.at[i])


def phase_pull_feed(n, z):
    tile = 256
    for name in ("Wd", "gu", "gf"):
        fetch(n, name).wait()

    def chunk(c, _):
        def column(t, _):
            at = pl.ds(pl.multiple_of(t * tile, tile), tile)
            up_at = pl.ds(pl.multiple_of(z.FH + t * tile, tile), tile)
            da = dot_nn(flat(n.gf[c]), flat(n.Wd[:, :, at]))
            value, slope = gelu_parts(n.gu[c, :, at].astype(f32))
            up = n.gu[c, :, up_at].astype(f32)
            n.gu[c, :, at] = (da * up * slope).astype(bf16)
            n.gu[c, :, up_at] = (da * value).astype(bf16)
            return 0

        lax.fori_loop(0, z.FH // tile, column, 0)

        @pl.when(c == 0)
        def _():
            fetch(n, "Wg").wait()

        slabs = tile // z.DR

        def output(t, _):
            y = dot_nt(n.gu[c], flat(n.Wg[pl.ds(t * slabs, slabs)]))
            at = pl.ds(pl.multiple_of(t * tile, tile), tile)
            n.sb[c, :, :, at] = y.astype(bf16).reshape(z.R, z.CT, tile)
            return 0

        lax.fori_loop(0, D // tile, output, 0)
        scatter_row(n, n.sb, n.rsr, n.gt_s, c)
        after(z, c, lambda d: scatter_more(n, n.sb, n.rsr, n.gt_s, d))
        return 0

    lax.fori_loop(0, z.N, chunk, 0)


def weight_grad(n, z, left, right, into):
    half = n.tb.shape[0]
    width = right.shape[-1]
    tile = min(256, width)
    slabs = half // z.DR
    for part in range(D // half):
        for c in range(z.N):
            block = left[c, :, :, part * half : (part + 1) * half]
            n.tb[:, c * z.W : (c + 1) * z.W] = jnp.transpose(flat(block))

        def column(t, _):
            at = pl.ds(pl.multiple_of(t * tile, tile), tile)
            y = dot_nn(n.tb[...], flat(right[:, :, at]).astype(bf16))
            into[part * slabs : (part + 1) * slabs, :, at] = y.astype(bf16).reshape(slabs, z.DR, tile)
            return 0

        lax.fori_loop(0, width // tile, column, 0)


def reduce_one(n, z, part, sx, sems):
    for k in range(z.C // 2):
        j = (n.sib + 2 * k) % z.C
        remote(part.at[j], sx.at[j // 2], sems.at[0, k], sems.at[1, j // 2], (n.sib, n.row)).start()


def reduce_two(n, z, part, sx, sems, rx, more, width):
    for k in range(z.C // 2):
        j = (n.clip + 2 * k) % z.C
        mine = (n.sib + 2 * k) % z.C
        remote(part.at[mine], sx.at[j // 2], sems.at[0, k], sems.at[1, j // 2], (n.sib, n.row)).wait()
        part[j] = (part[j].astype(f32) + sx[j // 2].astype(f32)).astype(bf16)
        if k:
            back = z.C // 2 - k - 1
            at = slice(0, width)
            remote(part.at[j, :, at], rx.at[back, :, at], more.at[0, k], more.at[1, back], (j, n.row)).start()


def reduce_late(n, z):
    at = slice(2 * z.HW, 3 * z.HW)
    for k in range(1, z.C // 2):
        j = (n.clip + 2 * k) % z.C
        back = z.C // 2 - k - 1
        remote(n.Wp.at[j, :, at], n.Rp.at[back, :, at], n.Rv_s.at[0, k], n.Rv_s.at[1, back], (j, n.row)).start()


def reduce_three(n, z, part, rx, more, put, late):
    total = part[n.clip].astype(f32)
    for k in range(1, z.C // 2):
        j = (n.clip + 2 * k) % z.C
        at = slice(0, 2 * z.HW) if late else slice(0, part.shape[2])
        remote(part.at[j, :, at], rx.at[k - 1, :, at], more.at[0, k], more.at[1, k - 1], (j, n.row)).wait()
        if late:
            at = slice(2 * z.HW, 3 * z.HW)
            remote(part.at[j, :, at], rx.at[k - 1, :, at], n.Rv_s.at[0, k], n.Rv_s.at[1, k - 1], (j, n.row)).wait()
        total = total + rx[k - 1].astype(f32)
    put(total)
    n.squares[...] += fold(total)


def fold(x):
    x = x * x
    total = x[:, :128]
    for i in range(1, x.shape[1] // 128):
        total = total + x[:, i * 128 : (i + 1) * 128]
    return jnp.sum(total.reshape(x.shape[0] // 8, 8, 128), 0)


def phase_pull_two(n, z):
    for name in ("stream", "branch", "gmid"):
        fetch(n, name).wait()

    def chunk(c, _):
        scatter_row_wait(n, n.sb, n.rsr, n.gt_s, c)

        def frame(i, _):
            f = c * z.CF + i
            rows = frame_rows(z, c, i)
            branch = n.branch[rows, :]
            hat, rstd = normed(n.stream[rows, :] + vec(n, 2, f) * branch)
            dx, d_shift, d_scale = norm_pull(hat, rstd, vec(n, 4, f), summed(n, z, c, i))
            n.gadp[3, pl.ds(f, 1), :] = d_shift
            n.gadp[4, pl.ds(f, 1), :] = d_scale
            mid = n.gmid[rows, :] + dx
            n.gmid[rows, :] = mid
            n.gadp[2, pl.ds(f, 1), :] = jnp.sum(mid * branch, 0, keepdims=True)
            n.gb[c, n.row, pl.ds(pl.multiple_of(i * z.LT, z.LT), z.LT), :] = (mid * vec(n, 2, f)).astype(bf16)
            return 0

        lax.fori_loop(0, z.CF, frame, 0)
        gather_row(n, n.gb, n.gb_s, c)
        after(z, c, lambda d: gather_more(n, n.gb, n.gb_s, d))
        return 0

    lax.fori_loop(0, z.N, chunk, 0)


def phase_pull_attend(n, z):
    for name in ("Wo", "q", "k", "v", "att", "lse"):
        fetch(n, name).wait()
    queries = 384 if z.W % 384 == 0 else z.W
    parts = z.W // queries

    def chunk(c, _):
        if z.N == 1:
            gather_more(n, n.gb, n.gb_s, c)
        gather_row_wait(n, n.gb, n.gb_s, c)
        do = dot_nn(flat(n.gb[c]), flat(n.Wo[...])).astype(bf16)
        for h in range(z.HD):
            mine = do[:, h * HSIZE : (h + 1) * HSIZE]
            n.do[h] = mine
            delta = jnp.sum(mine.astype(f32) * n.att[c, :, h * HSIZE : (h + 1) * HSIZE], -1, keepdims=True)
            n.delta[h] = jnp.transpose(jnp.broadcast_to(delta, (z.W, 128)))[:8]

        def head(step, _):
            h, u = step // parts, step % parts
            at = pl.ds(pl.multiple_of(u * queries, queries), queries)
            q, do = n.q[h, c, at, :], n.do[h, at, :]
            lse, delta = n.lse[h, c, :, at][:1], n.delta[h, :, at][:1]

            def block(j, masked):
                k, v = n.k[h, j], n.v[h, j]
                p = jnp.exp(dot_nt(k, q) - lse)
                if masked:
                    a = lax.broadcasted_iota(jnp.int32, p.shape, 0)
                    b = lax.broadcasted_iota(jnp.int32, p.shape, 1) + u * queries
                    p = jnp.where((a % z.CT) // z.LT <= (b % z.CT) // z.LT, p, 0.0)
                dv = dot_nn(p.astype(bf16), do)
                ds = (p * (dot_nt(v, do) - delta)).astype(bf16)
                n.dkv[h, j] += jnp.concatenate([dot_nn(ds, q), dv], -1)
                return dot_tn(ds, k)

            dq = block(c, True)
            n.dq[h, at, :] = lax.fori_loop(0, c, lambda j, dq: dq + block(j, False), dq)
            return 0

        n.dkv[:, c] = jnp.zeros_like(n.dkv[:, c])
        lax.fori_loop(0, z.HD * parts, head, 0)
        last(z, c, lambda d: gather_more(n, n.gb, n.gb_s, d))
        pl.when(c == 0)(lambda: reduce_middle(n, z, "g"))
        pl.when(c == z.N // 2)(lambda: early_row(n, z))
        pl.when(c == z.N - 1)(lambda: early_clip(n, z))
        per = 128 // HSIZE
        cos, sin = tables(n, c)
        for g in range(z.HW // 128):
            y = jnp.concatenate([n.dq[g * per + s] for s in range(per)], -1)
            y = turn(y, cos, -sin) * HSIZE**-0.5
            n.gp[c, :, g * 128 : (g + 1) * 128] = y.astype(bf16)
        return 0

    lax.fori_loop(0, z.N, chunk, 0)


def phase_pull_project(n, z):
    fetch(n, "Wp").wait()
    per = 128 // HSIZE
    tile = 256

    def chunk(c, _):
        cos, sin = tables(n, c)
        for g in range(z.HW // 128):
            y = jnp.concatenate([n.dkv[g * per + s, c][:, :HSIZE] for s in range(per)], -1)
            n.gp[c, :, z.HW + g * 128 : z.HW + (g + 1) * 128] = turn(y, cos, -sin).astype(bf16)
            y = jnp.concatenate([n.dkv[g * per + s, c][:, HSIZE:] for s in range(per)], -1)
            n.gp[c, :, 2 * z.HW + g * 128 : 2 * z.HW + (g + 1) * 128] = y.astype(bf16)
        slabs = tile // z.DR

        def output(t, _):
            y = dot_nt(n.gp[c], flat(n.Wp[pl.ds(t * slabs, slabs)]))
            at = pl.ds(pl.multiple_of(t * tile, tile), tile)
            n.sb[c, :, :, at] = y.astype(bf16).reshape(z.R, z.CT, tile)
            return 0

        lax.fori_loop(0, D // tile, output, 0)
        scatter_row(n, n.sb, n.rsr, n.go_s, c)
        after(z, c, lambda d: scatter_more(n, n.sb, n.rsr, n.go_s, d))
        return 0

    lax.fori_loop(0, z.N, chunk, 0)


def phase_pull_one(n, z):
    def chunk(c, _):
        scatter_row_wait(n, n.sb, n.rsr, n.go_s, c)

        def frame(i, _):
            f = c * z.CF + i
            rows = frame_rows(z, c, i)
            hat, rstd = normed(n.stream[rows, :])
            dx, d_shift, d_scale = norm_pull(hat, rstd, vec(n, 1, f), summed(n, z, c, i))
            n.gadp[0, pl.ds(f, 1), :] = d_shift
            n.gadp[1, pl.ds(f, 1), :] = d_scale
            n.gb[c, n.row, pl.ds(pl.multiple_of(i * z.LT, z.LT), z.LT), :] = (n.gmid[rows, :] + dx).astype(bf16)
            return 0

        lax.fori_loop(0, z.CF, frame, 0)
        return 0

    lax.fori_loop(0, z.N, chunk, 0)


def row_total(n, src, dst, cut):
    total = src[n.row, cut].astype(f32)
    for p in n.row_peer:
        total = total + dst[p, cut].astype(f32)
    return total


def swap_row_cut(n, src, dst, sems, cut):
    for k, p in enumerate(n.row_peer):
        remote(src.at[p, cut], dst.at[n.row, cut], sems.at[0, k], sems.at[1, n.row], (n.clip, p)).start()


def swap_row_cut_wait(n, src, dst, sems, cut):
    for k, p in enumerate(n.row_peer):
        remote(src.at[p, cut], dst.at[p, cut], sems.at[0, k], sems.at[1, p], (n.clip, p)).wait()


def is_late(z, clip):
    return clip < z.C // 4


def swap_owner(n, z, late):
    for k, p in enumerate(n.clip_peer):
        copy = remote(n.ca.at[p], n.da.at[n.clip], n.ca_s.at[0, k], n.ca_s.at[1, n.clip], (p, n.row))
        pl.when(is_late(z, p) == late)(copy.start)


def swap_owner_wait(n, z):
    for k, p in enumerate(n.clip_peer):
        remote(n.ca.at[p], n.da.at[p], n.ca_s.at[0, k], n.ca_s.at[1, p], (p, n.row)).wait_recv()


def swap_owner_sent(n, z):
    for k, p in enumerate(n.clip_peer):
        remote(n.ca.at[p], n.da.at[p], n.ca_s.at[0, k], n.ca_s.at[1, p], (p, n.row)).wait_send()


def owner_share(n, z):
    swap_owner_wait(n, z)
    n.da[n.clip] = n.ca[n.clip]
    n.ea2[n.row] = flat(n.da[...])
    share_row(n, n.ea2, n.ea2_s)


def owner_grads(n, z):
    share_row_wait(n, n.ea2, n.ea2_s)
    low = jnp.concatenate([n.ea2[r] for r in range(z.R)], -1)
    n.gc[...] = dot_nt(low, n.w_adapt[...].astype(bf16)).reshape(z.C, PAD, z.LW)
    swap_clip(n, n.gc, n.gd, n.gc_s)
    gadapt = dot_tn(n.cond[...], low)
    n.gadapt[...] = gadapt
    n.squares[...] += fold(gadapt)


def take_columns(n, z, owners):
    for r in range(z.R):
        for i in owners:
            col = i * z.AW + r * z.aw
            n.xa[r, i] = n.gadp[col // D, :, col % D : col % D + z.aw]


def early_row(n, z):
    hr = z.DR // z.R
    take_columns(n, z, range(z.C // 4, z.C))
    for r in range(z.R):
        for i in range(z.C):
            at = i * z.DR + r * hr
            n.xh[r, i] = n.ghead[at : at + hr, :].astype(n.xh.dtype)
    swap_row_cut(n, n.xa, n.ya, n.xa_s, pl.ds(z.C // 4, z.C - z.C // 4))
    swap_row(n, n.xh, n.yh, n.xh_s)


def early_clip(n, z):
    cut = pl.ds(z.C // 4, z.C - z.C // 4)
    swap_row_cut_wait(n, n.xa, n.ya, n.xa_s, cut)
    swap_row_wait(n, n.xh, n.yh, n.xh_s)
    n.ca[cut] = row_total(n, n.xa, n.ya, cut).astype(bf16)
    n.ch[...] = row_total(n, n.xh, n.yh, slice(None)).astype(n.ch.dtype)
    swap_owner(n, z, False)
    swap_clip(n, n.ch, n.dh, n.ch_s)
    n.dh[n.clip] = n.ch[n.clip]


def phase_small(n, z):
    pr, hr = z.PF // z.C, z.DR // z.R
    pw = D // z.R
    late = is_late(z, n.clip)
    early = jnp.logical_not(late)
    cut = pl.ds(0, z.C // 4)
    take_columns(n, z, range(z.C // 4))
    swap_row_cut(n, n.xa, n.ya, n.xb_s, cut)
    gpatch = dot_tn(n.inputs[...], jnp.concatenate([n.gb[c, n.row] for c in range(z.N)], 0))
    for r in range(z.R):
        n.xp[r] = gpatch[:, r * pw : (r + 1) * pw].astype(bf16)
    swap_row(n, n.xp, n.yp, n.xp_s)
    pl.when(early)(lambda: owner_share(n, z))
    swap_clip_wait(n, n.ch, n.dh, n.ch_s)
    sh = n.dh[0].astype(f32)
    for i in range(1, z.C):
        sh = sh + n.dh[i].astype(f32)
    n.eh[n.row] = sh
    share_row(n, n.eh, n.eh_s)
    swap_row_cut_wait(n, n.xa, n.ya, n.xb_s, cut)
    n.ca[cut] = row_total(n, n.xa, n.ya, cut).astype(bf16)
    swap_owner(n, z, True)
    swap_row_wait(n, n.xp, n.yp, n.xp_s)
    n.cp[...] = row_total(n, n.xp, n.yp, slice(None)).reshape(z.C, pr, pw).astype(n.cp.dtype)
    swap_clip(n, n.cp, n.dp, n.cp_s)
    n.dp[n.clip] = n.cp[n.clip]
    pl.when(early)(lambda: owner_grads(n, z))
    reduce_late(n, z)
    pl.when(late)(lambda: owner_share(n, z))
    reduce_end(n, z, "d")
    pl.when(late)(lambda: owner_grads(n, z))
    swap_owner_sent(n, z)
    swap_clip_wait(n, n.cp, n.dp, n.cp_s)
    sp = n.dp[0].astype(f32)
    for i in range(1, z.C):
        sp = sp + n.dp[i].astype(f32)
    n.ep[n.row] = sp
    share_row(n, n.ep, n.ep_s)
    n.squares[...] += fold(sp) + fold(sh)
    reduce_end(n, z, "g")
    swap_clip_wait(n, n.gc, n.gd, n.gc_s)
    total = n.gc[n.clip]
    for p in n.clip_peer:
        total = total + n.gd[p]
    pre = n.pre[pl.ds(pl.multiple_of(n.clip * PAD, PAD), PAD), :]
    sig = 1.0 / (1.0 + jnp.exp(-pre))
    n.gl[n.clip] = (total * (sig * (1.0 + pre * (1.0 - sig)))).astype(bf16)
    share_clip(n, n.gl, n.gl_s)
    reduce_end(n, z, "o")
    reduce_end(n, z, "p")
    share_row_wait(n, n.eh, n.eh_s)
    share_row_wait(n, n.ep, n.ep_s)
    for r in range(z.R):
        n.gpatch[:, r * pw : (r + 1) * pw] = n.ep[r]
        n.gheads[r * hr : (r + 1) * hr, :] = n.eh[r]
    share_clip_wait(n, n.gl, n.gl_s)
    n.glv[...] = dot_tn(flat(n.ea[...]), flat(n.gl[...]))
    glevel = n.glv[pl.ds(pl.multiple_of(n.clip * z.LR, z.LR), z.LR), :]
    n.glevel[...] = glevel
    n.squares[...] += fold(glevel)


def phase_stats(n, z):
    n.sa[n.row, 0:8] = n.squares[...]
    n.sa[n.row, 8:16] = n.loss[...]
    n.sa[n.row, 16:24] = n.weight[...]
    share_row(n, n.sa, n.sa_s)
    share_row_wait(n, n.sa, n.sa_s)
    total = n.sa[0]
    for r in range(1, z.R):
        total = total + n.sa[r]
    n.sc[n.clip] = total
    share_clip(n, n.sc, n.sc_s)
    share_clip_wait(n, n.sc, n.sc_s)
    total = n.sc[0]
    for i in range(1, z.C):
        total = total + n.sc[i]
    n.stats[...] = total


LOADED = ("Wd", "gu", "gf", "Wg", "stream", "branch", "gmid", "act", "two", "Wo", "q", "k", "v", "att", "lse", "Wp", "one")


def reduce_start(n, z, x):
    reduce_one(n, z, getattr(n, "W" + x), getattr(n, "S" + x), getattr(n, "S" + x + "_s"))


def reduce_middle(n, z, x):
    part, rx = getattr(n, "W" + x), getattr(n, "R" + x)
    width = 2 * z.HW if x == "p" else part.shape[2]
    reduce_two(n, z, part, getattr(n, "S" + x), getattr(n, "S" + x + "_s"), rx, getattr(n, "R" + x + "_s"), width)


def reduce_end(n, z, x):
    def put(total):
        if x == "p":
            for k in range(3):
                n.Gp[k] = total[:, k * z.HW : (k + 1) * z.HW]
        elif x == "g":
            tiles = z.FH // 128
            for t in range(tiles):
                for k in range(2):
                    at = k * z.FH + t * 128
                    n.Gg[pl.ds(2 * t + k, z.DR, stride=2 * tiles), :] = total[:, at : at + 128]
        else:
            getattr(n, "G" + x)[...] = jnp.transpose(total)

    reduce_three(n, z, getattr(n, "W" + x), getattr(n, "R" + x), getattr(n, "R" + x + "_s"), put, x == "p")


def backward_body(n, z):
    for name in LOADED:
        if name not in ("one", "two"):
            fetch(n, name).start()
    n.squares[...] = jnp.zeros_like(n.squares)
    n.gadp[...] = n.gad[...]
    enter(n, z)
    phase_pull_feed(n, z)
    fetch(n, "act").wait()
    weight_grad(n, z, n.gf, n.act, n.Wd)
    load_two = pltpu.make_async_copy(n.two_i, n.gf, n.in_s.at[LOADED.index("two")])
    load_two.start()
    reduce_start(n, z, "d")
    scatter_more(n, n.sb, n.rsr, n.gt_s, z.N - 1)
    phase_pull_two(n, z)
    reduce_middle(n, z, "d")
    load_two.wait()
    weight_grad(n, z, n.gf, n.gu, n.Wg)
    load_one = pltpu.make_async_copy(n.one_i, n.gf, n.in_s.at[LOADED.index("one")])
    load_one.start()
    reduce_start(n, z, "g")
    phase_pull_attend(n, z)
    weight_grad(n, z, n.gb, n.att, n.Wo)
    reduce_start(n, z, "o")
    phase_pull_project(n, z)
    load_one.wait()
    reduce_middle(n, z, "o")
    weight_grad(n, z, n.gf, n.gp, n.Wp)
    reduce_start(n, z, "p")
    scatter_more(n, n.sb, n.rsr, n.go_s, z.N - 1)
    reduce_middle(n, z, "p")
    phase_pull_one(n, z)
    phase_small(n, z)
    phase_stats(n, z)


def backward_call(z, kept, ins):
    sh = shapes_of(z)
    pr, hr, pw = z.PF // z.C, z.DR // z.R, D // z.R
    head_type = f32 if hr % 16 else bf16
    patch_type = f32 if pr % 16 else bf16
    widths = {"p": 3 * z.HW, "o": z.HW, "g": 2 * z.FH, "d": z.FH}
    outs = {
        "Gp": ((3, z.DR, z.HW), f32),
        "Go": ((z.HW, z.DR), f32),
        "Gg": ((z.DR * 2 * z.FH // 128, 128), f32),
        "Gd": ((z.FH, z.DR), f32),
    }
    outs.update(
        gpatch=((pr, D), f32),
        gheads=((z.DR, z.PF), f32),
        gadapt=((z.LW, z.AW), f32),
        glevel=((z.LR, z.LW), f32),
        stats=((24, 128), f32),
    )
    anys = {k + "_i": kept[k] for k in LOADED}
    scratch = vm(sh, [k for k in LOADED if k not in ("one", "two")] + ["gb", "sb", "rsr"])
    for x, w in widths.items():
        scratch["S" + x] = pltpu.VMEM((z.C // 2, z.DR, w), bf16)
        scratch["R" + x] = pltpu.VMEM((z.C // 2 - 1, z.DR, w), bf16)
    extra = {
        "tb": ((D // max(2, z.W // 192), z.N * z.W), bf16),
        "do": ((z.HD, z.W, HSIZE), bf16),
        "delta": ((z.HD, 8, z.W), f32),
        "dq": ((z.HD, z.W, HSIZE), f32),
        "dkv": ((z.HD, z.N, z.W, 2 * HSIZE), f32),
        "gp": ((z.N, z.W, 3 * z.HW), bf16),
        "gadp": ((VECTORS, PAD, D), f32),
        "squares": ((8, 128), f32),
        "xa": ((z.R, z.C, PAD, z.aw), f32),
        "ya": ((z.R, z.C, PAD, z.aw), f32),
        "xp": ((z.R, z.PF, pw), bf16),
        "yp": ((z.R, z.PF, pw), bf16),
        "xh": ((z.R, z.C, hr, z.PF), head_type),
        "yh": ((z.R, z.C, hr, z.PF), head_type),
        "ca": ((z.C, PAD, z.aw), bf16),
        "da": ((z.C, PAD, z.aw), bf16),
        "cp": ((z.C, pr, pw), patch_type),
        "dp": ((z.C, pr, pw), patch_type),
        "ch": ((z.C, hr, z.PF), head_type),
        "dh": ((z.C, hr, z.PF), head_type),
        "ea2": ((z.R, z.C * PAD, z.aw), bf16),
        "ep": ((z.R, pr, pw), f32),
        "eh": ((z.R, hr, z.PF), f32),
        "gc": ((z.C, PAD, z.LW), f32),
        "gd": ((z.C, PAD, z.LW), f32),
        "gl": ((z.C, PAD, z.LW), bf16),
        "glv": ((TF, z.LW), f32),
        "sa": ((z.R, 24, 128), f32),
        "sc": ((z.C, 24, 128), f32),
    }
    scratch.update(vm(extra, extra))
    dma = pltpu.SemaphoreType.DMA
    scratch["Rv_s"] = dma((2, z.C // 2))
    scratch["in_s"] = dma((len(LOADED),))
    for x in widths:
        scratch["S" + x + "_s"] = dma((2, z.C // 2))
        scratch["R" + x + "_s"] = dma((2, z.C // 2))
    for k in ("gt_s", "gb_s", "go_s"):
        scratch[k] = dma((2, z.N, max(6, z.R)))
    for k in ("xa_s", "xb_s", "xp_s", "xh_s", "ea2_s", "ep_s", "eh_s", "sa_s"):
        scratch[k] = dma((2, z.R))
    for k in ("ca_s", "cp_s", "ch_s", "gc_s", "gl_s", "sc_s"):
        scratch[k] = dma((2, z.C))
    return run(backward_body, z, 1, ins, anys, outs, scratch, (), 64 << 20)


WEIGHTS = ("patch", "level", "adapt", "project", "output", "gateup", "down", "head")


def packed(x):
    rows, pair, width = x.shape
    return jnp.transpose(x.reshape(rows, pair, width // 128, 128), (0, 2, 1, 3)).reshape(-1, 128)


def unpacked(x, shape):
    rows, pair, width = shape
    return jnp.transpose(x.reshape(rows, width // 128, pair, 128), (0, 2, 1, 3)).reshape(shape)


def to_kernel(values):
    values = list(values)
    values[3] = jnp.transpose(values[3], (1, 0, 2))
    values[5] = packed(values[5])
    return values


def from_kernel(values, gateup_shape):
    values = list(values)
    values[3] = jnp.transpose(values[3], (1, 0, 2))
    values[5] = unpacked(values[5], gateup_shape)
    return values


def adam_kernel(pf, stats, *refs):
    grads, masters, firsts, seconds = (refs[8 * i : 8 * i + 8] for i in range(4))
    scalars = refs[32:35]
    news, means, squares = (refs[35 + 8 * i : 43 + 8 * i] for i in range(3))
    weight_sum = jnp.sum(stats[16:24])
    grad_norm = jnp.sqrt(jnp.full((8, 128), jnp.sum(stats[0:8]))) / weight_sum
    factor = jnp.minimum(1.0, clip_level / (grad_norm + 1e-06)) / weight_sum
    scalars[0][0, 0] = jnp.sum(stats[8:16]) / pf
    scalars[1][0, 0] = weight_sum
    scalars[2][0, 0] = jnp.max(grad_norm)
    factor = factor[:1, :1]
    for g, m, f, s, new, mean, square in zip(grads, masters, firsts, seconds, news, means, squares):
        grad = g[...] * factor
        first_new = beta_one * f[...] + (1.0 - beta_one) * grad
        second_new = beta_two * s[...] + (1.0 - beta_two) * grad * grad
        first_hat = first_new * (1.0 / (1.0 - beta_one**STEP))
        second_hat = second_new * (1.0 / (1.0 - beta_two**STEP))
        master = m[...]
        new[...] = master - learn_rate * (first_hat / (jnp.sqrt(second_hat) + adam_eps) + decay_rate * master)
        mean[...] = first_new
        square[...] = second_new


def adam_call(z, stats, grads, masters, firsts, seconds):
    steps = 4
    split = (None, None, 0, 1, 0, 0, 0, 0)

    def spec(x, axis):
        if axis is None:
            return pl.BlockSpec(x.shape, lambda i: (0,) * x.ndim)
        block = tuple(d // steps if k == axis else d for k, d in enumerate(x.shape))
        return pl.BlockSpec(block, lambda i: tuple(i if k == axis else 0 for k in range(x.ndim)))

    specs = [spec(x, axis) for x, axis in zip(masters, split)]
    shapes = [jax.ShapeDtypeStruct(x.shape, f32) for x in masters]
    scalar = jax.ShapeDtypeStruct((1, 1), f32)
    result = pl.pallas_call(
        functools.partial(adam_kernel, z.PF),
        grid=(steps,),
        out_shape=[scalar] * 3 + shapes * 3,
        in_specs=[pl.BlockSpec(stats.shape, lambda i: (0, 0))] + specs * 4,
        out_specs=[pl.BlockSpec((1, 1), lambda i: (0, 0), memory_space=pltpu.SMEM)] * 3 + specs * 3,
        compiler_params=pltpu.CompilerParams(vmem_limit_bytes=64 << 20),
    )(stats, *grads, *masters, *firsts, *seconds)
    return result[:3], result[3:11], result[11:19], result[19:27]


def on_device(latents, noise, levels, *weights):
    masters, firsts, seconds = weights[:8], weights[8:16], weights[16:]
    a = dict(zip(["w_" + k for k in WEIGHTS], masters))
    a.update(latents=latents, noise=noise, levels=levels)
    z = sizes_of(latents, lax.axis_size("clip"), lax.axis_size("row"))
    ins, frame_weight = forward_inputs(z, a)
    kept = forward_call(z, ins)
    weight = jnp.sum(frame_weight) * z.LT
    back = {k: kept[k] for k in ("gad", "ghead", "loss", "pre", "cond", "ea", "mod")}
    back.update({k: ins[k] for k in ("w_adapt", "inputs", "tab")})
    back["weight"] = jnp.zeros((8, 128), f32).at[0, 0].set(weight)
    g = backward_call(z, kept, back)
    grads = (g["gpatch"], g["glevel"], g["gadapt"], g["Gp"], g["Go"], g["Gg"], g["Gd"], g["gheads"])
    scalars, *results = adam_call(z, g["stats"], grads, *(to_kernel(x) for x in (masters, firsts, seconds)))
    results = [from_kernel(x, masters[5].shape) for x in results]
    return tuple(x.reshape(()) for x in scalars) + tuple(x for result in results for x in result)


def solution(mesh):
    tokens = P("clip", None, "row", None, None)
    by_clip = P("clip", None)
    weights = (by_clip, P("clip", "row"), P("row", "clip"), P("clip", None, "row"), P("row", "clip"))
    weights = weights + (P("clip", None, "row"), P("row", "clip"), by_clip)
    return jax.shard_map(
        on_device,
        mesh=mesh,
        in_specs=(tokens, tokens, by_clip) + weights * 3,
        out_specs=(P(), P(), P()) + weights * 3,
        check_vma=False,
    )
```

```python
import functools
import math
import types

import jax
import jax.numpy as jnp
import numpy as np
from jax import lax
from jax.experimental import pallas as pl
from jax.experimental.pallas import tpu as pltpu
from jax.sharding import PartitionSpec as P

D = 1024
HEADS = 16
HSIZE = 64
TF = 256
LEVELS = 1000
STEP = 3
VECTORS = 8
PAD = 16

norm_eps = 1e-06
clip_level = 0.002
learn_rate = 0.03
beta_one = 0.9
beta_two = 0.95
decay_rate = 0.1
adam_eps = 1e-08

MESH = pl.DeviceIdType.MESH
f32 = jnp.float32
bf16 = jnp.bfloat16


def dot_nn(left, right):
    return jnp.dot(left, right, preferred_element_type=f32)


def dot_nt(left, right):
    return lax.dot_general(left, right, (((1,), (1,)), ((), ())), preferred_element_type=f32)


def dot_tn(left, right):
    return lax.dot_general(left, right, (((0,), (0,)), ((), ())), preferred_element_type=f32)


def frequencies(number):
    return jnp.exp(-math.log(10000.0) * jnp.arange(number, dtype=f32) / number)


def noise_plan(levels):
    ratio = levels.astype(f32) / LEVELS
    alpha_bar = jnp.cos((ratio + 0.008) / 1.008 * (math.pi / 2)) ** 2
    weight = jnp.minimum(1.0, 5.0 * (1.0 - alpha_bar) / alpha_bar)
    return (alpha_bar, weight)


def level_embedding(levels, half):
    angle = levels.astype(f32)[..., None] * frequencies(half)
    return jnp.concatenate([jnp.cos(angle), jnp.sin(angle)], -1)


def sizes_of(latents, clips, parts):
    z = types.SimpleNamespace()
    z.C, z.R = clips, parts
    z.F = latents.shape[1]
    z.rows, z.cols, z.PF = latents.shape[2], latents.shape[3], latents.shape[4]
    z.LT = z.rows * z.cols
    z.N = 3 if z.F % 3 == 0 else 1
    z.CF = z.F // z.N
    z.CT = z.CF * z.LT
    z.W = z.R * z.CT
    z.T = z.F * z.LT
    z.HD = HEADS // parts
    z.HW = z.HD * HSIZE
    z.FH = 4 * D // parts
    z.DR = D // clips
    z.LR = TF // clips
    z.LW = D // parts
    z.AW = VECTORS * D // clips
    z.aw = z.AW // parts
    return z


def rotary_consts(z):
    half = HSIZE // 2
    fp = half // 4
    rp = 3 * half // 8
    cp = half - fp - rp

    def freq(n):
        return np.exp(-math.log(10000.0) * np.arange(n, dtype=np.float32) / np.float32(n)).astype(np.float32)

    shape = (z.N, z.R, z.CF, z.rows, z.cols)
    frame = (np.arange(z.N)[:, None] * z.CF + np.arange(z.CF)[None, :]).astype(np.float32)
    frame = np.broadcast_to(frame[:, None, :, None, None], shape)
    prow = (np.arange(z.R)[:, None] * z.rows + np.arange(z.rows)[None, :]).astype(np.float32)
    prow = np.broadcast_to(prow[None, :, None, :, None], shape)
    pcol = np.broadcast_to(np.arange(z.cols, dtype=np.float32), shape)
    angle = np.concatenate(
        [frame[..., None] * freq(fp), prow[..., None] * freq(rp), pcol[..., None] * freq(cp)], -1
    ).astype(np.float32)
    angle = angle.reshape(z.N, z.W, half)
    cos, sin = np.cos(angle), np.sin(angle)
    return np.concatenate([cos, cos, sin, sin], -1).astype(np.float32)


def remote(src, dst, send_sem, recv_sem, device):
    return pltpu.make_async_remote_copy(
        src_ref=src, dst_ref=dst, send_sem=send_sem, recv_sem=recv_sem, device_id=device, device_id_type=MESH
    )


def place(n, z):
    n.clip = lax.axis_index("clip")
    n.row = lax.axis_index("row")
    n.sib = n.clip + 1 - 2 * (n.clip % 2)
    n.row_peer = [(n.row + k) % z.R for k in range(1, z.R)]
    n.clip_peer = [(n.clip + k) % z.C for k in range(1, z.C)]
    n.square = z.R == 4
    n.far = (n.row + 1 - 2 * (n.row % 2) + 2) % z.R
    n.x = (n.clip, n.row + 1 - 2 * (n.row % 2))
    n.y = (n.clip, (n.row + 2) % z.R)
    n.arrivals = 2 if n.square else z.R - 1
    n.line = z.C == 8
    place = n.clip // 2
    n.inner = jnp.logical_or(place == 1, place == 2)
    n.far_end = jnp.where(n.inner, n.clip + 4 - 8 * (place // 2), n.clip)
    n.near_end = jnp.where(n.inner, n.clip - 2 + 4 * (place // 2), n.clip)
    n.relay_to = jnp.where(place == 0, n.clip + 2, (n.clip - 2 + z.C) % z.C)
    n.core_peer = [(n.clip + 2 * k) % z.C for k in range(1, z.C // 2)]


def enter(n, z):
    barrier = pltpu.get_barrier_semaphore()
    for p in n.row_peer:
        pl.semaphore_signal(barrier, inc=1, device_id=(n.clip, p), device_id_type=MESH)
    for p in n.clip_peer:
        pl.semaphore_signal(barrier, inc=1, device_id=(p, n.row), device_id_type=MESH)
    pl.semaphore_wait(barrier, z.R + z.C - 2)


def send(src, dst, sems, slot, land, device):
    remote(src, dst, sems.at[(0,) + slot], sems.at[(1,) + land], device).start()


def sent(ref, sems, slot, device):
    remote(ref, ref, sems.at[(0,) + slot], sems.at[(1,) + slot], device).wait_send()


def got(ref, sems, slot, device):
    remote(ref, ref, sems.at[(0,) + slot], sems.at[(1,) + slot], device).wait_recv()


def halves(n, ref, c, p):
    rows = ref.shape[2] // 2
    return ref.at[c, p, :rows], ref.at[c, p, rows:]


def gather_row(n, full, sems, c):
    mine = full.at[c, n.row]
    if n.square:
        send(mine, mine, sems, (c, 0), (c, 0), n.x)
        send(mine, mine, sems, (c, 1), (c, 1), n.y)
        return
    for k, p in enumerate(n.row_peer):
        back = len(n.row_peer) - 1 - k
        send(mine, mine, sems, (c, k), (c, back), (n.clip, p))


def gather_more(n, full, sems, c):
    if n.square:
        got(full.at[c, n.x[1]], sems, (c, 0), n.x)
        block = halves(n, full, c, n.x[1])[0]
        send(block, block, sems, (c, 2), (c, 2), n.y)
        got(full.at[c, n.y[1]], sems, (c, 1), n.y)
        block = halves(n, full, c, n.y[1])[1]
        send(block, block, sems, (c, 3), (c, 3), n.x)


def gather_row_wait(n, full, sems, c):
    if n.square:
        low, high = halves(n, full, c, n.far)
        got(low, sems, (c, 2), n.y)
        got(high, sems, (c, 3), n.x)
        mine = full.at[c, n.row]
        sent(mine, sems, (c, 0), n.x)
        sent(mine, sems, (c, 1), n.y)
        sent(low, sems, (c, 2), n.y)
        sent(high, sems, (c, 3), n.x)
        return
    for k, p in enumerate(n.row_peer):
        block = full.at[c, p]
        got(block, sems, (c, k), (n.clip, p))
        sent(block, sems, (c, k), (n.clip, p))


def scatter_row(n, parts, landed, sems, c):
    if n.square:
        (xl, _), (_, yh), (fl, fh) = (halves(n, parts, c, p) for p in (n.x[1], n.y[1], n.far))
        send(fl, halves(n, landed, c, 2)[0], sems, (c, 0), (c, 0), n.x)
        send(fh, halves(n, landed, c, 2)[1], sems, (c, 1), (c, 1), n.y)
        send(xl, halves(n, landed, c, 0)[0], sems, (c, 2), (c, 2), n.x)
        send(yh, halves(n, landed, c, 1)[1], sems, (c, 3), (c, 3), n.y)
        return
    for k, p in enumerate(n.row_peer):
        back = len(n.row_peer) - 1 - k
        send(parts.at[c, p], landed.at[c, back], sems, (c, k), (c, back), (n.clip, p))


def scatter_more(n, parts, landed, sems, c):
    if n.square:
        rows = parts.shape[2] // 2
        low, high = halves(n, landed, c, 2)
        got(low, sems, (c, 0), n.x)
        parts[c, n.y[1], :rows] = (parts[c, n.y[1], :rows].astype(f32) + low[...].astype(f32)).astype(bf16)
        send(halves(n, parts, c, n.y[1])[0], halves(n, landed, c, 1)[0], sems, (c, 5), (c, 5), n.y)
        got(high, sems, (c, 1), n.y)
        parts[c, n.x[1], rows:] = (parts[c, n.x[1], rows:].astype(f32) + high[...].astype(f32)).astype(bf16)
        send(halves(n, parts, c, n.x[1])[1], halves(n, landed, c, 0)[1], sems, (c, 4), (c, 4), n.x)


def scatter_row_wait(n, parts, landed, sems, c):
    if n.square:
        (xl, xh), (yl, yh) = (halves(n, landed, c, k) for k in range(2))
        for slot, ref, peer in ((2, xl, n.x), (3, yh, n.y), (4, xh, n.x), (5, yl, n.y)):
            got(ref, sems, (c, slot), peer)
        for slot in range(6):
            sent(xl, sems, (c, slot), n.x)
        return
    for k, p in enumerate(n.row_peer):
        got(landed.at[c, k], sems, (c, k), (n.clip, p))
        sent(landed.at[c, k], sems, (c, k), (n.clip, p))


def share_row(n, buf, sems):
    for k, p in enumerate(n.row_peer):
        mine = buf.at[n.row]
        remote(mine, mine, sems.at[0, k], sems.at[1, n.row], (n.clip, p)).start()


def share_row_wait(n, buf, sems):
    for k, p in enumerate(n.row_peer):
        block = buf.at[p]
        remote(block, block, sems.at[0, k], sems.at[1, p], (n.clip, p)).wait()


def swap_row(n, src, dst, sems):
    for k, p in enumerate(n.row_peer):
        remote(src.at[p], dst.at[n.row], sems.at[0, k], sems.at[1, n.row], (n.clip, p)).start()


def swap_row_wait(n, src, dst, sems):
    for k, p in enumerate(n.row_peer):
        remote(src.at[p], dst.at[p], sems.at[0, k], sems.at[1, p], (n.clip, p)).wait()


def share_clip(n, buf, sems):
    for k, p in enumerate(n.clip_peer):
        mine = buf.at[n.clip]
        remote(mine, mine, sems.at[0, k], sems.at[1, n.clip], (p, n.row)).start()


def share_clip_wait(n, buf, sems):
    for k, p in enumerate(n.clip_peer):
        block = buf.at[p]
        remote(block, block, sems.at[0, k], sems.at[1, p], (p, n.row)).wait()


def swap_clip(n, src, dst, sems):
    for k, p in enumerate(n.clip_peer):
        remote(src.at[p], dst.at[n.clip], sems.at[0, k], sems.at[1, n.clip], (p, n.row)).start()


def swap_clip_wait(n, src, dst, sems):
    for k, p in enumerate(n.clip_peer):
        remote(src.at[p], dst.at[p], sems.at[0, k], sems.at[1, p], (p, n.row)).wait()


def skipped(n, z, p, relayed):
    if not relayed or not n.line:
        return None
    return jnp.logical_and(n.clip // 2 + p // 2 == 3, jnp.logical_not(n.inner))


def unless(skip, work):
    if skip is None:
        work()
    else:
        pl.when(jnp.logical_not(skip))(work)


def weight_send(n, z, buf, sems, relayed=False):
    mine = buf.at[n.clip]
    remote(mine, mine, sems.at[0, 0], sems.at[1, n.clip], (n.sib, n.row)).start()
    for k, p in enumerate(n.core_peer):
        copy = remote(mine, mine, sems.at[0, 1 + k], sems.at[1, n.clip], (p, n.row))
        unless(skipped(n, z, p, relayed), copy.start)


def weight_relay(n, z, buf, sems):
    if n.line:

        @pl.when(n.inner)
        def _():
            block = buf.at[n.far_end]
            remote(block, block, sems.at[0, 0], sems.at[1, n.far_end], (n.far_end, n.row)).wait_recv()
            remote(block, block, sems.at[0, z.C - 1], sems.at[1, n.far_end], (n.near_end, n.row)).start()


def weight_forward(n, z, buf, sems, relayed=False):
    for k, p in enumerate(n.core_peer):
        block = buf.at[p]
        known = jnp.logical_and(n.inner, p == n.far_end) if relayed and n.line else None
        unless(known, remote(block, block, sems.at[0, 1 + k], sems.at[1, p], (p, n.row)).wait_recv)
        remote(block, block, sems.at[0, z.C // 2 + k], sems.at[1, p], (n.sib, n.row)).start()


def weight_wait(n, z, buf, sems, relayed=False):
    block = buf.at[n.sib]
    remote(block, block, sems.at[0, 0], sems.at[1, n.sib], (n.sib, n.row)).wait()
    for k, p in enumerate(n.core_peer):
        j = (p // 2) * 2 + n.sib % 2
        block = buf.at[j]
        remote(block, block, sems.at[0, 1 + k], sems.at[1, j], (n.sib, n.row)).wait_recv()
        unless(skipped(n, z, p, relayed), remote(block, block, sems.at[0, 1 + k], sems.at[1, j], (n.sib, n.row)).wait_send)
        remote(block, block, sems.at[0, z.C // 2 + k], sems.at[1, j], (n.sib, n.row)).wait_send()
    if relayed and n.line:
        pl.when(n.inner)(remote(block, block, sems.at[0, z.C - 1], sems.at[1, n.sib], (n.sib, n.row)).wait_send)


def flat(x):
    return x.reshape((-1, x.shape[-1]))


def normed(x):
    centre = x - jnp.mean(x, -1, keepdims=True)
    rstd = lax.rsqrt(jnp.mean(centre * centre, -1, keepdims=True) + norm_eps)
    return centre * rstd, rstd


def norm_pull(n_hat, rstd, scale, grad):
    d_shift = jnp.sum(grad, 0, keepdims=True)
    d_scale = jnp.sum(grad * n_hat, 0, keepdims=True)
    dn = grad * (1.0 + scale)
    dx = rstd * (dn - jnp.mean(dn, -1, keepdims=True) - n_hat * jnp.mean(dn * n_hat, -1, keepdims=True))
    return dx, d_shift, d_scale


def vec(n, which, frame):
    return n.mod[which, pl.ds(frame, 1), :]


def frame_rows(z, c, i):
    return pl.ds(pl.multiple_of((c * z.CF + i) * z.LT, z.LT), z.LT)


def tables(n, c):
    x = n.tab[c]
    lane = lax.broadcasted_iota(jnp.int32, x.shape, 1)
    y = pltpu.roll(x, 64, 1)
    sin = jnp.where(lane < 64, y, x)
    return jnp.where(lane < 64, x, y), jnp.where(lane % HSIZE < HSIZE // 2, -sin, sin)


def turn(x, cos, sin):
    lane = lax.broadcasted_iota(jnp.int32, x.shape, 1)
    other = jnp.where(lane % HSIZE < HSIZE // 2, pltpu.roll(x, 128 - HSIZE // 2, 1), pltpu.roll(x, HSIZE // 2, 1))
    return x * cos + other * sin


def gelu_parts(x):
    k = math.sqrt(2.0 / math.pi)
    t = jnp.tanh(k * (x + 0.044715 * (x * x * x)))
    value = 0.5 * x * (1.0 + t)
    slope = 0.5 * (1.0 + t) + 0.5 * x * (1.0 - t * t) * (k * (1.0 + 3 * 0.044715 * (x * x)))
    return value, slope


def causal(z):
    a = (lax.broadcasted_iota(jnp.int32, (z.W, z.W), 0) % z.CT) // z.LT
    b = (lax.broadcasted_iota(jnp.int32, (z.W, z.W), 1) % z.CT) // z.LT
    return a, b


def after(z, c, more):
    if z.N > 1:
        pl.when(c > 0)(lambda: more(c - 1))


def last(z, c, more):
    if z.N > 1:
        pl.when(c == 0)(lambda: more(z.N - 1))


def phase_level(n, z):
    n.lv[n.clip] = n.w_level[...].astype(bf16)
    n.ea[n.clip] = n.emb[...]
    pw, hr = D // z.R, z.DR // z.R
    n.pq[n.row, n.clip] = n.w_patch[:, pl.ds(pl.multiple_of(n.row * pw, pw), pw)].astype(n.pq.dtype)
    n.hq[n.row, n.clip] = n.w_head[pl.ds(pl.multiple_of(n.row * hr, hr), hr), :].astype(n.hq.dtype)
    enter(n, z)
    share_clip(n, n.ea, n.ea_s)
    share_clip(n, n.lv, n.lv_s)
    share_clip(n, n.pq.at[n.row], n.pq_s)
    for k in range(3):
        n.Wp[n.clip, :, k * z.HW : (k + 1) * z.HW] = n.wp[k].astype(bf16)
    n.Wo[n.clip] = jnp.transpose(n.wo[...]).astype(bf16)
    weight_send(n, z, n.Wo, n.Wo_s)
    tiles = z.FH // 128
    for t in range(tiles):
        for k in range(2):
            at = k * z.FH + t * 128
            n.Wg[n.clip, :, at : at + 128] = n.wg[pl.ds(2 * t + k, z.DR, stride=2 * tiles), :].astype(bf16)
    n.Wd[n.clip] = jnp.transpose(n.wd[...]).astype(bf16)
    share_clip_wait(n, n.ea, n.ea_s)
    share_clip_wait(n, n.lv, n.lv_s)
    pre = dot_nn(flat(n.ea[...]), flat(n.lv[...]))
    n.pre[...] = pre
    cond = (pre * (1.0 / (1.0 + jnp.exp(-pre)))).astype(bf16)
    n.cond[...] = cond
    part = dot_nn(cond, n.w_adapt[...].astype(bf16))
    for p in range(z.R):
        for i in range(z.C):
            block = part[i * PAD : i * PAD + z.F, p * z.aw : (p + 1) * z.aw]
            n.pa[p, i * z.F : (i + 1) * z.F, :] = block
    swap_row(n, n.pa, n.ra, n.ra_s)
    share_clip_wait(n, n.pq.at[n.row], n.pq_s)
    share_row(n, n.pq, n.pr_s)
    swap_row_wait(n, n.pa, n.ra, n.ra_s)
    total = n.pa[n.row]
    for p in n.row_peer:
        total = total + n.ra[p]
    n.rs[...] = jnp.zeros_like(n.rs)
    for i in range(z.C):
        n.rs[i, : z.F, :] = total[i * z.F : (i + 1) * z.F]
    n.rb[n.clip] = n.rs[n.clip]
    swap_clip(n, n.rs, n.rb, n.rb_s)
    weight_send(n, z, n.Wp, n.Wp_s)
    share_row_wait(n, n.pq, n.pr_s)
    patch = jnp.concatenate([flat(n.pq[r]) for r in range(z.R)], -1).astype(bf16)
    for c in range(z.N):
        rows = slice(c * z.CT, (c + 1) * z.CT)
        n.stream[rows, :] = dot_nn(n.inputs[rows, :], patch)
    send_hat(n, z, 0)
    swap_clip_wait(n, n.rs, n.rb, n.rb_s)
    for i in range(z.C):
        n.ab[n.row, i * z.F : (i + 1) * z.F, :] = n.rb[i, : z.F, :]
    share_row(n, n.ab, n.ab_s)
    share_clip(n, n.hq.at[n.row], n.hq_s)
    weight_send(n, z, n.Wg, n.Wg_s, True)
    weight_send(n, z, n.Wd, n.Wd_s)
    for c in range(1, z.N):
        send_hat(n, z, c)
        gather_more(n, n.one, n.one_s, c - 1)
    n.mod[...] = jnp.zeros_like(n.mod)
    share_row_wait(n, n.ab, n.ab_s)
    for i in range(z.C):
        for r in range(z.R):
            col = i * z.AW + r * z.aw
            n.mod[col // D, : z.F, col % D : col % D + z.aw] = n.ab[r, i * z.F : (i + 1) * z.F, :]


def send_hat(n, z, c):
    def frame(i, _):
        hat, unused = normed(n.stream[frame_rows(z, c, i), :])
        n.one[c, n.row, pl.ds(pl.multiple_of(i * z.LT, z.LT), z.LT), :] = hat.astype(bf16)
        return 0

    lax.fori_loop(0, z.CF, frame, 0)
    gather_row(n, n.one, n.one_s, c)


def modulate_chunk(n, z, c):
    def frame(step, _):
        p, i = step // z.CF, step % z.CF
        f = c * z.CF + i
        rows = pl.ds(pl.multiple_of(i * z.LT, z.LT), z.LT)
        y = n.one[c, p, rows, :].astype(f32) * (1.0 + vec(n, 1, f)) + vec(n, 0, f)
        n.one[c, p, rows, :] = y.astype(bf16)
        return 0

    lax.fori_loop(0, z.R * z.CF, frame, 0)


def phase_attend(n, z):
    queries = 384 if z.W % 384 == 0 else z.W
    parts = z.W // queries
    weight_forward(n, z, n.Wp, n.Wp_s)
    weight_wait(n, z, n.Wp, n.Wp_s)

    def chunk(c, _):
        if z.N == 1:
            gather_more(n, n.one, n.one_s, c)
        gather_row_wait(n, n.one, n.one_s, c)
        modulate_chunk(n, z, c)
        x = flat(n.one[c])
        pr = dot_nn(x, flat(n.Wp[...]))
        cos, sin = tables(n, c)
        for which in range(3):
            dest = (n.q, n.k, n.v)[which]
            for g in range(z.HW // 128):
                at = which * z.HW + g * 128
                y = pr[:, at : at + 128]
                if which < 2:
                    y = turn(y, cos, sin)
                if which == 0:
                    y = y * HSIZE**-0.5
                y = y.astype(bf16)
                for s in range(128 // HSIZE):
                    dest[g * (128 // HSIZE) + s, c] = y[:, s * HSIZE : (s + 1) * HSIZE]

        def heads(past):
            def head(step, _):
                h, u = step // parts, step % parts
                at = pl.ds(pl.multiple_of(u * queries, queries), queries)
                q = n.q[h, past, at, :]
                s = dot_nt(q, n.k[h, past])
                a = (lax.broadcasted_iota(jnp.int32, s.shape, 0) + u * queries) % z.CT // z.LT
                b = lax.broadcasted_iota(jnp.int32, s.shape, 1) % z.CT // z.LT
                scores = [dot_nt(q, n.k[h, j]) for j in range(past)] + [jnp.where(b <= a, s, -1e30)]
                m = functools.reduce(jnp.maximum, [jnp.max(s, -1, keepdims=True) for s in scores])
                exps = [jnp.exp(s - m) for s in scores]
                total = sum(jnp.sum(e, -1, keepdims=True) for e in exps)
                o = sum(dot_nn(e.astype(bf16), n.v[h, j]) for j, e in enumerate(exps))
                n.oh[h, at, :] = o / total
                lse = jnp.broadcast_to(m + jnp.log(total), (queries, 128))
                n.lse[h, past, :, at] = jnp.transpose(lse)[:8]
                return 0

            lax.fori_loop(0, z.HD * parts, head, 0)

        for past in range(z.N):
            pl.when(c == past)(functools.partial(heads, past))

        @pl.when(c == 0)
        def _():
            weight_forward(n, z, n.Wo, n.Wo_s)
            weight_wait(n, z, n.Wo, n.Wo_s)

        att = jnp.concatenate([n.oh[h] for h in range(z.HD)], -1)
        n.att[c] = att
        n.sb[c] = dot_nt(att.astype(bf16), flat(n.Wo[...])).astype(bf16).reshape(z.R, z.CT, D)
        last(z, c, lambda d: gather_more(n, n.one, n.one_s, d))
        scatter_row(n, n.sb, n.rsr, n.br_s, c)
        pl.when(c == (z.N - 1) // 2)(lambda: weight_relay(n, z, n.Wg, n.Wg_s))
        after(z, c, lambda d: scatter_more(n, n.sb, n.rsr, n.br_s, d))
        return 0

    lax.fori_loop(0, z.N, chunk, 0)


def summed(n, z, c, i):
    rows = pl.ds(pl.multiple_of(i * z.LT, z.LT), z.LT)
    total = n.sb[c, n.row, rows, :].astype(f32)
    for k in range(n.arrivals):
        total = total + n.rsr[c, k, rows, :].astype(f32)
    return total


def phase_two(n, z):
    def chunk(c, _):
        if z.N == 1:
            scatter_more(n, n.sb, n.rsr, n.br_s, c)
        scatter_row_wait(n, n.sb, n.rsr, n.br_s, c)

        def frame(i, _):
            f = c * z.CF + i
            rows = frame_rows(z, c, i)
            branch = summed(n, z, c, i)
            n.branch[rows, :] = branch
            mid = n.stream[rows, :] + vec(n, 2, f) * branch
            hat, unused = normed(mid)
            y = hat * (1.0 + vec(n, 4, f)) + vec(n, 3, f)
            n.two[c, n.row, pl.ds(pl.multiple_of(i * z.LT, z.LT), z.LT), :] = y.astype(bf16)
            return 0

        lax.fori_loop(0, z.CF, frame, 0)
        last(z, c, lambda d: scatter_more(n, n.sb, n.rsr, n.br_s, d))
        gather_row(n, n.two, n.two_s, c)
        after(z, c, lambda d: gather_more(n, n.two, n.two_s, d))
        return 0

    lax.fori_loop(0, z.N, chunk, 0)


def phase_feed(n, z):
    share_clip_wait(n, n.hq.at[n.row], n.hq_s)
    share_row(n, n.hq, n.hr_s)
    weight_forward(n, z, n.Wg, n.Wg_s, True)
    weight_wait(n, z, n.Wg, n.Wg_s, True)
    tile = 256

    def chunk(c, _):
        if z.N == 1:
            gather_more(n, n.two, n.two_s, c)
        gather_row_wait(n, n.two, n.two_s, c)

        def column(t, _):
            at = pl.ds(pl.multiple_of(t * tile, tile), tile)
            up_at = pl.ds(pl.multiple_of(z.FH + t * tile, tile), tile)
            x = flat(n.two[c])
            gate = dot_nn(x, flat(n.Wg[:, :, at]))
            up = dot_nn(x, flat(n.Wg[:, :, up_at]))
            value, unused = gelu_parts(gate)
            n.act[c, :, at] = (value * up).astype(bf16)
            n.gu[c, :, at] = gate.astype(bf16)
            n.gu[c, :, up_at] = up.astype(bf16)
            return 0

        lax.fori_loop(0, z.FH // tile, column, 0)

        @pl.when(c == 0)
        def _():
            weight_forward(n, z, n.Wd, n.Wd_s)
            weight_wait(n, z, n.Wd, n.Wd_s)

        slabs = tile // z.DR

        def output(t, _):
            y = dot_nt(n.act[c], flat(n.Wd[pl.ds(t * slabs, slabs)]))
            at = pl.ds(pl.multiple_of(t * tile, tile), tile)
            n.sb[c, :, :, at] = y.astype(bf16).reshape(z.R, z.CT, tile)
            return 0

        lax.fori_loop(0, D // tile, output, 0)
        last(z, c, lambda d: gather_more(n, n.two, n.two_s, d))
        scatter_row(n, n.sb, n.rsr, n.fd_s, c)
        after(z, c, lambda d: scatter_more(n, n.sb, n.rsr, n.fd_s, d))
        return 0

    lax.fori_loop(0, z.N, chunk, 0)


def phase_top(n, z):
    share_row_wait(n, n.hq, n.hr_s)
    hr = z.DR // z.R
    for i in range(z.C):
        for r in range(z.R):
            n.Wh[i, r * hr : (r + 1) * hr, :] = n.hq[r, i].astype(bf16)
    n.ghead[...] = jnp.zeros_like(n.ghead)
    n.loss[...] = jnp.zeros_like(n.loss)
    n.gad[...] = jnp.zeros_like(n.gad)

    def chunk(c, _):
        if z.N == 1:
            scatter_more(n, n.sb, n.rsr, n.fd_s, c)
        scatter_row_wait(n, n.sb, n.rsr, n.fd_s, c)

        def ahead(i, _):
            f = c * z.CF + i
            rows = frame_rows(z, c, i)
            here = pl.ds(pl.multiple_of(i * z.LT, z.LT), z.LT)
            feed = summed(n, z, c, i)
            mid = n.stream[rows, :] + vec(n, 2, f) * n.branch[rows, :]
            n.feed[here, :] = feed
            hat, rstd = normed(mid + vec(n, 5, f) * feed)
            n.hat[here, :] = hat
            n.rstd[here, :] = jnp.broadcast_to(rstd, (z.LT, 128))
            n.end[here, :] = (hat * (1.0 + vec(n, 7, f)) + vec(n, 6, f)).astype(bf16)
            return 0

        lax.fori_loop(0, z.CF, ahead, 0)
        rows = pl.ds(pl.multiple_of(c * z.CT, z.CT), z.CT)
        missed = dot_nn(n.end[...], flat(n.Wh[...])) - n.noise[rows, :]
        weight = n.fw[rows, :]
        n.loss[...] += jnp.sum((weight * (missed * missed)).reshape(z.CT // 8, 8, z.PF), 0)
        gp = ((2.0 / z.PF) * weight * missed).astype(bf16)
        n.ghead[...] += dot_tn(n.end[...], gp)
        n.gend[...] = dot_nt(gp, flat(n.Wh[...]))

        def back(i, _):
            f = c * z.CF + i
            rows = frame_rows(z, c, i)
            here = pl.ds(pl.multiple_of(i * z.LT, z.LT), z.LT)
            dx, d_shift, d_scale = norm_pull(n.hat[here, :], n.rstd[here, :1], vec(n, 7, f), n.gend[here, :])
            n.gad[6, pl.ds(f, 1), :] = d_shift
            n.gad[7, pl.ds(f, 1), :] = d_scale
            n.gad[5, pl.ds(f, 1), :] = jnp.sum(dx * n.feed[here, :], 0, keepdims=True)
            n.gmid[rows, :] = dx
            n.gf[c, n.row, here, :] = (dx * vec(n, 5, f)).astype(bf16)
            return 0

        lax.fori_loop(0, z.CF, back, 0)
        last(z, c, lambda d: scatter_more(n, n.sb, n.rsr, n.fd_s, d))
        gather_row(n, n.gf, n.gf_s, c)
        after(z, c, lambda d: gather_more(n, n.gf, n.gf_s, d))
        return 0

    lax.fori_loop(0, z.N, chunk, 0)


def run(body, z, cid, ins, anys, outs, scratch, export, vmem):
    names = list(ins) + list(anys) + list(outs) + list(scratch)

    def kernel(*refs):
        n = types.SimpleNamespace(**dict(zip(names, refs)))
        place(n, z)
        body(n, z)

    result = pl.pallas_call(
        kernel,
        out_shape=[jax.ShapeDtypeStruct(s, d) for s, d in outs.values()],
        in_specs=[pl.BlockSpec(memory_space=pltpu.VMEM)] * len(ins) + [pl.BlockSpec(memory_space=pl.ANY)] * len(anys),
        out_specs=[pl.BlockSpec(memory_space=pl.ANY if k in export else pltpu.VMEM) for k in outs],
        scratch_shapes=list(scratch.values()),
        compiler_params=pltpu.CompilerParams(collective_id=cid, has_side_effects=True, vmem_limit_bytes=vmem),
    )(*ins.values(), *anys.values())
    return dict(zip(outs, result))


KEPT = ("one", "two", "gf", "Wp", "Wo", "Wg", "Wd", "q", "k", "v", "att", "lse", "gu", "act", "stream", "branch", "gmid", "mod")


def forward_body(n, z):
    def export(*names):
        for name in names:
            i = KEPT.index(name)
            pltpu.make_async_copy(getattr(n, name), getattr(n, name + "_o"), n.ex_s.at[i]).start()

    phase_level(n, z)
    export("mod", "stream")
    phase_attend(n, z)
    export("one", "Wp", "Wo", "q", "k", "v", "att", "lse")
    phase_two(n, z)
    export("branch")
    phase_feed(n, z)
    export("two", "Wg", "Wd", "gu", "act")
    phase_top(n, z)
    export("gmid")
    gather_more(n, n.gf, n.gf_s, z.N - 1)
    for c in range(z.N):
        gather_row_wait(n, n.gf, n.gf_s, c)
    export("gf")
    for i, name in enumerate(KEPT):
        pltpu.make_async_copy(getattr(n, name), getattr(n, name + "_o"), n.ex_s.at[i]).wait()


def shapes_of(z):
    rowed = (z.N, z.R, z.CT, D)
    return {
        "one": (rowed, bf16),
        "two": (rowed, bf16),
        "gf": (rowed, bf16),
        "gb": (rowed, bf16),
        "sb": (rowed, bf16),
        "rsr": ((z.N, z.R - 1, z.CT, D), bf16),
        "Wp": ((z.C, z.DR, 3 * z.HW), bf16),
        "Wo": ((z.C, z.DR, z.HW), bf16),
        "Wg": ((z.C, z.DR, 2 * z.FH), bf16),
        "Wd": ((z.C, z.DR, z.FH), bf16),
        "Wh": ((z.C, z.DR, z.PF), bf16),
        "q": ((z.HD, z.N, z.W, HSIZE), bf16),
        "k": ((z.HD, z.N, z.W, HSIZE), bf16),
        "v": ((z.HD, z.N, z.W, HSIZE), bf16),
        "att": ((z.N, z.W, z.HW), f32),
        "oh": ((z.HD, z.W, HSIZE), f32),
        "lse": ((z.HD, z.N, 8, z.W), f32),
        "gu": ((z.N, z.W, 2 * z.FH), bf16),
        "act": ((z.N, z.W, z.FH), bf16),
        "stream": ((z.T, D), f32),
        "branch": ((z.T, D), f32),
        "gmid": ((z.T, D), f32),
        "mod": ((VECTORS, PAD, D), f32),
        "gad": ((VECTORS, PAD, D), f32),
        "ghead": ((D, z.PF), f32),
        "loss": ((8, z.PF), f32),
        "pre": ((z.C * PAD, z.LW), f32),
        "cond": ((z.C * PAD, z.LW), bf16),
        "lv": ((z.C, z.LR, z.LW), bf16),
        "ea": ((z.C, PAD, TF), bf16),
        "pq": ((z.R, z.C, z.PF // z.C, D // z.R), f32 if z.PF // z.C % 16 else bf16),
        "hq": ((z.R, z.C, z.DR // z.R, z.PF), f32 if z.DR // z.R % 16 else bf16),
        "pa": ((z.R, z.C * z.F, z.aw), f32),
        "ra": ((z.R, z.C * z.F, z.aw), f32),
        "rs": ((z.C, PAD, z.aw), f32),
        "rb": ((z.C, PAD, z.aw), f32),
        "ab": ((z.R, z.C * z.F, z.aw), f32),
        "feed": ((z.CT, D), f32),
        "hat": ((z.CT, D), f32),
        "rstd": ((z.CT, 128), f32),
        "end": ((z.CT, D), bf16),
        "gend": ((z.CT, D), f32),
    }


def vm(shapes, names):
    return {k: pltpu.VMEM(*shapes[k]) for k in names}


def forward_call(z, ins):
    sh = shapes_of(z)
    direct = ("gad", "ghead", "loss", "pre", "cond", "ea")
    outs = {k: sh[k] for k in direct}
    outs.update({k + "_o": sh[k] for k in KEPT})
    rest = ["Wh", "oh", "sb", "rsr", "lv", "pq", "hq", "pa", "ra", "rs", "rb", "ab", "feed", "hat", "rstd", "end", "gend"]
    scratch = vm(sh, list(KEPT) + rest)
    dma = pltpu.SemaphoreType.DMA
    for k in ("ea_s", "lv_s", "pq_s", "rb_s", "hq_s", "Wp_s", "Wo_s", "Wg_s", "Wd_s"):
        scratch[k] = dma((2, z.C))
    for k in ("ra_s", "ab_s", "pr_s", "hr_s"):
        scratch[k] = dma((2, z.R))
    for k in ("one_s", "br_s", "two_s", "fd_s", "gf_s"):
        scratch[k] = dma((2, z.N, max(6, z.R)))
    scratch["ex_s"] = dma((len(KEPT),))
    got = run(forward_body, z, 0, ins, {}, outs, scratch, [k + "_o" for k in KEPT], 60 << 20)
    return {(k[:-2] if k.endswith("_o") else k): v for k, v in got.items()}


def forward_inputs(z, a):
    alpha_bar, frame_weight = noise_plan(a["levels"])
    latents = a["latents"].reshape(z.F, z.LT, z.PF)
    noise = a["noise"].reshape(z.F, z.LT, z.PF)
    noisy = jnp.sqrt(alpha_bar)[0, :, None, None] * latents + jnp.sqrt(1.0 - alpha_bar)[0, :, None, None] * noise
    emb = level_embedding(a["levels"][0], TF // 2).astype(bf16)
    return {
        "emb": jnp.pad(emb, ((0, PAD - z.F), (0, 0))),
        "w_level": a["w_level"],
        "w_patch": a["w_patch"],
        "w_head": a["w_head"],
        "w_adapt": a["w_adapt"],
        "wp": jnp.transpose(a["w_project"], (1, 0, 2)),
        "wo": a["w_output"],
        "wg": packed(a["w_gateup"]),
        "wd": a["w_down"],
        "inputs": noisy.astype(bf16).reshape(z.T, z.PF),
        "noise": noise.reshape(z.T, z.PF),
        "fw": jnp.broadcast_to(frame_weight[0][:, None, None], (z.F, z.LT, z.PF)).reshape(z.T, z.PF),
        "tab": jnp.asarray(rotary_consts(z)),
    }, frame_weight


def fetch(n, name):
    i = LOADED.index(name)
    return pltpu.make_async_copy(getattr(n, name + "_i"), getattr(n, name), n.in_s.at[i])


def phase_pull_feed(n, z):
    tile = 256
    for name in ("Wd", "gu", "gf"):
        fetch(n, name).wait()

    def chunk(s, _):
        c = z.N - 1 - s
        def column(t, _):
            at = pl.ds(pl.multiple_of(t * tile, tile), tile)
            up_at = pl.ds(pl.multiple_of(z.FH + t * tile, tile), tile)
            da = dot_nn(flat(n.gf[c]), flat(n.Wd[:, :, at]))
            value, slope = gelu_parts(n.gu[c, :, at].astype(f32))
            up = n.gu[c, :, up_at].astype(f32)
            n.gu[c, :, at] = (da * up * slope).astype(bf16)
            n.gu[c, :, up_at] = (da * value).astype(bf16)
            return 0

        lax.fori_loop(0, z.FH // tile, column, 0)

        @pl.when(s == 0)
        def _():
            fetch(n, "Wg").wait()

        slabs = tile // z.DR

        def output(t, _):
            y = dot_nt(n.gu[c], flat(n.Wg[pl.ds(t * slabs, slabs)]))
            at = pl.ds(pl.multiple_of(t * tile, tile), tile)
            n.sb[c, :, :, at] = y.astype(bf16).reshape(z.R, z.CT, tile)
            return 0

        lax.fori_loop(0, D // tile, output, 0)
        scatter_row(n, n.sb, n.rsr, n.gt_s, c)
        after(z, s, lambda d: scatter_more(n, n.sb, n.rsr, n.gt_s, z.N - 1 - d))
        return 0

    lax.fori_loop(0, z.N, chunk, 0)


def weight_grad(n, z, left, right, into):
    half = n.tb.shape[0]
    width = right.shape[-1]
    tile = min(256, width)
    slabs = half // z.DR
    for part in range(D // half):
        for c in range(z.N):
            block = left[c, :, :, part * half : (part + 1) * half]
            n.tb[:, c * z.W : (c + 1) * z.W] = jnp.transpose(flat(block))

        def column(t, _):
            at = pl.ds(pl.multiple_of(t * tile, tile), tile)
            y = dot_nn(n.tb[...], flat(right[:, :, at]).astype(bf16))
            into[part * slabs : (part + 1) * slabs, :, at] = y.astype(bf16).reshape(slabs, z.DR, tile)
            return 0

        lax.fori_loop(0, width // tile, column, 0)


def reduce_one(n, z, part, sx, sems):
    for k in range(z.C // 2):
        j = (n.sib + 2 * k) % z.C
        remote(part.at[j], sx.at[j // 2], sems.at[0, k], sems.at[1, j // 2], (n.sib, n.row)).start()


def reduce_two(n, z, part, sx, sems, rx, more, width, relayed):
    for k in range(z.C // 2):
        j = (n.clip + 2 * k) % z.C
        mine = (n.sib + 2 * k) % z.C
        remote(part.at[mine], sx.at[j // 2], sems.at[0, k], sems.at[1, j // 2], (n.sib, n.row)).wait()
        part[j] = (part[j].astype(f32) + sx[j // 2].astype(f32)).astype(bf16)
        if k:
            back = z.C // 2 - k - 1
            at = slice(0, width)
            copy = remote(part.at[j, :, at], rx.at[back, :, at], more.at[0, k], more.at[1, back], (j, n.row))
            if relayed:
                skip = skipped(n, z, j, True)
                hold = jnp.logical_and(n.inner, k == 2)
                pl.when(jnp.logical_not(jnp.logical_or(skip, hold)))(copy.start)
                pl.when(skip)(remote(part.at[j], n.Xg, n.Xg_s.at[0], n.Xg_s.at[1], (n.relay_to, n.row)).start)
            else:
                copy.start()


def reduce_relay(n, z):
    if n.line:

        @pl.when(n.inner)
        def _():
            j = (n.clip + 4) % z.C
            remote(n.Wg.at[j], n.Xg, n.Xg_s.at[0], n.Xg_s.at[1], (j, n.row)).wait_recv()
            n.Wg[j] = (n.Wg[j].astype(f32) + n.Xg[...].astype(f32)).astype(bf16)
            back = z.C // 2 - 3
            remote(n.Wg.at[j], n.Rg.at[back], n.Rg_s.at[0, 2], n.Rg_s.at[1, back], (j, n.row)).start()


def reduce_late(n, z):
    at = slice(2 * z.HW, 3 * z.HW)
    for k in range(1, z.C // 2):
        j = (n.clip + 2 * k) % z.C
        back = z.C // 2 - k - 1
        remote(n.Wp.at[j, :, at], n.Rp.at[back, :, at], n.Rv_s.at[0, k], n.Rv_s.at[1, back], (j, n.row)).start()


def reduce_three(n, z, part, rx, more, put, late, relayed):
    total = part[n.clip].astype(f32)
    for k in range(1, z.C // 2):
        j = (n.clip + 2 * k) % z.C
        at = slice(0, 2 * z.HW) if late else slice(0, part.shape[2])
        copy = remote(part.at[j, :, at], rx.at[k - 1, :, at], more.at[0, k], more.at[1, k - 1], (j, n.row))
        skip = skipped(n, z, j, relayed)
        unless(skip, copy.wait)
        if skip is not None:
            pl.when(skip)(remote(part.at[j], n.Xg, n.Xg_s.at[0], n.Xg_s.at[1], (n.relay_to, n.row)).wait_send)
        if late:
            at = slice(2 * z.HW, 3 * z.HW)
            remote(part.at[j, :, at], rx.at[k - 1, :, at], n.Rv_s.at[0, k], n.Rv_s.at[1, k - 1], (j, n.row)).wait()
        total = total + rx[k - 1].astype(f32)
    put(total)
    n.squares[...] += fold(total)


def fold(x):
    x = x * x
    total = x[:, :128]
    for i in range(1, x.shape[1] // 128):
        total = total + x[:, i * 128 : (i + 1) * 128]
    return jnp.sum(total.reshape(x.shape[0] // 8, 8, 128), 0)


def phase_pull_two(n, z):
    for name in ("stream", "branch", "gmid"):
        fetch(n, name).wait()

    def chunk(s, _):
        c = z.N - 1 - s
        scatter_row_wait(n, n.sb, n.rsr, n.gt_s, c)

        def frame(i, _):
            f = c * z.CF + i
            rows = frame_rows(z, c, i)
            branch = n.branch[rows, :]
            hat, rstd = normed(n.stream[rows, :] + vec(n, 2, f) * branch)
            dx, d_shift, d_scale = norm_pull(hat, rstd, vec(n, 4, f), summed(n, z, c, i))
            n.gadp[3, pl.ds(f, 1), :] = d_shift
            n.gadp[4, pl.ds(f, 1), :] = d_scale
            mid = n.gmid[rows, :] + dx
            n.gmid[rows, :] = mid
            n.gadp[2, pl.ds(f, 1), :] = jnp.sum(mid * branch, 0, keepdims=True)
            n.gb[c, n.row, pl.ds(pl.multiple_of(i * z.LT, z.LT), z.LT), :] = (mid * vec(n, 2, f)).astype(bf16)
            return 0

        lax.fori_loop(0, z.CF, frame, 0)
        gather_row(n, n.gb, n.gb_s, c)
        pl.when(s == 0)(lambda: reduce_middle(n, z, "d"))
        after(z, s, lambda d: gather_more(n, n.gb, n.gb_s, z.N - 1 - d))
        return 0

    lax.fori_loop(0, z.N, chunk, 0)


def phase_pull_attend(n, z):
    for name in ("Wo", "q", "k", "v", "att", "lse"):
        fetch(n, name).wait()
    n.dkv[...] = jnp.zeros_like(n.dkv)
    queries = 384 if z.W % 384 == 0 else z.W
    parts = z.W // queries

    def chunk(s, _):
        c = z.N - 1 - s
        if z.N == 1:
            gather_more(n, n.gb, n.gb_s, c)
        gather_row_wait(n, n.gb, n.gb_s, c)
        do = dot_nn(flat(n.gb[c]), flat(n.Wo[...])).astype(bf16)
        for h in range(z.HD):
            mine = do[:, h * HSIZE : (h + 1) * HSIZE]
            n.do[h] = mine
            delta = jnp.sum(mine.astype(f32) * n.att[c, :, h * HSIZE : (h + 1) * HSIZE], -1, keepdims=True)
            n.delta[h] = jnp.transpose(jnp.broadcast_to(delta, (z.W, 128)))[:8]
        pl.when(s == 0)(lambda: reduce_middle(n, z, "g"))

        def head(step, _):
            h, u = step // parts, step % parts
            at = pl.ds(pl.multiple_of(u * queries, queries), queries)
            q, do = n.q[h, c, at, :], n.do[h, at, :]
            lse, delta = n.lse[h, c, :, at][:1], n.delta[h, :, at][:1]

            def block(j, masked):
                k, v = n.k[h, j], n.v[h, j]
                p = jnp.exp(dot_nt(k, q) - lse)
                if masked:
                    a = lax.broadcasted_iota(jnp.int32, p.shape, 0)
                    b = lax.broadcasted_iota(jnp.int32, p.shape, 1) + u * queries
                    p = jnp.where((a % z.CT) // z.LT <= (b % z.CT) // z.LT, p, 0.0)
                dv = dot_nn(p.astype(bf16), do)
                ds = (p * (dot_nt(v, do) - delta)).astype(bf16)
                n.dkv[h, j] += jnp.concatenate([dot_nn(ds, q), dv], -1)
                return dot_tn(ds, k)

            dq = block(c, True)
            n.dq[h, at, :] = lax.fori_loop(0, c, lambda j, dq: dq + block(j, False), dq)
            return 0

        lax.fori_loop(0, z.HD * parts, head, 0)
        last(z, s, lambda d: gather_more(n, n.gb, n.gb_s, z.N - 1 - d))
        pl.when(s == z.N // 2)(lambda: early_row(n, z))
        pl.when(s == z.N // 2)(lambda: reduce_relay(n, z))
        pl.when(s == z.N - 1)(lambda: early_clip(n, z))
        per = 128 // HSIZE
        cos, sin = tables(n, c)
        for g in range(z.HW // 128):
            y = jnp.concatenate([n.dq[g * per + s] for s in range(per)], -1)
            y = turn(y, cos, -sin) * HSIZE**-0.5
            n.gp[c, :, g * 128 : (g + 1) * 128] = y.astype(bf16)
        pl.when(s == 0)(fetch(n, "Wp").wait)
        project_chunk(n, z, c)
        after(z, s, lambda d: scatter_more(n, n.sb, n.rsr, n.go_s, z.N - 1 - d))
        return 0

    lax.fori_loop(0, z.N, chunk, 0)


def project_chunk(n, z, c):
    per = 128 // HSIZE
    tile = 256
    slabs = tile // z.DR
    cos, sin = tables(n, c)
    for g in range(z.HW // 128):
        at = z.HW + g * 128
        y = jnp.concatenate([n.dkv[g * per + h, c][:, :HSIZE] for h in range(per)], -1)
        n.gp[c, :, at : at + 128] = turn(y, cos, -sin).astype(bf16)
        at = 2 * z.HW + g * 128
        y = jnp.concatenate([n.dkv[g * per + h, c][:, HSIZE:] for h in range(per)], -1)
        n.gp[c, :, at : at + 128] = y.astype(bf16)

    def output(t, _):
        y = dot_nt(n.gp[c], flat(n.Wp[pl.ds(t * slabs, slabs)]))
        at = pl.ds(pl.multiple_of(t * tile, tile), tile)
        n.sb[c, :, :, at] = y.astype(bf16).reshape(z.R, z.CT, tile)
        return 0

    lax.fori_loop(0, D // tile, output, 0)
    scatter_row(n, n.sb, n.rsr, n.go_s, c)


def phase_pull_one(n, z):
    def chunk(s, _):
        c = z.N - 1 - s
        scatter_row_wait(n, n.sb, n.rsr, n.go_s, c)

        def frame(i, _):
            f = c * z.CF + i
            rows = frame_rows(z, c, i)
            hat, rstd = normed(n.stream[rows, :])
            dx, d_shift, d_scale = norm_pull(hat, rstd, vec(n, 1, f), summed(n, z, c, i))
            n.gadp[0, pl.ds(f, 1), :] = d_shift
            n.gadp[1, pl.ds(f, 1), :] = d_scale
            n.gb[c, n.row, pl.ds(pl.multiple_of(i * z.LT, z.LT), z.LT), :] = (n.gmid[rows, :] + dx).astype(bf16)
            return 0

        lax.fori_loop(0, z.CF, frame, 0)
        return 0

    lax.fori_loop(0, z.N, chunk, 0)


def row_total(n, src, dst, cut):
    total = src[n.row, cut].astype(f32)
    for p in n.row_peer:
        total = total + dst[p, cut].astype(f32)
    return total


def swap_row_cut(n, src, dst, sems, cut):
    for k, p in enumerate(n.row_peer):
        remote(src.at[p, cut], dst.at[n.row, cut], sems.at[0, k], sems.at[1, n.row], (n.clip, p)).start()


def swap_row_cut_wait(n, src, dst, sems, cut):
    for k, p in enumerate(n.row_peer):
        remote(src.at[p, cut], dst.at[p, cut], sems.at[0, k], sems.at[1, p], (n.clip, p)).wait()


def is_late(z, clip):
    return clip < z.C // 4


def swap_owner(n, z, late):
    for k, p in enumerate(n.clip_peer):
        copy = remote(n.ca.at[p], n.da.at[n.clip], n.ca_s.at[0, k], n.ca_s.at[1, n.clip], (p, n.row))
        pl.when(is_late(z, p) == late)(copy.start)


def swap_owner_wait(n, z):
    for k, p in enumerate(n.clip_peer):
        remote(n.ca.at[p], n.da.at[p], n.ca_s.at[0, k], n.ca_s.at[1, p], (p, n.row)).wait_recv()


def swap_owner_sent(n, z):
    for k, p in enumerate(n.clip_peer):
        remote(n.ca.at[p], n.da.at[p], n.ca_s.at[0, k], n.ca_s.at[1, p], (p, n.row)).wait_send()


def owner_share(n, z):
    swap_owner_wait(n, z)
    n.da[n.clip] = n.ca[n.clip]
    n.ea2[n.row] = flat(n.da[...])
    share_row(n, n.ea2, n.ea2_s)


def owner_grads(n, z):
    share_row_wait(n, n.ea2, n.ea2_s)
    low = jnp.concatenate([n.ea2[r] for r in range(z.R)], -1)
    n.gc[...] = dot_nt(low, n.w_adapt[...].astype(bf16)).reshape(z.C, PAD, z.LW)
    swap_clip(n, n.gc, n.gd, n.gc_s)
    gadapt = dot_tn(n.cond[...], low)
    n.gadapt[...] = gadapt
    n.squares[...] += fold(gadapt)


def take_columns(n, z, owners):
    for r in range(z.R):
        for i in owners:
            col = i * z.AW + r * z.aw
            n.xa[r, i] = n.gadp[col // D, :, col % D : col % D + z.aw]


def early_row(n, z):
    hr = z.DR // z.R
    take_columns(n, z, range(z.C // 4, z.C))
    for r in range(z.R):
        for i in range(z.C):
            at = i * z.DR + r * hr
            n.xh[r, i] = n.ghead[at : at + hr, :].astype(n.xh.dtype)
    swap_row_cut(n, n.xa, n.ya, n.xa_s, pl.ds(z.C // 4, z.C - z.C // 4))
    swap_row(n, n.xh, n.yh, n.xh_s)


def early_clip(n, z):
    cut = pl.ds(z.C // 4, z.C - z.C // 4)
    swap_row_cut_wait(n, n.xa, n.ya, n.xa_s, cut)
    swap_row_wait(n, n.xh, n.yh, n.xh_s)
    n.ca[cut] = row_total(n, n.xa, n.ya, cut).astype(bf16)
    n.ch[...] = row_total(n, n.xh, n.yh, slice(None)).astype(n.ch.dtype)
    swap_owner(n, z, False)
    swap_clip(n, n.ch, n.dh, n.ch_s)
    n.dh[n.clip] = n.ch[n.clip]


def phase_small(n, z):
    pr, hr = z.PF // z.C, z.DR // z.R
    pw = D // z.R
    late = is_late(z, n.clip)
    early = jnp.logical_not(late)
    cut = pl.ds(0, z.C // 4)
    take_columns(n, z, range(z.C // 4))
    swap_row_cut(n, n.xa, n.ya, n.xb_s, cut)
    gpatch = dot_tn(n.inputs[...], jnp.concatenate([n.gb[c, n.row] for c in range(z.N)], 0))
    for r in range(z.R):
        n.xp[r] = gpatch[:, r * pw : (r + 1) * pw].astype(bf16)
    swap_row(n, n.xp, n.yp, n.xp_s)
    pl.when(early)(lambda: owner_share(n, z))
    swap_clip_wait(n, n.ch, n.dh, n.ch_s)
    sh = n.dh[0].astype(f32)
    for i in range(1, z.C):
        sh = sh + n.dh[i].astype(f32)
    n.eh[n.row] = sh
    share_row(n, n.eh, n.eh_s)
    swap_row_cut_wait(n, n.xa, n.ya, n.xb_s, cut)
    n.ca[cut] = row_total(n, n.xa, n.ya, cut).astype(bf16)
    swap_owner(n, z, True)
    swap_row_wait(n, n.xp, n.yp, n.xp_s)
    n.cp[...] = row_total(n, n.xp, n.yp, slice(None)).reshape(z.C, pr, pw).astype(n.cp.dtype)
    swap_clip(n, n.cp, n.dp, n.cp_s)
    n.dp[n.clip] = n.cp[n.clip]
    pl.when(early)(lambda: owner_grads(n, z))
    reduce_late(n, z)
    pl.when(late)(lambda: owner_share(n, z))
    reduce_end(n, z, "d")
    pl.when(late)(lambda: owner_grads(n, z))
    swap_owner_sent(n, z)
    swap_clip_wait(n, n.cp, n.dp, n.cp_s)
    sp = n.dp[0].astype(f32)
    for i in range(1, z.C):
        sp = sp + n.dp[i].astype(f32)
    n.ep[n.row] = sp
    share_row(n, n.ep, n.ep_s)
    n.squares[...] += fold(sp) + fold(sh)
    reduce_end(n, z, "g")
    swap_clip_wait(n, n.gc, n.gd, n.gc_s)
    total = n.gc[n.clip]
    for p in n.clip_peer:
        total = total + n.gd[p]
    pre = n.pre[pl.ds(pl.multiple_of(n.clip * PAD, PAD), PAD), :]
    sig = 1.0 / (1.0 + jnp.exp(-pre))
    n.gl[n.clip] = (total * (sig * (1.0 + pre * (1.0 - sig)))).astype(bf16)
    share_clip(n, n.gl, n.gl_s)
    reduce_end(n, z, "o")
    reduce_end(n, z, "p")
    share_row_wait(n, n.eh, n.eh_s)
    share_row_wait(n, n.ep, n.ep_s)
    for r in range(z.R):
        n.gpatch[:, r * pw : (r + 1) * pw] = n.ep[r]
        n.gheads[r * hr : (r + 1) * hr, :] = n.eh[r]
    share_clip_wait(n, n.gl, n.gl_s)
    n.glv[...] = dot_tn(flat(n.ea[...]), flat(n.gl[...]))
    glevel = n.glv[pl.ds(pl.multiple_of(n.clip * z.LR, z.LR), z.LR), :]
    n.glevel[...] = glevel
    n.squares[...] += fold(glevel)


def phase_stats(n, z):
    lines = [jnp.sum(ref[...], 0, keepdims=True) for ref in (n.squares, n.loss, n.weight)]
    n.sa[n.row] = jnp.concatenate(lines + [jnp.zeros((5, 128), f32)], 0)
    share_row(n, n.sa, n.sa_s)
    share_row_wait(n, n.sa, n.sa_s)
    total = n.sa[0]
    for r in range(1, z.R):
        total = total + n.sa[r]
    n.sc[n.clip] = total
    share_clip(n, n.sc, n.sc_s)
    share_clip_wait(n, n.sc, n.sc_s)
    total = n.sc[0]
    for i in range(1, z.C):
        total = total + n.sc[i]
    n.stats[...] = total


LOADED = ("Wd", "gu", "gf", "Wg", "stream", "branch", "gmid", "act", "two", "Wo", "q", "k", "v", "att", "lse", "Wp", "one")


def reduce_start(n, z, x):
    reduce_one(n, z, getattr(n, "W" + x), getattr(n, "S" + x), getattr(n, "S" + x + "_s"))


def reduce_middle(n, z, x):
    part, rx = getattr(n, "W" + x), getattr(n, "R" + x)
    width = 2 * z.HW if x == "p" else part.shape[2]
    reduce_two(n, z, part, getattr(n, "S" + x), getattr(n, "S" + x + "_s"), rx, getattr(n, "R" + x + "_s"), width, x == "g" and n.line)


def reduce_end(n, z, x):
    def put(total):
        if x == "p":
            for k in range(3):
                n.Gp[k] = total[:, k * z.HW : (k + 1) * z.HW]
        elif x == "g":
            tiles = z.FH // 128
            for t in range(tiles):
                for k in range(2):
                    at = k * z.FH + t * 128
                    n.Gg[pl.ds(2 * t + k, z.DR, stride=2 * tiles), :] = total[:, at : at + 128]
        else:
            getattr(n, "G" + x)[...] = jnp.transpose(total)

    reduce_three(n, z, getattr(n, "W" + x), getattr(n, "R" + x), getattr(n, "R" + x + "_s"), put, x == "p", x == "g")


def backward_body(n, z):
    for name in LOADED:
        if name not in ("one", "two"):
            fetch(n, name).start()
    n.squares[...] = jnp.zeros_like(n.squares)
    n.gadp[...] = n.gad[...]
    if n.line:
        for k, p in enumerate(n.core_peer):

            @pl.when(skipped(n, z, p, True))
            def _():
                n.Rg[k] = jnp.zeros_like(n.Rg[k])

    enter(n, z)
    phase_pull_feed(n, z)
    fetch(n, "act").wait()
    weight_grad(n, z, n.gf, n.act, n.Wd)
    load_two = pltpu.make_async_copy(n.two_i, n.gf, n.in_s.at[LOADED.index("two")])
    load_two.start()
    reduce_start(n, z, "d")
    scatter_more(n, n.sb, n.rsr, n.gt_s, 0)
    phase_pull_two(n, z)
    load_two.wait()
    weight_grad(n, z, n.gf, n.gu, n.Wg)
    load_one = pltpu.make_async_copy(n.one_i, n.gf, n.in_s.at[LOADED.index("one")])
    load_one.start()
    reduce_start(n, z, "g")
    phase_pull_attend(n, z)
    load_one.wait()
    weight_grad(n, z, n.gf, n.gp, n.Wp)
    scatter_more(n, n.sb, n.rsr, n.go_s, 0)
    reduce_start(n, z, "p")
    weight_grad(n, z, n.gb, n.att, n.Wo)
    reduce_start(n, z, "o")
    reduce_middle(n, z, "p")
    reduce_middle(n, z, "o")
    phase_pull_one(n, z)
    phase_small(n, z)
    phase_stats(n, z)


def backward_call(z, kept, ins):
    sh = shapes_of(z)
    pr, hr, pw = z.PF // z.C, z.DR // z.R, D // z.R
    head_type = f32 if hr % 16 else bf16
    patch_type = f32 if pr % 16 else bf16
    widths = {"p": 3 * z.HW, "o": z.HW, "g": 2 * z.FH, "d": z.FH}
    outs = {
        "Gp": ((3, z.DR, z.HW), f32),
        "Go": ((z.HW, z.DR), f32),
        "Gg": ((z.DR * 2 * z.FH // 128, 128), f32),
        "Gd": ((z.FH, z.DR), f32),
    }
    outs.update(
        gpatch=((pr, D), f32),
        gheads=((z.DR, z.PF), f32),
        gadapt=((z.LW, z.AW), f32),
        glevel=((z.LR, z.LW), f32),
        stats=((8, 128), f32),
    )
    anys = {k + "_i": kept[k] for k in LOADED}
    scratch = vm(sh, [k for k in LOADED if k not in ("one", "two")] + ["gb", "sb", "rsr"])
    for x, w in widths.items():
        scratch["S" + x] = pltpu.VMEM((z.C // 2, z.DR, w), bf16)
        scratch["R" + x] = pltpu.VMEM((z.C // 2 - 1, z.DR, w), bf16)
    extra = {
        "tb": ((D // max(2, z.W // 192), z.N * z.W), bf16),
        "do": ((z.HD, z.W, HSIZE), bf16),
        "delta": ((z.HD, 8, z.W), f32),
        "dq": ((z.HD, z.W, HSIZE), f32),
        "dkv": ((z.HD, z.N, z.W, 2 * HSIZE), f32),
        "gp": ((z.N, z.W, 3 * z.HW), bf16),
        "gadp": ((VECTORS, PAD, D), f32),
        "squares": ((8, 128), f32),
        "xa": ((z.R, z.C, PAD, z.aw), f32),
        "ya": ((z.R, z.C, PAD, z.aw), f32),
        "xp": ((z.R, z.PF, pw), bf16),
        "yp": ((z.R, z.PF, pw), bf16),
        "xh": ((z.R, z.C, hr, z.PF), head_type),
        "yh": ((z.R, z.C, hr, z.PF), head_type),
        "ca": ((z.C, PAD, z.aw), bf16),
        "da": ((z.C, PAD, z.aw), bf16),
        "cp": ((z.C, pr, pw), patch_type),
        "dp": ((z.C, pr, pw), patch_type),
        "ch": ((z.C, hr, z.PF), head_type),
        "dh": ((z.C, hr, z.PF), head_type),
        "ea2": ((z.R, z.C * PAD, z.aw), bf16),
        "ep": ((z.R, pr, pw), f32),
        "eh": ((z.R, hr, z.PF), f32),
        "gc": ((z.C, PAD, z.LW), f32),
        "gd": ((z.C, PAD, z.LW), f32),
        "gl": ((z.C, PAD, z.LW), bf16),
        "glv": ((TF, z.LW), f32),
        "sa": ((z.R, 8, 128), f32),
        "sc": ((z.C, 8, 128), f32),
    }
    scratch.update(vm(extra, extra))
    dma = pltpu.SemaphoreType.DMA
    if z.C == 8:
        scratch["Xg"] = pltpu.VMEM((z.DR, 2 * z.FH), bf16)
        scratch["Xg_s"] = dma((2,))
    scratch["Rv_s"] = dma((2, z.C // 2))
    scratch["in_s"] = dma((len(LOADED),))
    for x in widths:
        scratch["S" + x + "_s"] = dma((2, z.C // 2))
        scratch["R" + x + "_s"] = dma((2, z.C // 2))
    for k in ("gt_s", "gb_s", "go_s"):
        scratch[k] = dma((2, z.N, max(6, z.R)))
    for k in ("xa_s", "xb_s", "xp_s", "xh_s", "ea2_s", "ep_s", "eh_s", "sa_s"):
        scratch[k] = dma((2, z.R))
    for k in ("ca_s", "cp_s", "ch_s", "gc_s", "gl_s", "sc_s"):
        scratch[k] = dma((2, z.C))
    return run(backward_body, z, 1, ins, anys, outs, scratch, (), 64 << 20)


WEIGHTS = ("patch", "level", "adapt", "project", "output", "gateup", "down", "head")


def packed(x):
    rows, pair, width = x.shape
    return jnp.transpose(x.reshape(rows, pair, width // 128, 128), (0, 2, 1, 3)).reshape(-1, 128)


def unpacked(x, shape):
    rows, pair, width = shape
    return jnp.transpose(x.reshape(rows, width // 128, pair, 128), (0, 2, 1, 3)).reshape(shape)


def to_kernel(values):
    values = list(values)
    values[3] = jnp.transpose(values[3], (1, 0, 2))
    values[5] = packed(values[5])
    return values


def from_kernel(values, gateup_shape):
    values = list(values)
    values[3] = jnp.transpose(values[3], (1, 0, 2))
    values[5] = unpacked(values[5], gateup_shape)
    return values


def adam_kernel(pf, stats, *refs):
    grads, masters, firsts, seconds = (refs[8 * i : 8 * i + 8] for i in range(4))
    scalars = refs[32:35]
    news, means, squares = (refs[35 + 8 * i : 43 + 8 * i] for i in range(3))
    weight_sum = jnp.sum(stats[2:3])
    grad_norm = jnp.sqrt(jnp.full((8, 128), jnp.sum(stats[0:1]))) / weight_sum
    factor = jnp.minimum(1.0, clip_level / (grad_norm + 1e-06)) / weight_sum
    scalars[0][0, 0] = jnp.sum(stats[1:2]) / pf
    scalars[1][0, 0] = weight_sum
    scalars[2][0, 0] = jnp.max(grad_norm)
    factor = factor[:1, :1]
    for g, m, f, s, new, mean, square in zip(grads, masters, firsts, seconds, news, means, squares):
        grad = g[...] * factor
        first_new = beta_one * f[...] + (1.0 - beta_one) * grad
        second_new = beta_two * s[...] + (1.0 - beta_two) * grad * grad
        first_hat = first_new * (1.0 / (1.0 - beta_one**STEP))
        second_hat = second_new * (1.0 / (1.0 - beta_two**STEP))
        master = m[...]
        new[...] = master - learn_rate * (first_hat / (jnp.sqrt(second_hat) + adam_eps) + decay_rate * master)
        mean[...] = first_new
        square[...] = second_new


def adam_call(z, stats, grads, masters, firsts, seconds):
    steps = 4
    split = (None, None, 0, 1, 0, 0, 0, 0)

    def spec(x, axis):
        if axis is None:
            return pl.BlockSpec(x.shape, lambda i: (0,) * x.ndim)
        block = tuple(d // steps if k == axis else d for k, d in enumerate(x.shape))
        return pl.BlockSpec(block, lambda i: tuple(i if k == axis else 0 for k in range(x.ndim)))

    specs = [spec(x, axis) for x, axis in zip(masters, split)]
    shapes = [jax.ShapeDtypeStruct(x.shape, f32) for x in masters]
    scalar = jax.ShapeDtypeStruct((1, 1), f32)
    result = pl.pallas_call(
        functools.partial(adam_kernel, z.PF),
        grid=(steps,),
        out_shape=[scalar] * 3 + shapes * 3,
        in_specs=[pl.BlockSpec(stats.shape, lambda i: (0, 0))] + specs * 4,
        out_specs=[pl.BlockSpec((1, 1), lambda i: (0, 0), memory_space=pltpu.SMEM)] * 3 + specs * 3,
        compiler_params=pltpu.CompilerParams(vmem_limit_bytes=64 << 20),
    )(stats, *grads, *masters, *firsts, *seconds)
    return result[:3], result[3:11], result[11:19], result[19:27]


def on_device(latents, noise, levels, *weights):
    masters, firsts, seconds = weights[:8], weights[8:16], weights[16:]
    a = dict(zip(["w_" + k for k in WEIGHTS], masters))
    a.update(latents=latents, noise=noise, levels=levels)
    z = sizes_of(latents, lax.axis_size("clip"), lax.axis_size("row"))
    ins, frame_weight = forward_inputs(z, a)
    kept = forward_call(z, ins)
    weight = jnp.sum(frame_weight) * z.LT
    back = {k: kept[k] for k in ("gad", "ghead", "loss", "pre", "cond", "ea", "mod")}
    back.update({k: ins[k] for k in ("w_adapt", "inputs", "tab")})
    back["weight"] = jnp.zeros((8, 128), f32).at[0, 0].set(weight)
    g = backward_call(z, kept, back)
    grads = (g["gpatch"], g["glevel"], g["gadapt"], g["Gp"], g["Go"], g["Gg"], g["Gd"], g["gheads"])
    scalars, *results = adam_call(z, g["stats"], grads, *(to_kernel(x) for x in (masters, firsts, seconds)))
    results = [from_kernel(x, masters[5].shape) for x in results]
    return tuple(x.reshape(()) for x in scalars) + tuple(x for result in results for x in result)


def solution(mesh):
    tokens = P("clip", None, "row", None, None)
    by_clip = P("clip", None)
    weights = (by_clip, P("clip", "row"), P("row", "clip"), P("clip", None, "row"), P("row", "clip"))
    weights = weights + (P("clip", None, "row"), P("row", "clip"), by_clip)
    return jax.shard_map(
        on_device,
        mesh=mesh,
        in_specs=(tokens, tokens, by_clip) + weights * 3,
        out_specs=(P(), P(), P()) + weights * 3,
        check_vma=False,
    )
```

```python
import functools
import math
import types

import jax
import jax.numpy as jnp
import numpy as np
from jax import lax
from jax.experimental import pallas as pl
from jax.experimental.pallas import tpu as pltpu
from jax.sharding import PartitionSpec as P

D = 1024
HEADS = 16
HSIZE = 64
TF = 256
LEVELS = 1000
STEP = 3
VECTORS = 8
PAD = 16

norm_eps = 1e-06
clip_level = 0.002
learn_rate = 0.03
beta_one = 0.9
beta_two = 0.95
decay_rate = 0.1
adam_eps = 1e-08

MESH = pl.DeviceIdType.MESH
f32 = jnp.float32
bf16 = jnp.bfloat16


def dot_nn(left, right):
    return jnp.dot(left, right, preferred_element_type=f32)


def dot_nt(left, right):
    return lax.dot_general(left, right, (((1,), (1,)), ((), ())), preferred_element_type=f32)


def dot_tn(left, right):
    return lax.dot_general(left, right, (((0,), (0,)), ((), ())), preferred_element_type=f32)


def frequencies(number):
    return jnp.exp(-math.log(10000.0) * jnp.arange(number, dtype=f32) / number)


def noise_plan(levels):
    ratio = levels.astype(f32) / LEVELS
    alpha_bar = jnp.cos((ratio + 0.008) / 1.008 * (math.pi / 2)) ** 2
    weight = jnp.minimum(1.0, 5.0 * (1.0 - alpha_bar) / alpha_bar)
    return (alpha_bar, weight)


def level_embedding(levels, half):
    angle = levels.astype(f32)[..., None] * frequencies(half)
    return jnp.concatenate([jnp.cos(angle), jnp.sin(angle)], -1)


def sizes_of(latents, clips, parts):
    z = types.SimpleNamespace()
    z.C, z.R = clips, parts
    z.F = latents.shape[1]
    z.rows, z.cols, z.PF = latents.shape[2], latents.shape[3], latents.shape[4]
    z.LT = z.rows * z.cols
    z.N = 3 if z.F % 3 == 0 else 1
    z.CF = z.F // z.N
    z.CT = z.CF * z.LT
    z.W = z.R * z.CT
    z.T = z.F * z.LT
    z.HD = HEADS // parts
    z.HW = z.HD * HSIZE
    z.FH = 4 * D // parts
    z.DR = D // clips
    z.LR = TF // clips
    z.LW = D // parts
    z.AW = VECTORS * D // clips
    z.aw = z.AW // parts
    return z


def rotary_consts(z):
    half = HSIZE // 2
    fp = half // 4
    rp = 3 * half // 8
    cp = half - fp - rp

    def freq(n):
        return np.exp(-math.log(10000.0) * np.arange(n, dtype=np.float32) / np.float32(n)).astype(np.float32)

    shape = (z.N, z.R, z.CF, z.rows, z.cols)
    frame = (np.arange(z.N)[:, None] * z.CF + np.arange(z.CF)[None, :]).astype(np.float32)
    frame = np.broadcast_to(frame[:, None, :, None, None], shape)
    prow = (np.arange(z.R)[:, None] * z.rows + np.arange(z.rows)[None, :]).astype(np.float32)
    prow = np.broadcast_to(prow[None, :, None, :, None], shape)
    pcol = np.broadcast_to(np.arange(z.cols, dtype=np.float32), shape)
    angle = np.concatenate(
        [frame[..., None] * freq(fp), prow[..., None] * freq(rp), pcol[..., None] * freq(cp)], -1
    ).astype(np.float32)
    angle = angle.reshape(z.N, z.W, half)
    cos, sin = np.cos(angle), np.sin(angle)
    return np.concatenate([cos, cos, sin, sin], -1).astype(np.float32)


def remote(src, dst, send_sem, recv_sem, device):
    return pltpu.make_async_remote_copy(
        src_ref=src, dst_ref=dst, send_sem=send_sem, recv_sem=recv_sem, device_id=device, device_id_type=MESH
    )


def place(n, z):
    n.clip = lax.axis_index("clip")
    n.row = lax.axis_index("row")
    n.sib = n.clip + 1 - 2 * (n.clip % 2)
    n.row_peer = [(n.row + k) % z.R for k in range(1, z.R)]
    n.clip_peer = [(n.clip + k) % z.C for k in range(1, z.C)]
    n.square = z.R == 4
    n.far = (n.row + 1 - 2 * (n.row % 2) + 2) % z.R
    n.x = (n.clip, n.row + 1 - 2 * (n.row % 2))
    n.y = (n.clip, (n.row + 2) % z.R)
    n.arrivals = 2 if n.square else z.R - 1
    n.line = z.C == 8
    place = n.clip // 2
    n.inner = jnp.logical_or(place == 1, place == 2)
    n.far_end = jnp.where(n.inner, n.clip + 4 - 8 * (place // 2), n.clip)
    n.near_end = jnp.where(n.inner, n.clip - 2 + 4 * (place // 2), n.clip)
    n.relay_to = jnp.where(place == 0, n.clip + 2, (n.clip - 2 + z.C) % z.C)
    n.core_peer = [(n.clip + 2 * k) % z.C for k in range(1, z.C // 2)]


def enter(n, z):
    barrier = pltpu.get_barrier_semaphore()
    for p in n.row_peer:
        pl.semaphore_signal(barrier, inc=1, device_id=(n.clip, p), device_id_type=MESH)
    for p in n.clip_peer:
        pl.semaphore_signal(barrier, inc=1, device_id=(p, n.row), device_id_type=MESH)
    pl.semaphore_wait(barrier, z.R + z.C - 2)


def send(src, dst, sems, slot, land, device):
    remote(src, dst, sems.at[(0,) + slot], sems.at[(1,) + land], device).start()


def sent(ref, sems, slot, device):
    remote(ref, ref, sems.at[(0,) + slot], sems.at[(1,) + slot], device).wait_send()


def got(ref, sems, slot, device):
    remote(ref, ref, sems.at[(0,) + slot], sems.at[(1,) + slot], device).wait_recv()


def halves(n, ref, c, p):
    rows = ref.shape[2] // 2
    return ref.at[c, p, :rows], ref.at[c, p, rows:]


def gather_row(n, full, sems, c):
    mine = full.at[c, n.row]
    if n.square:
        send(mine, mine, sems, (c, 0), (c, 0), n.x)
        send(mine, mine, sems, (c, 1), (c, 1), n.y)
        return
    for k, p in enumerate(n.row_peer):
        back = len(n.row_peer) - 1 - k
        send(mine, mine, sems, (c, k), (c, back), (n.clip, p))


def gather_more(n, full, sems, c):
    if n.square:
        got(full.at[c, n.x[1]], sems, (c, 0), n.x)
        block = halves(n, full, c, n.x[1])[0]
        send(block, block, sems, (c, 2), (c, 2), n.y)
        got(full.at[c, n.y[1]], sems, (c, 1), n.y)
        block = halves(n, full, c, n.y[1])[1]
        send(block, block, sems, (c, 3), (c, 3), n.x)


def gather_row_wait(n, full, sems, c):
    if n.square:
        low, high = halves(n, full, c, n.far)
        got(low, sems, (c, 2), n.y)
        got(high, sems, (c, 3), n.x)
        mine = full.at[c, n.row]
        sent(mine, sems, (c, 0), n.x)
        sent(mine, sems, (c, 1), n.y)
        sent(low, sems, (c, 2), n.y)
        sent(high, sems, (c, 3), n.x)
        return
    for k, p in enumerate(n.row_peer):
        block = full.at[c, p]
        got(block, sems, (c, k), (n.clip, p))
        sent(block, sems, (c, k), (n.clip, p))


def scatter_row(n, parts, landed, sems, c):
    if n.square:
        (xl, _), (_, yh), (fl, fh) = (halves(n, parts, c, p) for p in (n.x[1], n.y[1], n.far))
        send(fl, halves(n, landed, c, 2)[0], sems, (c, 0), (c, 0), n.x)
        send(fh, halves(n, landed, c, 2)[1], sems, (c, 1), (c, 1), n.y)
        send(xl, halves(n, landed, c, 0)[0], sems, (c, 2), (c, 2), n.x)
        send(yh, halves(n, landed, c, 1)[1], sems, (c, 3), (c, 3), n.y)
        return
    for k, p in enumerate(n.row_peer):
        back = len(n.row_peer) - 1 - k
        send(parts.at[c, p], landed.at[c, back], sems, (c, k), (c, back), (n.clip, p))


def scatter_more(n, parts, landed, sems, c):
    if n.square:
        rows = parts.shape[2] // 2
        low, high = halves(n, landed, c, 2)
        got(low, sems, (c, 0), n.x)
        parts[c, n.y[1], :rows] = (parts[c, n.y[1], :rows].astype(f32) + low[...].astype(f32)).astype(bf16)
        send(halves(n, parts, c, n.y[1])[0], halves(n, landed, c, 1)[0], sems, (c, 5), (c, 5), n.y)
        got(high, sems, (c, 1), n.y)
        parts[c, n.x[1], rows:] = (parts[c, n.x[1], rows:].astype(f32) + high[...].astype(f32)).astype(bf16)
        send(halves(n, parts, c, n.x[1])[1], halves(n, landed, c, 0)[1], sems, (c, 4), (c, 4), n.x)


def scatter_row_wait(n, parts, landed, sems, c):
    if n.square:
        (xl, xh), (yl, yh) = (halves(n, landed, c, k) for k in range(2))
        for slot, ref, peer in ((2, xl, n.x), (3, yh, n.y), (4, xh, n.x), (5, yl, n.y)):
            got(ref, sems, (c, slot), peer)
        for slot in range(6):
            sent(xl, sems, (c, slot), n.x)
        return
    for k, p in enumerate(n.row_peer):
        got(landed.at[c, k], sems, (c, k), (n.clip, p))
        sent(landed.at[c, k], sems, (c, k), (n.clip, p))


def share_row(n, buf, sems):
    for k, p in enumerate(n.row_peer):
        mine = buf.at[n.row]
        remote(mine, mine, sems.at[0, k], sems.at[1, n.row], (n.clip, p)).start()


def share_row_wait(n, buf, sems):
    for k, p in enumerate(n.row_peer):
        block = buf.at[p]
        remote(block, block, sems.at[0, k], sems.at[1, p], (n.clip, p)).wait()


def swap_row(n, src, dst, sems):
    for k, p in enumerate(n.row_peer):
        remote(src.at[p], dst.at[n.row], sems.at[0, k], sems.at[1, n.row], (n.clip, p)).start()


def swap_row_wait(n, src, dst, sems):
    for k, p in enumerate(n.row_peer):
        remote(src.at[p], dst.at[p], sems.at[0, k], sems.at[1, p], (n.clip, p)).wait()


def share_clip(n, buf, sems):
    for k, p in enumerate(n.clip_peer):
        mine = buf.at[n.clip]
        remote(mine, mine, sems.at[0, k], sems.at[1, n.clip], (p, n.row)).start()


def share_clip_wait(n, buf, sems):
    for k, p in enumerate(n.clip_peer):
        block = buf.at[p]
        remote(block, block, sems.at[0, k], sems.at[1, p], (p, n.row)).wait()


def swap_clip(n, src, dst, sems):
    for k, p in enumerate(n.clip_peer):
        remote(src.at[p], dst.at[n.clip], sems.at[0, k], sems.at[1, n.clip], (p, n.row)).start()


def swap_clip_wait(n, src, dst, sems):
    for k, p in enumerate(n.clip_peer):
        remote(src.at[p], dst.at[p], sems.at[0, k], sems.at[1, p], (p, n.row)).wait()


def skipped(n, z, p, relayed):
    if not relayed or not n.line:
        return None
    return jnp.logical_and(n.clip // 2 + p // 2 == 3, jnp.logical_not(n.inner))


def unless(skip, work):
    if skip is None:
        work()
    else:
        pl.when(jnp.logical_not(skip))(work)


def weight_send(n, z, buf, sems, relayed=False):
    mine = buf.at[n.clip]
    remote(mine, mine, sems.at[0, 0], sems.at[1, n.clip], (n.sib, n.row)).start()
    for k, p in enumerate(n.core_peer):
        copy = remote(mine, mine, sems.at[0, 1 + k], sems.at[1, n.clip], (p, n.row))
        unless(skipped(n, z, p, relayed), copy.start)


def weight_relay(n, z, buf, sems):
    if n.line:

        @pl.when(n.inner)
        def _():
            block = buf.at[n.far_end]
            remote(block, block, sems.at[0, 0], sems.at[1, n.far_end], (n.far_end, n.row)).wait_recv()
            remote(block, block, sems.at[0, z.C - 1], sems.at[1, n.far_end], (n.near_end, n.row)).start()


def weight_forward(n, z, buf, sems, relayed=False):
    for k, p in enumerate(n.core_peer):
        block = buf.at[p]
        known = jnp.logical_and(n.inner, p == n.far_end) if relayed and n.line else None
        unless(known, remote(block, block, sems.at[0, 1 + k], sems.at[1, p], (p, n.row)).wait_recv)
        remote(block, block, sems.at[0, z.C // 2 + k], sems.at[1, p], (n.sib, n.row)).start()


def weight_wait(n, z, buf, sems, relayed=False):
    block = buf.at[n.sib]
    remote(block, block, sems.at[0, 0], sems.at[1, n.sib], (n.sib, n.row)).wait()
    for k, p in enumerate(n.core_peer):
        j = (p // 2) * 2 + n.sib % 2
        block = buf.at[j]
        remote(block, block, sems.at[0, 1 + k], sems.at[1, j], (n.sib, n.row)).wait_recv()
        unless(skipped(n, z, p, relayed), remote(block, block, sems.at[0, 1 + k], sems.at[1, j], (n.sib, n.row)).wait_send)
        remote(block, block, sems.at[0, z.C // 2 + k], sems.at[1, j], (n.sib, n.row)).wait_send()
    if relayed and n.line:
        pl.when(n.inner)(remote(block, block, sems.at[0, z.C - 1], sems.at[1, n.sib], (n.sib, n.row)).wait_send)


def flat(x):
    return x.reshape((-1, x.shape[-1]))


def normed(x):
    centre = x - jnp.mean(x, -1, keepdims=True)
    rstd = lax.rsqrt(jnp.mean(centre * centre, -1, keepdims=True) + norm_eps)
    return centre * rstd, rstd


def norm_pull(n_hat, rstd, scale, grad):
    d_shift = jnp.sum(grad, 0, keepdims=True)
    d_scale = jnp.sum(grad * n_hat, 0, keepdims=True)
    dn = grad * (1.0 + scale)
    dx = rstd * (dn - jnp.mean(dn, -1, keepdims=True) - n_hat * jnp.mean(dn * n_hat, -1, keepdims=True))
    return dx, d_shift, d_scale


def vec(n, which, frame):
    return n.mod[which, pl.ds(frame, 1), :]


def frame_rows(z, c, i):
    return pl.ds(pl.multiple_of((c * z.CF + i) * z.LT, z.LT), z.LT)


def tables(n, c):
    x = n.tab[c]
    lane = lax.broadcasted_iota(jnp.int32, x.shape, 1)
    y = pltpu.roll(x, 64, 1)
    sin = jnp.where(lane < 64, y, x)
    return jnp.where(lane < 64, x, y), jnp.where(lane % HSIZE < HSIZE // 2, -sin, sin)


def turn(x, cos, sin):
    lane = lax.broadcasted_iota(jnp.int32, x.shape, 1)
    other = jnp.where(lane % HSIZE < HSIZE // 2, pltpu.roll(x, 128 - HSIZE // 2, 1), pltpu.roll(x, HSIZE // 2, 1))
    return x * cos + other * sin


def gelu_parts(x):
    k = math.sqrt(2.0 / math.pi)
    t = jnp.tanh(k * (x + 0.044715 * (x * x * x)))
    value = 0.5 * x * (1.0 + t)
    slope = 0.5 * (1.0 + t) + 0.5 * x * (1.0 - t * t) * (k * (1.0 + 3 * 0.044715 * (x * x)))
    return value, slope


def causal(z):
    a = (lax.broadcasted_iota(jnp.int32, (z.W, z.W), 0) % z.CT) // z.LT
    b = (lax.broadcasted_iota(jnp.int32, (z.W, z.W), 1) % z.CT) // z.LT
    return a, b


def after(z, c, more):
    if z.N > 1:
        pl.when(c > 0)(lambda: more(c - 1))


def last(z, c, more):
    if z.N > 1:
        pl.when(c == 0)(lambda: more(z.N - 1))


def phase_level(n, z):
    for name in HELD:
        hold(n, name).start()
    n.lv[n.clip] = n.w_level[...].astype(bf16)
    n.ea[n.clip] = n.emb[...]
    pw, hr = D // z.R, z.DR // z.R
    n.pq[n.row, n.clip] = n.w_patch[:, pl.ds(pl.multiple_of(n.row * pw, pw), pw)].astype(n.pq.dtype)
    n.hq[n.row, n.clip] = n.w_head[pl.ds(pl.multiple_of(n.row * hr, hr), hr), :].astype(n.hq.dtype)
    enter(n, z)
    share_clip(n, n.ea, n.ea_s)
    share_clip(n, n.lv, n.lv_s)
    share_clip(n, n.pq.at[n.row], n.pq_s)
    for name in ("wp", "wo", "wg", "wd"):
        hold(n, name).wait()
    for k in range(3):
        n.Wp[n.clip, :, k * z.HW : (k + 1) * z.HW] = n.wp[k].astype(bf16)
    n.Wo[n.clip] = jnp.transpose(n.wo[...]).astype(bf16)
    weight_send(n, z, n.Wo, n.Wo_s)
    tiles = z.FH // 128
    for t in range(tiles):
        for k in range(2):
            at = k * z.FH + t * 128
            n.Wg[n.clip, :, at : at + 128] = n.wg[pl.ds(2 * t + k, z.DR, stride=2 * tiles), :].astype(bf16)
    n.Wd[n.clip] = jnp.transpose(n.wd[...]).astype(bf16)
    share_clip_wait(n, n.ea, n.ea_s)
    share_clip_wait(n, n.lv, n.lv_s)
    pre = dot_nn(flat(n.ea[...]), flat(n.lv[...]))
    n.pre[...] = pre
    cond = (pre * (1.0 / (1.0 + jnp.exp(-pre)))).astype(bf16)
    n.cond[...] = cond
    hold(n, "w_adapt").wait()
    part = dot_nn(cond, n.w_adapt[...].astype(bf16))
    for p in range(z.R):
        for i in range(z.C):
            block = part[i * PAD : i * PAD + z.F, p * z.aw : (p + 1) * z.aw]
            n.pa[p, i * z.F : (i + 1) * z.F, :] = block
    swap_row(n, n.pa, n.ra, n.ra_s)
    share_clip_wait(n, n.pq.at[n.row], n.pq_s)
    share_row(n, n.pq, n.pr_s)
    swap_row_wait(n, n.pa, n.ra, n.ra_s)
    total = n.pa[n.row]
    for p in n.row_peer:
        total = total + n.ra[p]
    n.rs[...] = jnp.zeros_like(n.rs)
    for i in range(z.C):
        n.rs[i, : z.F, :] = total[i * z.F : (i + 1) * z.F]
    n.rb[n.clip] = n.rs[n.clip]
    swap_clip(n, n.rs, n.rb, n.rb_s)
    weight_send(n, z, n.Wp, n.Wp_s)
    share_row_wait(n, n.pq, n.pr_s)
    for name in ("inputs", "tab", "noise", "fw"):
        hold(n, name).wait()
    patch = jnp.concatenate([flat(n.pq[r]) for r in range(z.R)], -1).astype(bf16)
    for c in range(z.N):
        rows = slice(c * z.CT, (c + 1) * z.CT)
        n.stream[rows, :] = dot_nn(n.inputs[rows, :], patch)
    send_hat(n, z, 0)
    swap_clip_wait(n, n.rs, n.rb, n.rb_s)
    for i in range(z.C):
        n.ab[n.row, i * z.F : (i + 1) * z.F, :] = n.rb[i, : z.F, :]
    share_row(n, n.ab, n.ab_s)
    share_clip(n, n.hq.at[n.row], n.hq_s)
    weight_send(n, z, n.Wg, n.Wg_s, True)
    weight_send(n, z, n.Wd, n.Wd_s)
    for c in range(1, z.N):
        send_hat(n, z, c)
        gather_more(n, n.one, n.one_s, c - 1)
    n.mod[...] = jnp.zeros_like(n.mod)
    share_row_wait(n, n.ab, n.ab_s)
    for i in range(z.C):
        for r in range(z.R):
            col = i * z.AW + r * z.aw
            n.mod[col // D, : z.F, col % D : col % D + z.aw] = n.ab[r, i * z.F : (i + 1) * z.F, :]


def send_hat(n, z, c):
    def frame(i, _):
        hat, unused = normed(n.stream[frame_rows(z, c, i), :])
        n.one[c, n.row, pl.ds(pl.multiple_of(i * z.LT, z.LT), z.LT), :] = hat.astype(bf16)
        return 0

    lax.fori_loop(0, z.CF, frame, 0)
    gather_row(n, n.one, n.one_s, c)


def modulate_chunk(n, z, c):
    def frame(step, _):
        p, i = step // z.CF, step % z.CF
        f = c * z.CF + i
        rows = pl.ds(pl.multiple_of(i * z.LT, z.LT), z.LT)
        y = n.one[c, p, rows, :].astype(f32) * (1.0 + vec(n, 1, f)) + vec(n, 0, f)
        n.one[c, p, rows, :] = y.astype(bf16)
        return 0

    lax.fori_loop(0, z.R * z.CF, frame, 0)


def phase_attend(n, z):
    queries = 384 if z.W % 384 == 0 else z.W
    parts = z.W // queries
    weight_forward(n, z, n.Wp, n.Wp_s)
    weight_wait(n, z, n.Wp, n.Wp_s)

    def chunk(c, _):
        if z.N == 1:
            gather_more(n, n.one, n.one_s, c)
        gather_row_wait(n, n.one, n.one_s, c)
        modulate_chunk(n, z, c)
        x = flat(n.one[c])
        pr = dot_nn(x, flat(n.Wp[...]))
        cos, sin = tables(n, c)
        for which in range(3):
            dest = (n.q, n.k, n.v)[which]
            for g in range(z.HW // 128):
                at = which * z.HW + g * 128
                y = pr[:, at : at + 128]
                if which < 2:
                    y = turn(y, cos, sin)
                if which == 0:
                    y = y * HSIZE**-0.5
                y = y.astype(bf16)
                for s in range(128 // HSIZE):
                    dest[g * (128 // HSIZE) + s, c] = y[:, s * HSIZE : (s + 1) * HSIZE]

        def heads(past):
            def head(step, _):
                h, u = step // parts, step % parts
                at = pl.ds(pl.multiple_of(u * queries, queries), queries)
                q = n.q[h, past, at, :]
                s = dot_nt(q, n.k[h, past])
                a = (lax.broadcasted_iota(jnp.int32, s.shape, 0) + u * queries) % z.CT // z.LT
                b = lax.broadcasted_iota(jnp.int32, s.shape, 1) % z.CT // z.LT
                scores = [dot_nt(q, n.k[h, j]) for j in range(past)] + [jnp.where(b <= a, s, -1e30)]
                m = functools.reduce(jnp.maximum, [jnp.max(s, -1, keepdims=True) for s in scores])
                exps = [jnp.exp(s - m) for s in scores]
                total = sum(jnp.sum(e, -1, keepdims=True) for e in exps)
                o = sum(dot_nn(e.astype(bf16), n.v[h, j]) for j, e in enumerate(exps))
                n.oh[h, at, :] = o / total
                lse = jnp.broadcast_to(m + jnp.log(total), (queries, 128))
                n.lse[h, past, :, at] = jnp.transpose(lse)[:8]
                return 0

            lax.fori_loop(0, z.HD * parts, head, 0)

        for past in range(z.N):
            pl.when(c == past)(functools.partial(heads, past))

        @pl.when(c == 0)
        def _():
            weight_forward(n, z, n.Wo, n.Wo_s)
            weight_wait(n, z, n.Wo, n.Wo_s)

        att = jnp.concatenate([n.oh[h] for h in range(z.HD)], -1)
        n.att[c] = att
        n.sb[c] = dot_nt(att.astype(bf16), flat(n.Wo[...])).astype(bf16).reshape(z.R, z.CT, D)
        last(z, c, lambda d: gather_more(n, n.one, n.one_s, d))
        scatter_row(n, n.sb, n.rsr, n.br_s, c)
        pl.when(c == (z.N - 1) // 2)(lambda: weight_relay(n, z, n.Wg, n.Wg_s))
        after(z, c, lambda d: scatter_more(n, n.sb, n.rsr, n.br_s, d))
        return 0

    lax.fori_loop(0, z.N, chunk, 0)


def summed(n, z, c, i):
    rows = pl.ds(pl.multiple_of(i * z.LT, z.LT), z.LT)
    total = n.sb[c, n.row, rows, :].astype(f32)
    for k in range(n.arrivals):
        total = total + n.rsr[c, k, rows, :].astype(f32)
    return total


def phase_two(n, z):
    def chunk(c, _):
        if z.N == 1:
            scatter_more(n, n.sb, n.rsr, n.br_s, c)
        scatter_row_wait(n, n.sb, n.rsr, n.br_s, c)

        def frame(i, _):
            f = c * z.CF + i
            rows = frame_rows(z, c, i)
            branch = summed(n, z, c, i)
            n.branch[rows, :] = branch
            mid = n.stream[rows, :] + vec(n, 2, f) * branch
            hat, unused = normed(mid)
            y = hat * (1.0 + vec(n, 4, f)) + vec(n, 3, f)
            n.two[c, n.row, pl.ds(pl.multiple_of(i * z.LT, z.LT), z.LT), :] = y.astype(bf16)
            return 0

        lax.fori_loop(0, z.CF, frame, 0)
        last(z, c, lambda d: scatter_more(n, n.sb, n.rsr, n.br_s, d))
        gather_row(n, n.two, n.two_s, c)
        after(z, c, lambda d: gather_more(n, n.two, n.two_s, d))
        return 0

    lax.fori_loop(0, z.N, chunk, 0)


def phase_feed(n, z):
    share_clip_wait(n, n.hq.at[n.row], n.hq_s)
    share_row(n, n.hq, n.hr_s)
    weight_forward(n, z, n.Wg, n.Wg_s, True)
    weight_wait(n, z, n.Wg, n.Wg_s, True)
    tile = 256

    def chunk(c, _):
        if z.N == 1:
            gather_more(n, n.two, n.two_s, c)
        gather_row_wait(n, n.two, n.two_s, c)

        def column(t, _):
            at = pl.ds(pl.multiple_of(t * tile, tile), tile)
            up_at = pl.ds(pl.multiple_of(z.FH + t * tile, tile), tile)
            x = flat(n.two[c])
            gate = dot_nn(x, flat(n.Wg[:, :, at]))
            up = dot_nn(x, flat(n.Wg[:, :, up_at]))
            value, unused = gelu_parts(gate)
            n.act[c, :, at] = (value * up).astype(bf16)
            n.gu[c, :, at] = gate.astype(bf16)
            n.gu[c, :, up_at] = up.astype(bf16)
            return 0

        lax.fori_loop(0, z.FH // tile, column, 0)

        @pl.when(c == 0)
        def _():
            weight_forward(n, z, n.Wd, n.Wd_s)
            weight_wait(n, z, n.Wd, n.Wd_s)

        slabs = tile // z.DR

        def output(t, _):
            y = dot_nt(n.act[c], flat(n.Wd[pl.ds(t * slabs, slabs)]))
            at = pl.ds(pl.multiple_of(t * tile, tile), tile)
            n.sb[c, :, :, at] = y.astype(bf16).reshape(z.R, z.CT, tile)
            return 0

        lax.fori_loop(0, D // tile, output, 0)
        last(z, c, lambda d: gather_more(n, n.two, n.two_s, d))
        scatter_row(n, n.sb, n.rsr, n.fd_s, c)
        after(z, c, lambda d: scatter_more(n, n.sb, n.rsr, n.fd_s, d))
        return 0

    lax.fori_loop(0, z.N, chunk, 0)


def phase_top(n, z):
    share_row_wait(n, n.hq, n.hr_s)
    hr = z.DR // z.R
    for i in range(z.C):
        for r in range(z.R):
            n.Wh[i, r * hr : (r + 1) * hr, :] = n.hq[r, i].astype(bf16)
    n.ghead[...] = jnp.zeros_like(n.ghead)
    n.loss[...] = jnp.zeros_like(n.loss)
    n.weight[...] = jnp.sum(n.fw[...].reshape(z.T // 8, 8, z.PF), 0) * (1.0 / z.PF)
    n.gad[...] = jnp.zeros_like(n.gad)

    def chunk(c, _):
        if z.N == 1:
            scatter_more(n, n.sb, n.rsr, n.fd_s, c)
        scatter_row_wait(n, n.sb, n.rsr, n.fd_s, c)

        def ahead(i, _):
            f = c * z.CF + i
            rows = frame_rows(z, c, i)
            here = pl.ds(pl.multiple_of(i * z.LT, z.LT), z.LT)
            feed = summed(n, z, c, i)
            mid = n.stream[rows, :] + vec(n, 2, f) * n.branch[rows, :]
            n.feed[here, :] = feed
            hat, rstd = normed(mid + vec(n, 5, f) * feed)
            n.hat[here, :] = hat
            n.rstd[here, :] = jnp.broadcast_to(rstd, (z.LT, 128))
            n.end[here, :] = (hat * (1.0 + vec(n, 7, f)) + vec(n, 6, f)).astype(bf16)
            return 0

        lax.fori_loop(0, z.CF, ahead, 0)
        rows = pl.ds(pl.multiple_of(c * z.CT, z.CT), z.CT)
        missed = dot_nn(n.end[...], flat(n.Wh[...])) - n.noise[rows, :]
        weight = n.fw[rows, :]
        n.loss[...] += jnp.sum((weight * (missed * missed)).reshape(z.CT // 8, 8, z.PF), 0)
        gp = ((2.0 / z.PF) * weight * missed).astype(bf16)
        n.ghead[...] += dot_tn(n.end[...], gp)
        n.gend[...] = dot_nt(gp, flat(n.Wh[...]))

        def back(i, _):
            f = c * z.CF + i
            rows = frame_rows(z, c, i)
            here = pl.ds(pl.multiple_of(i * z.LT, z.LT), z.LT)
            dx, d_shift, d_scale = norm_pull(n.hat[here, :], n.rstd[here, :1], vec(n, 7, f), n.gend[here, :])
            n.gad[6, pl.ds(f, 1), :] = d_shift
            n.gad[7, pl.ds(f, 1), :] = d_scale
            n.gad[5, pl.ds(f, 1), :] = jnp.sum(dx * n.feed[here, :], 0, keepdims=True)
            n.gmid[rows, :] = dx
            n.gf[c, n.row, here, :] = (dx * vec(n, 5, f)).astype(bf16)
            return 0

        lax.fori_loop(0, z.CF, back, 0)
        last(z, c, lambda d: scatter_more(n, n.sb, n.rsr, n.fd_s, d))
        gather_row(n, n.gf, n.gf_s, c)
        after(z, c, lambda d: gather_more(n, n.gf, n.gf_s, d))
        return 0

    lax.fori_loop(0, z.N, chunk, 0)


def run(body, z, cid, ins, anys, outs, scratch, export, vmem):
    names = list(ins) + list(anys) + list(outs) + list(scratch)

    def kernel(*refs):
        n = types.SimpleNamespace(**dict(zip(names, refs)))
        place(n, z)
        body(n, z)

    result = pl.pallas_call(
        kernel,
        out_shape=[jax.ShapeDtypeStruct(s, d) for s, d in outs.values()],
        in_specs=[pl.BlockSpec(memory_space=pltpu.VMEM)] * len(ins) + [pl.BlockSpec(memory_space=pl.ANY)] * len(anys),
        out_specs=[pl.BlockSpec(memory_space=pl.ANY if k in export else pltpu.VMEM) for k in outs],
        scratch_shapes=list(scratch.values()),
        compiler_params=pltpu.CompilerParams(collective_id=cid, has_side_effects=True, vmem_limit_bytes=vmem),
    )(*ins.values(), *anys.values())
    return dict(zip(outs, result))


KEPT = ("one", "two", "gf", "Wp", "Wo", "Wg", "Wd", "q", "k", "v", "att", "lse", "gu", "act", "stream", "branch", "gmid", "mod")


HELD = ("wp", "wo", "w_adapt", "wg", "wd", "inputs", "tab", "noise", "fw")


def hold(n, name):
    return pltpu.make_async_copy(getattr(n, name + "_i"), getattr(n, name), n.in_s.at[HELD.index(name)])


def forward_body(n, z):
    def export(*names):
        for name in names:
            i = KEPT.index(name)
            pltpu.make_async_copy(getattr(n, name), getattr(n, name + "_o"), n.ex_s.at[i]).start()

    phase_level(n, z)
    export("mod", "stream")
    phase_attend(n, z)
    export("one", "Wp", "Wo", "q", "k", "v", "att", "lse")
    phase_two(n, z)
    export("branch")
    phase_feed(n, z)
    export("two", "Wg", "Wd", "gu", "act")
    phase_top(n, z)
    export("gmid")
    gather_more(n, n.gf, n.gf_s, z.N - 1)
    for c in range(z.N):
        gather_row_wait(n, n.gf, n.gf_s, c)
    export("gf")
    for i, name in enumerate(KEPT):
        pltpu.make_async_copy(getattr(n, name), getattr(n, name + "_o"), n.ex_s.at[i]).wait()


def shapes_of(z):
    rowed = (z.N, z.R, z.CT, D)
    return dict(
        one=(rowed, bf16),
        two=(rowed, bf16),
        gf=(rowed, bf16),
        gb=(rowed, bf16),
        sb=(rowed, bf16),
        rsr=((z.N, z.R - 1, z.CT, D), bf16),
        Wp=((z.C, z.DR, 3 * z.HW), bf16),
        Wo=((z.C, z.DR, z.HW), bf16),
        Wg=((z.C, z.DR, 2 * z.FH), bf16),
        Wd=((z.C, z.DR, z.FH), bf16),
        Wh=((z.C, z.DR, z.PF), bf16),
        q=((z.HD, z.N, z.W, HSIZE), bf16),
        k=((z.HD, z.N, z.W, HSIZE), bf16),
        v=((z.HD, z.N, z.W, HSIZE), bf16),
        att=((z.N, z.W, z.HW), f32),
        oh=((z.HD, z.W, HSIZE), f32),
        lse=((z.HD, z.N, 8, z.W), f32),
        gu=((z.N, z.W, 2 * z.FH), bf16),
        act=((z.N, z.W, z.FH), bf16),
        stream=((z.T, D), f32),
        branch=((z.T, D), f32),
        gmid=((z.T, D), f32),
        mod=((VECTORS, PAD, D), f32),
        gad=((VECTORS, PAD, D), f32),
        ghead=((D, z.PF), f32),
        loss=((8, z.PF), f32),
        weight=((8, z.PF), f32),
        pre=((z.C * PAD, z.LW), f32),
        cond=((z.C * PAD, z.LW), bf16),
        lv=((z.C, z.LR, z.LW), bf16),
        ea=((z.C, PAD, TF), bf16),
        pq=((z.R, z.C, z.PF // z.C, D // z.R), f32 if z.PF // z.C % 16 else bf16),
        hq=((z.R, z.C, z.DR // z.R, z.PF), f32 if z.DR // z.R % 16 else bf16),
        pa=((z.R, z.C * z.F, z.aw), f32),
        ra=((z.R, z.C * z.F, z.aw), f32),
        rs=((z.C, PAD, z.aw), f32),
        rb=((z.C, PAD, z.aw), f32),
        ab=((z.R, z.C * z.F, z.aw), f32),
        feed=((z.CT, D), f32),
        hat=((z.CT, D), f32),
        rstd=((z.CT, 128), f32),
        end=((z.CT, D), bf16),
        gend=((z.CT, D), f32),
    )


def vm(shapes, names):
    return {k: pltpu.VMEM(*shapes[k]) for k in names}


def forward_call(z, ins):
    sh = shapes_of(z)
    direct = ("gad", "ghead", "loss", "weight", "pre", "cond", "ea")
    outs = {k: sh[k] for k in direct}
    outs.update({k + "_o": sh[k] for k in KEPT})
    rest = ["Wh", "oh", "sb", "rsr", "lv", "pq", "hq", "pa", "ra", "rs", "rb", "ab", "feed", "hat", "rstd", "end", "gend"]
    scratch = vm(sh, list(KEPT) + rest)
    dma = pltpu.SemaphoreType.DMA
    for k in ("ea_s", "lv_s", "pq_s", "rb_s", "hq_s", "Wp_s", "Wo_s", "Wg_s", "Wd_s"):
        scratch[k] = dma((2, z.C))
    for k in ("ra_s", "ab_s", "pr_s", "hr_s"):
        scratch[k] = dma((2, z.R))
    for k in ("one_s", "br_s", "two_s", "fd_s", "gf_s"):
        scratch[k] = dma((2, z.N, max(6, z.R)))
    scratch["ex_s"] = dma((len(KEPT),))
    scratch["in_s"] = dma((len(HELD),))
    scratch.update({k: pltpu.VMEM(ins[k].shape, ins[k].dtype) for k in HELD})
    anys = {k + "_i": ins[k] for k in HELD}
    ins = {k: v for k, v in ins.items() if k not in HELD}
    got = run(forward_body, z, 0, ins, anys, outs, scratch, [k + "_o" for k in KEPT], 60 << 20)
    return {(k[:-2] if k.endswith("_o") else k): v for k, v in got.items()}


def forward_inputs(z, a):
    alpha_bar, frame_weight = noise_plan(a["levels"])
    latents = a["latents"].reshape(z.F, z.LT, z.PF)
    noise = a["noise"].reshape(z.F, z.LT, z.PF)
    noisy = jnp.sqrt(alpha_bar)[0, :, None, None] * latents + jnp.sqrt(1.0 - alpha_bar)[0, :, None, None] * noise
    emb = level_embedding(a["levels"][0], TF // 2).astype(bf16)
    return {
        "emb": jnp.pad(emb, ((0, PAD - z.F), (0, 0))),
        "w_level": a["w_level"],
        "w_patch": a["w_patch"],
        "w_head": a["w_head"],
        "w_adapt": a["w_adapt"],
        "wp": jnp.transpose(a["w_project"], (1, 0, 2)),
        "wo": a["w_output"],
        "wg": packed(a["w_gateup"]),
        "wd": a["w_down"],
        "inputs": noisy.astype(bf16).reshape(z.T, z.PF),
        "noise": noise.reshape(z.T, z.PF),
        "fw": jnp.broadcast_to(frame_weight[0][:, None, None], (z.F, z.LT, z.PF)).reshape(z.T, z.PF),
        "tab": jnp.asarray(rotary_consts(z)),
    }


def fetch(n, name):
    i = (LOADED + LATER).index(name)
    return pltpu.make_async_copy(getattr(n, name + "_i"), getattr(n, name), n.in_s.at[i])


def phase_pull_feed(n, z):
    tile = 256
    for name in ("Wd", "gu", "gf"):
        fetch(n, name).wait()

    def chunk(s, _):
        c = z.N - 1 - s
        def column(t, _):
            at = pl.ds(pl.multiple_of(t * tile, tile), tile)
            up_at = pl.ds(pl.multiple_of(z.FH + t * tile, tile), tile)
            da = dot_nn(flat(n.gf[c]), flat(n.Wd[:, :, at]))
            value, slope = gelu_parts(n.gu[c, :, at].astype(f32))
            up = n.gu[c, :, up_at].astype(f32)
            n.gu[c, :, at] = (da * up * slope).astype(bf16)
            n.gu[c, :, up_at] = (da * value).astype(bf16)
            return 0

        lax.fori_loop(0, z.FH // tile, column, 0)

        @pl.when(s == 0)
        def _():
            fetch(n, "Wg").wait()

        slabs = tile // z.DR

        def output(t, _):
            y = dot_nt(n.gu[c], flat(n.Wg[pl.ds(t * slabs, slabs)]))
            at = pl.ds(pl.multiple_of(t * tile, tile), tile)
            n.sb[c, :, :, at] = y.astype(bf16).reshape(z.R, z.CT, tile)
            return 0

        lax.fori_loop(0, D // tile, output, 0)
        scatter_row(n, n.sb, n.rsr, n.gt_s, c)
        after(z, s, lambda d: scatter_more(n, n.sb, n.rsr, n.gt_s, z.N - 1 - d))
        return 0

    lax.fori_loop(0, z.N, chunk, 0)


def weight_grad(n, z, left, right, into):
    half = n.tb.shape[0]
    width = right.shape[-1]
    tile = min(256, width)
    slabs = half // z.DR
    for part in range(D // half):
        for c in range(z.N):
            block = left[c, :, :, part * half : (part + 1) * half]
            n.tb[:, c * z.W : (c + 1) * z.W] = jnp.transpose(flat(block))

        def column(t, _):
            at = pl.ds(pl.multiple_of(t * tile, tile), tile)
            y = dot_nn(n.tb[...], flat(right[:, :, at]).astype(bf16))
            into[part * slabs : (part + 1) * slabs, :, at] = y.astype(bf16).reshape(slabs, z.DR, tile)
            return 0

        lax.fori_loop(0, width // tile, column, 0)


def reduce_one(n, z, part, sx, sems):
    for k in range(z.C // 2):
        j = (n.sib + 2 * k) % z.C
        remote(part.at[j], sx.at[j // 2], sems.at[0, k], sems.at[1, j // 2], (n.sib, n.row)).start()


def reduce_two(n, z, part, sx, sems, rx, more, width, relayed):
    for k in range(z.C // 2):
        j = (n.clip + 2 * k) % z.C
        mine = (n.sib + 2 * k) % z.C
        remote(part.at[mine], sx.at[j // 2], sems.at[0, k], sems.at[1, j // 2], (n.sib, n.row)).wait()
        part[j] = (part[j].astype(f32) + sx[j // 2].astype(f32)).astype(bf16)
        if k:
            back = z.C // 2 - k - 1
            at = slice(0, width)
            copy = remote(part.at[j, :, at], rx.at[back, :, at], more.at[0, k], more.at[1, back], (j, n.row))
            if relayed:
                skip = skipped(n, z, j, True)
                hold = jnp.logical_and(n.inner, k == 2)
                pl.when(jnp.logical_not(jnp.logical_or(skip, hold)))(copy.start)
                pl.when(skip)(remote(part.at[j], n.Xg, n.Xg_s.at[0], n.Xg_s.at[1], (n.relay_to, n.row)).start)
            else:
                copy.start()


def reduce_relay(n, z):
    if n.line:

        @pl.when(n.inner)
        def _():
            j = (n.clip + 4) % z.C
            remote(n.Wg.at[j], n.Xg, n.Xg_s.at[0], n.Xg_s.at[1], (j, n.row)).wait_recv()
            n.Wg[j] = (n.Wg[j].astype(f32) + n.Xg[...].astype(f32)).astype(bf16)
            back = z.C // 2 - 3
            remote(n.Wg.at[j], n.Rg.at[back], n.Rg_s.at[0, 2], n.Rg_s.at[1, back], (j, n.row)).start()


def reduce_late(n, z):
    at = slice(2 * z.HW, 3 * z.HW)
    for k in range(1, z.C // 2):
        j = (n.clip + 2 * k) % z.C
        back = z.C // 2 - k - 1
        remote(n.Wp.at[j, :, at], n.Rp.at[back, :, at], n.Rv_s.at[0, k], n.Rv_s.at[1, back], (j, n.row)).start()


def reduce_three(n, z, part, rx, more, put, late, relayed):
    total = part[n.clip].astype(f32)
    for k in range(1, z.C // 2):
        j = (n.clip + 2 * k) % z.C
        at = slice(0, 2 * z.HW) if late else slice(0, part.shape[2])
        copy = remote(part.at[j, :, at], rx.at[k - 1, :, at], more.at[0, k], more.at[1, k - 1], (j, n.row))
        skip = skipped(n, z, j, relayed)
        unless(skip, copy.wait)
        if skip is not None:
            pl.when(skip)(remote(part.at[j], n.Xg, n.Xg_s.at[0], n.Xg_s.at[1], (n.relay_to, n.row)).wait_send)
        if late:
            at = slice(2 * z.HW, 3 * z.HW)
            remote(part.at[j, :, at], rx.at[k - 1, :, at], n.Rv_s.at[0, k], n.Rv_s.at[1, k - 1], (j, n.row)).wait()
        total = total + rx[k - 1].astype(f32)
    put(total)
    n.squares[...] += fold(total)


def fold(x):
    x = x * x
    total = x[:, :128]
    for i in range(1, x.shape[1] // 128):
        total = total + x[:, i * 128 : (i + 1) * 128]
    return jnp.sum(total.reshape(x.shape[0] // 8, 8, 128), 0)


def phase_pull_two(n, z):
    for name in ("stream", "branch", "gmid") + LATER:
        fetch(n, name).wait()

    def chunk(s, _):
        c = z.N - 1 - s
        scatter_row_wait(n, n.sb, n.rsr, n.gt_s, c)

        def frame(i, _):
            f = c * z.CF + i
            rows = frame_rows(z, c, i)
            branch = n.branch[rows, :]
            hat, rstd = normed(n.stream[rows, :] + vec(n, 2, f) * branch)
            dx, d_shift, d_scale = norm_pull(hat, rstd, vec(n, 4, f), summed(n, z, c, i))
            n.gad[3, pl.ds(f, 1), :] = d_shift
            n.gad[4, pl.ds(f, 1), :] = d_scale
            mid = n.gmid[rows, :] + dx
            n.gmid[rows, :] = mid
            n.gad[2, pl.ds(f, 1), :] = jnp.sum(mid * branch, 0, keepdims=True)
            n.gb[c, n.row, pl.ds(pl.multiple_of(i * z.LT, z.LT), z.LT), :] = (mid * vec(n, 2, f)).astype(bf16)
            return 0

        lax.fori_loop(0, z.CF, frame, 0)
        gather_row(n, n.gb, n.gb_s, c)
        pl.when(s == 0)(lambda: reduce_middle(n, z, "d"))
        after(z, s, lambda d: gather_more(n, n.gb, n.gb_s, z.N - 1 - d))
        return 0

    lax.fori_loop(0, z.N, chunk, 0)


def phase_pull_attend(n, z):
    for name in ("Wo", "q", "k", "v", "att", "lse"):
        fetch(n, name).wait()
    n.dkv[...] = jnp.zeros_like(n.dkv)
    queries = 384 if z.W % 384 == 0 else z.W
    parts = z.W // queries

    def chunk(s, _):
        c = z.N - 1 - s
        if z.N == 1:
            gather_more(n, n.gb, n.gb_s, c)
        gather_row_wait(n, n.gb, n.gb_s, c)
        do = dot_nn(flat(n.gb[c]), flat(n.Wo[...])).astype(bf16)
        for h in range(z.HD):
            mine = do[:, h * HSIZE : (h + 1) * HSIZE]
            n.do[h] = mine
            delta = jnp.sum(mine.astype(f32) * n.att[c, :, h * HSIZE : (h + 1) * HSIZE], -1, keepdims=True)
            n.delta[h] = jnp.transpose(jnp.broadcast_to(delta, (z.W, 128)))[:8]
        pl.when(s == 0)(lambda: reduce_middle(n, z, "g"))

        def head(step, _):
            h, u = step // parts, step % parts
            at = pl.ds(pl.multiple_of(u * queries, queries), queries)
            q, do = n.q[h, c, at, :], n.do[h, at, :]
            lse, delta = n.lse[h, c, :, at][:1], n.delta[h, :, at][:1]

            def block(j, masked):
                k, v = n.k[h, j], n.v[h, j]
                p = jnp.exp(dot_nt(k, q) - lse)
                if masked:
                    a = lax.broadcasted_iota(jnp.int32, p.shape, 0)
                    b = lax.broadcasted_iota(jnp.int32, p.shape, 1) + u * queries
                    p = jnp.where((a % z.CT) // z.LT <= (b % z.CT) // z.LT, p, 0.0)
                dv = dot_nn(p.astype(bf16), do)
                ds = (p * (dot_nt(v, do) - delta)).astype(bf16)
                n.dkv[h, j] += jnp.concatenate([dot_nn(ds, q), dv], -1)
                return dot_tn(ds, k)

            dq = block(c, True)
            n.dq[h, at, :] = lax.fori_loop(0, c, lambda j, dq: dq + block(j, False), dq)
            return 0

        lax.fori_loop(0, z.HD * parts, head, 0)
        last(z, s, lambda d: gather_more(n, n.gb, n.gb_s, z.N - 1 - d))
        pl.when(s == z.N // 2)(lambda: early_row(n, z))
        pl.when(s == z.N // 2)(lambda: reduce_relay(n, z))
        pl.when(s == z.N - 1)(lambda: early_clip(n, z))
        per = 128 // HSIZE
        cos, sin = tables(n, c)
        for g in range(z.HW // 128):
            y = jnp.concatenate([n.dq[g * per + s] for s in range(per)], -1)
            y = turn(y, cos, -sin) * HSIZE**-0.5
            n.gp[c, :, g * 128 : (g + 1) * 128] = y.astype(bf16)
        pl.when(s == 0)(fetch(n, "Wp").wait)
        project_chunk(n, z, c)
        after(z, s, lambda d: scatter_more(n, n.sb, n.rsr, n.go_s, z.N - 1 - d))
        return 0

    lax.fori_loop(0, z.N, chunk, 0)


def project_chunk(n, z, c):
    per = 128 // HSIZE
    tile = 256
    slabs = tile // z.DR
    cos, sin = tables(n, c)
    for g in range(z.HW // 128):
        at = z.HW + g * 128
        y = jnp.concatenate([n.dkv[g * per + h, c][:, :HSIZE] for h in range(per)], -1)
        n.gp[c, :, at : at + 128] = turn(y, cos, -sin).astype(bf16)
        at = 2 * z.HW + g * 128
        y = jnp.concatenate([n.dkv[g * per + h, c][:, HSIZE:] for h in range(per)], -1)
        n.gp[c, :, at : at + 128] = y.astype(bf16)

    def output(t, _):
        y = dot_nt(n.gp[c], flat(n.Wp[pl.ds(t * slabs, slabs)]))
        at = pl.ds(pl.multiple_of(t * tile, tile), tile)
        n.sb[c, :, :, at] = y.astype(bf16).reshape(z.R, z.CT, tile)
        return 0

    lax.fori_loop(0, D // tile, output, 0)
    scatter_row(n, n.sb, n.rsr, n.go_s, c)


def phase_pull_one(n, z):
    def chunk(s, _):
        c = z.N - 1 - s
        scatter_row_wait(n, n.sb, n.rsr, n.go_s, c)

        def frame(i, _):
            f = c * z.CF + i
            rows = frame_rows(z, c, i)
            hat, rstd = normed(n.stream[rows, :])
            dx, d_shift, d_scale = norm_pull(hat, rstd, vec(n, 1, f), summed(n, z, c, i))
            n.gad[0, pl.ds(f, 1), :] = d_shift
            n.gad[1, pl.ds(f, 1), :] = d_scale
            n.gb[c, n.row, pl.ds(pl.multiple_of(i * z.LT, z.LT), z.LT), :] = (n.gmid[rows, :] + dx).astype(bf16)
            return 0

        lax.fori_loop(0, z.CF, frame, 0)
        return 0

    lax.fori_loop(0, z.N, chunk, 0)


def row_total(n, src, dst, cut):
    total = src[n.row, cut].astype(f32)
    for p in n.row_peer:
        total = total + dst[p, cut].astype(f32)
    return total


def swap_row_cut(n, src, dst, sems, cut):
    for k, p in enumerate(n.row_peer):
        remote(src.at[p, cut], dst.at[n.row, cut], sems.at[0, k], sems.at[1, n.row], (n.clip, p)).start()


def swap_row_cut_wait(n, src, dst, sems, cut):
    for k, p in enumerate(n.row_peer):
        remote(src.at[p, cut], dst.at[p, cut], sems.at[0, k], sems.at[1, p], (n.clip, p)).wait()


def is_late(z, clip):
    return clip < z.C // 4


def swap_owner(n, z, late):
    for k, p in enumerate(n.clip_peer):
        copy = remote(n.ca.at[p], n.da.at[n.clip], n.ca_s.at[0, k], n.ca_s.at[1, n.clip], (p, n.row))
        pl.when(is_late(z, p) == late)(copy.start)


def swap_owner_wait(n, z):
    for k, p in enumerate(n.clip_peer):
        remote(n.ca.at[p], n.da.at[p], n.ca_s.at[0, k], n.ca_s.at[1, p], (p, n.row)).wait_recv()


def swap_owner_sent(n, z):
    for k, p in enumerate(n.clip_peer):
        remote(n.ca.at[p], n.da.at[p], n.ca_s.at[0, k], n.ca_s.at[1, p], (p, n.row)).wait_send()


def owner_share(n, z):
    swap_owner_wait(n, z)
    n.da[n.clip] = n.ca[n.clip]
    n.ea2[n.row] = flat(n.da[...])
    share_row(n, n.ea2, n.ea2_s)


def owner_grads(n, z):
    share_row_wait(n, n.ea2, n.ea2_s)
    low = jnp.concatenate([n.ea2[r] for r in range(z.R)], -1)
    n.gc[...] = dot_nt(low, n.w_adapt[...].astype(bf16)).reshape(z.C, PAD, z.LW)
    swap_clip(n, n.gc, n.gd, n.gc_s)
    gadapt = dot_tn(n.cond[...], low)
    n.gadapt[...] = gadapt
    n.squares[...] += fold(gadapt)


def take_columns(n, z, owners):
    for r in range(z.R):
        for i in owners:
            col = i * z.AW + r * z.aw
            n.xa[r, i] = n.gad[col // D, :, col % D : col % D + z.aw]


def early_row(n, z):
    hr = z.DR // z.R
    take_columns(n, z, range(z.C // 4, z.C))
    for r in range(z.R):
        for i in range(z.C):
            at = i * z.DR + r * hr
            n.xh[r, i] = n.ghead[at : at + hr, :].astype(n.xh.dtype)
    swap_row_cut(n, n.xa, n.ya, n.xa_s, pl.ds(z.C // 4, z.C - z.C // 4))
    swap_row(n, n.xh, n.yh, n.xh_s)


def early_clip(n, z):
    cut = pl.ds(z.C // 4, z.C - z.C // 4)
    swap_row_cut_wait(n, n.xa, n.ya, n.xa_s, cut)
    swap_row_wait(n, n.xh, n.yh, n.xh_s)
    n.ca[cut] = row_total(n, n.xa, n.ya, cut).astype(bf16)
    n.ch[...] = row_total(n, n.xh, n.yh, slice(None)).astype(n.ch.dtype)
    swap_owner(n, z, False)
    swap_clip(n, n.ch, n.dh, n.ch_s)
    n.dh[n.clip] = n.ch[n.clip]


def phase_small(n, z):
    pr, hr = z.PF // z.C, z.DR // z.R
    pw = D // z.R
    late = is_late(z, n.clip)
    early = jnp.logical_not(late)
    cut = pl.ds(0, z.C // 4)
    take_columns(n, z, range(z.C // 4))
    swap_row_cut(n, n.xa, n.ya, n.xb_s, cut)
    gpatch = dot_tn(n.inputs[...], jnp.concatenate([n.gb[c, n.row] for c in range(z.N)], 0))
    for r in range(z.R):
        n.xp[r] = gpatch[:, r * pw : (r + 1) * pw].astype(bf16)
    swap_row(n, n.xp, n.yp, n.xp_s)
    pl.when(early)(lambda: owner_share(n, z))
    swap_clip_wait(n, n.ch, n.dh, n.ch_s)
    sh = n.dh[0].astype(f32)
    for i in range(1, z.C):
        sh = sh + n.dh[i].astype(f32)
    n.eh[n.row] = sh
    share_row(n, n.eh, n.eh_s)
    swap_row_cut_wait(n, n.xa, n.ya, n.xb_s, cut)
    n.ca[cut] = row_total(n, n.xa, n.ya, cut).astype(bf16)
    swap_owner(n, z, True)
    swap_row_wait(n, n.xp, n.yp, n.xp_s)
    n.cp[...] = row_total(n, n.xp, n.yp, slice(None)).reshape(z.C, pr, pw).astype(n.cp.dtype)
    swap_clip(n, n.cp, n.dp, n.cp_s)
    n.dp[n.clip] = n.cp[n.clip]
    pl.when(early)(lambda: owner_grads(n, z))
    reduce_late(n, z)
    pl.when(late)(lambda: owner_share(n, z))
    reduce_end(n, z, "d")
    pl.when(late)(lambda: owner_grads(n, z))
    swap_owner_sent(n, z)
    swap_clip_wait(n, n.cp, n.dp, n.cp_s)
    sp = n.dp[0].astype(f32)
    for i in range(1, z.C):
        sp = sp + n.dp[i].astype(f32)
    n.ep[n.row] = sp
    share_row(n, n.ep, n.ep_s)
    n.squares[...] += fold(sp) + fold(sh)
    reduce_end(n, z, "g")
    swap_clip_wait(n, n.gc, n.gd, n.gc_s)
    total = n.gc[n.clip]
    for p in n.clip_peer:
        total = total + n.gd[p]
    pre = n.pre[pl.ds(pl.multiple_of(n.clip * PAD, PAD), PAD), :]
    sig = 1.0 / (1.0 + jnp.exp(-pre))
    n.gl[n.clip] = (total * (sig * (1.0 + pre * (1.0 - sig)))).astype(bf16)
    share_clip(n, n.gl, n.gl_s)
    reduce_end(n, z, "o")
    reduce_end(n, z, "p")
    share_row_wait(n, n.eh, n.eh_s)
    share_row_wait(n, n.ep, n.ep_s)
    for r in range(z.R):
        n.gpatch[:, r * pw : (r + 1) * pw] = n.ep[r]
        n.gheads[r * hr : (r + 1) * hr, :] = n.eh[r]
    share_clip_wait(n, n.gl, n.gl_s)
    n.glv[...] = dot_tn(flat(n.ea[...]), flat(n.gl[...]))
    glevel = n.glv[pl.ds(pl.multiple_of(n.clip * z.LR, z.LR), z.LR), :]
    n.glevel[...] = glevel
    n.squares[...] += fold(glevel)


def phase_stats(n, z):
    lines = [jnp.sum(ref[...], 0, keepdims=True) for ref in (n.squares, n.loss, n.weight)]
    n.sa[n.row] = jnp.concatenate(lines + [jnp.zeros((5, 128), f32)], 0)
    share_row(n, n.sa, n.sa_s)
    share_row_wait(n, n.sa, n.sa_s)
    total = n.sa[0]
    for r in range(1, z.R):
        total = total + n.sa[r]
    n.sc[n.clip] = total
    share_clip(n, n.sc, n.sc_s)
    share_clip_wait(n, n.sc, n.sc_s)
    total = n.sc[0]
    for i in range(1, z.C):
        total = total + n.sc[i]
    n.stats[...] = total


LOADED = ("Wd", "gu", "gf", "Wg", "stream", "branch", "gmid", "act", "two", "Wo", "q", "k", "v", "att", "lse", "Wp", "one")
LATER = ("mod", "gad", "tab", "ghead", "w_adapt", "inputs", "cond", "ea", "pre")


def reduce_start(n, z, x):
    reduce_one(n, z, getattr(n, "W" + x), getattr(n, "S" + x), getattr(n, "S" + x + "_s"))


def reduce_middle(n, z, x):
    part, rx = getattr(n, "W" + x), getattr(n, "R" + x)
    width = 2 * z.HW if x == "p" else part.shape[2]
    reduce_two(n, z, part, getattr(n, "S" + x), getattr(n, "S" + x + "_s"), rx, getattr(n, "R" + x + "_s"), width, x == "g" and n.line)


def reduce_end(n, z, x):
    def put(total):
        if x == "p":
            for k in range(3):
                n.Gp[k] = total[:, k * z.HW : (k + 1) * z.HW]
        elif x == "g":
            tiles = z.FH // 128
            for t in range(tiles):
                for k in range(2):
                    at = k * z.FH + t * 128
                    n.Gg[pl.ds(2 * t + k, z.DR, stride=2 * tiles), :] = total[:, at : at + 128]
        else:
            getattr(n, "G" + x)[...] = jnp.transpose(total)

    reduce_three(n, z, getattr(n, "W" + x), getattr(n, "R" + x), getattr(n, "R" + x + "_s"), put, x == "p", x == "g")


def backward_body(n, z):
    for name in LOADED + LATER:
        if name not in ("one", "two"):
            fetch(n, name).start()
    n.squares[...] = jnp.zeros_like(n.squares)
    if n.line:
        for k, p in enumerate(n.core_peer):

            @pl.when(skipped(n, z, p, True))
            def _():
                n.Rg[k] = jnp.zeros_like(n.Rg[k])

    enter(n, z)
    phase_pull_feed(n, z)
    fetch(n, "act").wait()
    weight_grad(n, z, n.gf, n.act, n.Wd)
    load_two = pltpu.make_async_copy(n.two_i, n.gf, n.in_s.at[LOADED.index("two")])
    load_two.start()
    reduce_start(n, z, "d")
    scatter_more(n, n.sb, n.rsr, n.gt_s, 0)
    phase_pull_two(n, z)
    load_two.wait()
    weight_grad(n, z, n.gf, n.gu, n.Wg)
    load_one = pltpu.make_async_copy(n.one_i, n.gf, n.in_s.at[LOADED.index("one")])
    load_one.start()
    reduce_start(n, z, "g")
    phase_pull_attend(n, z)
    load_one.wait()
    weight_grad(n, z, n.gf, n.gp, n.Wp)
    scatter_more(n, n.sb, n.rsr, n.go_s, 0)
    reduce_start(n, z, "p")
    weight_grad(n, z, n.gb, n.att, n.Wo)
    reduce_start(n, z, "o")
    reduce_middle(n, z, "p")
    reduce_middle(n, z, "o")
    phase_pull_one(n, z)
    phase_small(n, z)
    phase_stats(n, z)


def backward_call(z, kept, ins):
    sh = shapes_of(z)
    pr, hr, pw = z.PF // z.C, z.DR // z.R, D // z.R
    head_type = f32 if hr % 16 else bf16
    patch_type = f32 if pr % 16 else bf16
    widths = {"p": 3 * z.HW, "o": z.HW, "g": 2 * z.FH, "d": z.FH}
    outs = {
        "Gp": ((3, z.DR, z.HW), f32),
        "Go": ((z.HW, z.DR), f32),
        "Gg": ((z.DR * 2 * z.FH // 128, 128), f32),
        "Gd": ((z.FH, z.DR), f32),
    }
    outs.update(
        gpatch=((pr, D), f32),
        gheads=((z.DR, z.PF), f32),
        gadapt=((z.LW, z.AW), f32),
        glevel=((z.LR, z.LW), f32),
        stats=((8, 128), f32),
    )
    anys = {k + "_i": kept[k] for k in LOADED}
    anys.update({k + "_i": ins[k] for k in LATER})
    scratch = vm(sh, [k for k in LOADED if k not in ("one", "two")] + ["gb", "sb", "rsr"])
    scratch.update({k: pltpu.VMEM(ins[k].shape, ins[k].dtype) for k in LATER})
    ins = {k: v for k, v in ins.items() if k not in LATER}
    for x, w in widths.items():
        scratch["S" + x] = pltpu.VMEM((z.C // 2, z.DR, w), bf16)
        scratch["R" + x] = pltpu.VMEM((z.C // 2 - 1, z.DR, w), bf16)
    extra = dict(
        tb=((D // max(2, z.W // 192), z.N * z.W), bf16),
        do=((z.HD, z.W, HSIZE), bf16),
        delta=((z.HD, 8, z.W), f32),
        dq=((z.HD, z.W, HSIZE), f32),
        dkv=((z.HD, z.N, z.W, 2 * HSIZE), f32),
        gp=((z.N, z.W, 3 * z.HW), bf16),
        squares=((8, 128), f32),
        xa=((z.R, z.C, PAD, z.aw), f32),
        ya=((z.R, z.C, PAD, z.aw), f32),
        xp=((z.R, z.PF, pw), bf16),
        yp=((z.R, z.PF, pw), bf16),
        xh=((z.R, z.C, hr, z.PF), head_type),
        yh=((z.R, z.C, hr, z.PF), head_type),
        ca=((z.C, PAD, z.aw), bf16),
        da=((z.C, PAD, z.aw), bf16),
        cp=((z.C, pr, pw), patch_type),
        dp=((z.C, pr, pw), patch_type),
        ch=((z.C, hr, z.PF), head_type),
        dh=((z.C, hr, z.PF), head_type),
        ea2=((z.R, z.C * PAD, z.aw), bf16),
        ep=((z.R, pr, pw), f32),
        eh=((z.R, hr, z.PF), f32),
        gc=((z.C, PAD, z.LW), f32),
        gd=((z.C, PAD, z.LW), f32),
        gl=((z.C, PAD, z.LW), bf16),
        glv=((TF, z.LW), f32),
        sa=((z.R, 8, 128), f32),
        sc=((z.C, 8, 128), f32),
    )
    scratch.update(vm(extra, extra))
    dma = pltpu.SemaphoreType.DMA
    if z.C == 8:
        scratch["Xg"] = pltpu.VMEM((z.DR, 2 * z.FH), bf16)
        scratch["Xg_s"] = dma((2,))
    scratch["Rv_s"] = dma((2, z.C // 2))
    scratch["in_s"] = dma((len(LOADED + LATER),))
    for x in widths:
        scratch["S" + x + "_s"] = dma((2, z.C // 2))
        scratch["R" + x + "_s"] = dma((2, z.C // 2))
    for k in ("gt_s", "gb_s", "go_s"):
        scratch[k] = dma((2, z.N, max(6, z.R)))
    for k in ("xa_s", "xb_s", "xp_s", "xh_s", "ea2_s", "ep_s", "eh_s", "sa_s"):
        scratch[k] = dma((2, z.R))
    for k in ("ca_s", "cp_s", "ch_s", "gc_s", "gl_s", "sc_s"):
        scratch[k] = dma((2, z.C))
    return run(backward_body, z, 1, ins, anys, outs, scratch, (), 64 << 20)


WEIGHTS = ("patch", "level", "adapt", "project", "output", "gateup", "down", "head")


def packed(x):
    rows, pair, width = x.shape
    return jnp.transpose(x.reshape(rows, pair, width // 128, 128), (0, 2, 1, 3)).reshape(-1, 128)


def unpacked(x, shape):
    rows, pair, width = shape
    return jnp.transpose(x.reshape(rows, width // 128, pair, 128), (0, 2, 1, 3)).reshape(shape)


def to_kernel(values):
    values = list(values)
    values[3] = jnp.transpose(values[3], (1, 0, 2))
    values[5] = packed(values[5])
    return values


def from_kernel(values, gateup_shape):
    values = list(values)
    values[3] = jnp.transpose(values[3], (1, 0, 2))
    values[5] = unpacked(values[5], gateup_shape)
    return values


def adam_kernel(pf, stats, *refs):
    grads, masters, firsts, seconds = (refs[8 * i : 8 * i + 8] for i in range(4))
    scalars = refs[32:35]
    news, means, squares = (refs[35 + 8 * i : 43 + 8 * i] for i in range(3))
    weight_sum = jnp.sum(stats[2:3])
    grad_norm = jnp.sqrt(jnp.full((8, 128), jnp.sum(stats[0:1]))) / weight_sum
    factor = jnp.minimum(1.0, clip_level / (grad_norm + 1e-06)) / weight_sum
    scalars[0][0, 0] = jnp.sum(stats[1:2]) / pf
    scalars[1][0, 0] = weight_sum
    scalars[2][0, 0] = jnp.max(grad_norm)
    factor = factor[:1, :1]
    for g, m, f, s, new, mean, square in zip(grads, masters, firsts, seconds, news, means, squares):
        grad = g[...] * factor
        first_new = beta_one * f[...] + (1.0 - beta_one) * grad
        second_new = beta_two * s[...] + (1.0 - beta_two) * grad * grad
        first_hat = first_new * (1.0 / (1.0 - beta_one**STEP))
        second_hat = second_new * (1.0 / (1.0 - beta_two**STEP))
        master = m[...]
        new[...] = master - learn_rate * (first_hat / (jnp.sqrt(second_hat) + adam_eps) + decay_rate * master)
        mean[...] = first_new
        square[...] = second_new


def adam_call(z, stats, grads, masters, firsts, seconds):
    steps = 2
    split = (None, None, 0, 1, 0, 0, 0, 0)

    def spec(x, axis):
        if axis is None:
            return pl.BlockSpec(x.shape, lambda i: (0,) * x.ndim)
        block = tuple(d // steps if k == axis else d for k, d in enumerate(x.shape))
        return pl.BlockSpec(block, lambda i: tuple(i if k == axis else 0 for k in range(x.ndim)))

    specs = [spec(x, axis) for x, axis in zip(masters, split)]
    shapes = [jax.ShapeDtypeStruct(x.shape, f32) for x in masters]
    scalar = jax.ShapeDtypeStruct((1, 1), f32)
    result = pl.pallas_call(
        functools.partial(adam_kernel, z.PF),
        grid=(steps,),
        out_shape=[scalar] * 3 + shapes * 3,
        in_specs=[pl.BlockSpec(stats.shape, lambda i: (0, 0))] + specs * 4,
        out_specs=[pl.BlockSpec((1, 1), lambda i: (0, 0), memory_space=pltpu.SMEM)] * 3 + specs * 3,
        compiler_params=pltpu.CompilerParams(vmem_limit_bytes=64 << 20),
    )(stats, *grads, *masters, *firsts, *seconds)
    return result[:3], result[3:11], result[11:19], result[19:27]


def on_device(latents, noise, levels, *weights):
    masters, firsts, seconds = weights[:8], weights[8:16], weights[16:]
    a = dict(zip(["w_" + k for k in WEIGHTS], masters))
    a.update(latents=latents, noise=noise, levels=levels)
    z = sizes_of(latents, lax.axis_size("clip"), lax.axis_size("row"))
    ins = forward_inputs(z, a)
    kept = forward_call(z, ins)
    back = {k: kept[k] for k in ("gad", "ghead", "loss", "weight", "pre", "cond", "ea", "mod")}
    back.update({k: ins[k] for k in ("w_adapt", "inputs", "tab")})
    g = backward_call(z, kept, back)
    grads = (g["gpatch"], g["glevel"], g["gadapt"], g["Gp"], g["Go"], g["Gg"], g["Gd"], g["gheads"])
    scalars, *results = adam_call(z, g["stats"], grads, *(to_kernel(x) for x in (masters, firsts, seconds)))
    results = [from_kernel(x, masters[5].shape) for x in results]
    return tuple(x.reshape(()) for x in scalars) + tuple(x for result in results for x in result)


def solution(mesh):
    tokens = P("clip", None, "row", None, None)
    by_clip = P("clip", None)
    weights = (by_clip, P("clip", "row"), P("row", "clip"), P("clip", None, "row"), P("row", "clip"))
    weights = weights + (P("clip", None, "row"), P("row", "clip"), by_clip)
    return jax.shard_map(
        on_device,
        mesh=mesh,
        in_specs=(tokens, tokens, by_clip) + weights * 3,
        out_specs=(P(), P(), P()) + weights * 3,
        check_vma=False,
    )
```

```python
import functools
import math
import types

import jax
import jax.numpy as jnp
import numpy as np
from jax import lax
from jax.experimental import pallas as pl
from jax.experimental.pallas import tpu as pltpu
from jax.sharding import PartitionSpec as P

D = 1024
HEADS = 16
HSIZE = 64
TF = 256
LEVELS = 1000
STEP = 3
VECTORS = 8
PAD = 16

norm_eps = 1e-06
clip_level = 0.002
learn_rate = 0.03
beta_one = 0.9
beta_two = 0.95
decay_rate = 0.1
adam_eps = 1e-08

MESH = pl.DeviceIdType.MESH
f32 = jnp.float32
bf16 = jnp.bfloat16


def dot_nn(left, right):
    return jnp.dot(left, right, preferred_element_type=f32)


def dot_nt(left, right):
    return lax.dot_general(left, right, (((1,), (1,)), ((), ())), preferred_element_type=f32)


def dot_tn(left, right):
    return lax.dot_general(left, right, (((0,), (0,)), ((), ())), preferred_element_type=f32)


def frequencies(number):
    return jnp.exp(-math.log(10000.0) * jnp.arange(number, dtype=f32) / number)


def noise_plan(levels):
    ratio = levels.astype(f32) / LEVELS
    alpha_bar = jnp.cos((ratio + 0.008) / 1.008 * (math.pi / 2)) ** 2
    weight = jnp.minimum(1.0, 5.0 * (1.0 - alpha_bar) / alpha_bar)
    return (alpha_bar, weight)


def level_embedding(levels, half):
    angle = levels.astype(f32)[..., None] * frequencies(half)
    return jnp.concatenate([jnp.cos(angle), jnp.sin(angle)], -1)


def sizes_of(latents, clips, parts):
    z = types.SimpleNamespace()
    z.C, z.R = clips, parts
    z.F = latents.shape[1]
    z.rows, z.cols, z.PF = latents.shape[2], latents.shape[3], latents.shape[4]
    z.LT = z.rows * z.cols
    z.N = 3 if z.F % 3 == 0 else 1
    z.CF = z.F // z.N
    z.CT = z.CF * z.LT
    z.W = z.R * z.CT
    z.T = z.F * z.LT
    z.HD = HEADS // parts
    z.HW = z.HD * HSIZE
    z.FH = 4 * D // parts
    z.DR = D // clips
    z.LR = TF // clips
    z.LW = D // parts
    z.AW = VECTORS * D // clips
    z.aw = z.AW // parts
    return z


def rotary_consts(z):
    half = HSIZE // 2
    fp = half // 4
    rp = 3 * half // 8
    cp = half - fp - rp

    def freq(n):
        return np.exp(-math.log(10000.0) * np.arange(n, dtype=np.float32) / np.float32(n)).astype(np.float32)

    shape = (z.N, z.R, z.CF, z.rows, z.cols)
    frame = (np.arange(z.N)[:, None] * z.CF + np.arange(z.CF)[None, :]).astype(np.float32)
    frame = np.broadcast_to(frame[:, None, :, None, None], shape)
    prow = (np.arange(z.R)[:, None] * z.rows + np.arange(z.rows)[None, :]).astype(np.float32)
    prow = np.broadcast_to(prow[None, :, None, :, None], shape)
    pcol = np.broadcast_to(np.arange(z.cols, dtype=np.float32), shape)
    angle = np.concatenate(
        [frame[..., None] * freq(fp), prow[..., None] * freq(rp), pcol[..., None] * freq(cp)], -1
    ).astype(np.float32)
    angle = angle.reshape(z.N, z.W, half)
    cos, sin = np.cos(angle), np.sin(angle)
    return np.concatenate([cos, cos, sin, sin], -1).astype(np.float32)


def remote(src, dst, send_sem, recv_sem, device):
    return pltpu.make_async_remote_copy(
        src_ref=src, dst_ref=dst, send_sem=send_sem, recv_sem=recv_sem, device_id=device, device_id_type=MESH
    )


def place(n, z):
    n.clip = lax.axis_index("clip")
    n.row = lax.axis_index("row")
    n.sib = n.clip + 1 - 2 * (n.clip % 2)
    n.row_peer = [(n.row + k) % z.R for k in range(1, z.R)]
    n.clip_peer = [(n.clip + k) % z.C for k in range(1, z.C)]
    n.square = z.R == 4
    n.far = (n.row + 1 - 2 * (n.row % 2) + 2) % z.R
    n.x = (n.clip, n.row + 1 - 2 * (n.row % 2))
    n.y = (n.clip, (n.row + 2) % z.R)
    n.arrivals = 2 if n.square else z.R - 1
    n.line = z.C == 8
    place = n.clip // 2
    n.inner = jnp.logical_or(place == 1, place == 2)
    n.far_end = jnp.where(n.inner, n.clip + 4 - 8 * (place // 2), n.clip)
    n.near_end = jnp.where(n.inner, n.clip - 2 + 4 * (place // 2), n.clip)
    n.relay_to = jnp.where(place == 0, n.clip + 2, (n.clip - 2 + z.C) % z.C)
    n.core_peer = [(n.clip + 2 * k) % z.C for k in range(1, z.C // 2)]


def enter(n, z):
    barrier = pltpu.get_barrier_semaphore()
    for p in n.row_peer:
        pl.semaphore_signal(barrier, inc=1, device_id=(n.clip, p), device_id_type=MESH)
    for p in n.clip_peer:
        pl.semaphore_signal(barrier, inc=1, device_id=(p, n.row), device_id_type=MESH)
    pl.semaphore_wait(barrier, z.R + z.C - 2)


def send(src, dst, sems, slot, land, device):
    remote(src, dst, sems.at[(0,) + slot], sems.at[(1,) + land], device).start()


def sent(ref, sems, slot, device):
    remote(ref, ref, sems.at[(0,) + slot], sems.at[(1,) + slot], device).wait_send()


def got(ref, sems, slot, device):
    remote(ref, ref, sems.at[(0,) + slot], sems.at[(1,) + slot], device).wait_recv()


def halves(n, ref, c, p):
    rows = ref.shape[2] // 2
    return ref.at[c, p, :rows], ref.at[c, p, rows:]


def gather_row(n, full, sems, c):
    mine = full.at[c, n.row]
    if n.square:
        send(mine, mine, sems, (c, 0), (c, 0), n.x)
        send(mine, mine, sems, (c, 1), (c, 1), n.y)
        return
    for k, p in enumerate(n.row_peer):
        back = len(n.row_peer) - 1 - k
        send(mine, mine, sems, (c, k), (c, back), (n.clip, p))


def gather_more(n, full, sems, c):
    if n.square:
        got(full.at[c, n.x[1]], sems, (c, 0), n.x)
        block = halves(n, full, c, n.x[1])[0]
        send(block, block, sems, (c, 2), (c, 2), n.y)
        got(full.at[c, n.y[1]], sems, (c, 1), n.y)
        block = halves(n, full, c, n.y[1])[1]
        send(block, block, sems, (c, 3), (c, 3), n.x)


def gather_row_wait(n, full, sems, c):
    if n.square:
        low, high = halves(n, full, c, n.far)
        got(low, sems, (c, 2), n.y)
        got(high, sems, (c, 3), n.x)
        mine = full.at[c, n.row]
        sent(mine, sems, (c, 0), n.x)
        sent(mine, sems, (c, 1), n.y)
        sent(low, sems, (c, 2), n.y)
        sent(high, sems, (c, 3), n.x)
        return
    for k, p in enumerate(n.row_peer):
        block = full.at[c, p]
        got(block, sems, (c, k), (n.clip, p))
        sent(block, sems, (c, k), (n.clip, p))


def scatter_row(n, parts, landed, sems, c):
    if n.square:
        (xl, _), (_, yh), (fl, fh) = (halves(n, parts, c, p) for p in (n.x[1], n.y[1], n.far))
        send(fl, halves(n, landed, c, 2)[0], sems, (c, 0), (c, 0), n.x)
        send(fh, halves(n, landed, c, 2)[1], sems, (c, 1), (c, 1), n.y)
        send(xl, halves(n, landed, c, 0)[0], sems, (c, 2), (c, 2), n.x)
        send(yh, halves(n, landed, c, 1)[1], sems, (c, 3), (c, 3), n.y)
        return
    for k, p in enumerate(n.row_peer):
        back = len(n.row_peer) - 1 - k
        send(parts.at[c, p], landed.at[c, back], sems, (c, k), (c, back), (n.clip, p))


def scatter_more(n, parts, landed, sems, c):
    if n.square:
        rows = parts.shape[2] // 2
        low, high = halves(n, landed, c, 2)
        got(low, sems, (c, 0), n.x)
        parts[c, n.y[1], :rows] = (parts[c, n.y[1], :rows].astype(f32) + low[...].astype(f32)).astype(bf16)
        send(halves(n, parts, c, n.y[1])[0], halves(n, landed, c, 1)[0], sems, (c, 5), (c, 5), n.y)
        got(high, sems, (c, 1), n.y)
        parts[c, n.x[1], rows:] = (parts[c, n.x[1], rows:].astype(f32) + high[...].astype(f32)).astype(bf16)
        send(halves(n, parts, c, n.x[1])[1], halves(n, landed, c, 0)[1], sems, (c, 4), (c, 4), n.x)


def scatter_row_wait(n, parts, landed, sems, c):
    if n.square:
        (xl, xh), (yl, yh) = (halves(n, landed, c, k) for k in range(2))
        for slot, ref, peer in ((2, xl, n.x), (3, yh, n.y), (4, xh, n.x), (5, yl, n.y)):
            got(ref, sems, (c, slot), peer)
        for slot in range(6):
            sent(xl, sems, (c, slot), n.x)
        return
    for k, p in enumerate(n.row_peer):
        got(landed.at[c, k], sems, (c, k), (n.clip, p))
        sent(landed.at[c, k], sems, (c, k), (n.clip, p))


def share_row(n, buf, sems):
    for k, p in enumerate(n.row_peer):
        mine = buf.at[n.row]
        remote(mine, mine, sems.at[0, k], sems.at[1, n.row], (n.clip, p)).start()


def share_row_wait(n, buf, sems):
    for k, p in enumerate(n.row_peer):
        block = buf.at[p]
        remote(block, block, sems.at[0, k], sems.at[1, p], (n.clip, p)).wait()


def swap_row(n, src, dst, sems):
    for k, p in enumerate(n.row_peer):
        remote(src.at[p], dst.at[n.row], sems.at[0, k], sems.at[1, n.row], (n.clip, p)).start()


def swap_row_wait(n, src, dst, sems):
    for k, p in enumerate(n.row_peer):
        remote(src.at[p], dst.at[p], sems.at[0, k], sems.at[1, p], (n.clip, p)).wait()


def share_clip(n, buf, sems):
    for k, p in enumerate(n.clip_peer):
        mine = buf.at[n.clip]
        remote(mine, mine, sems.at[0, k], sems.at[1, n.clip], (p, n.row)).start()


def share_clip_wait(n, buf, sems):
    for k, p in enumerate(n.clip_peer):
        block = buf.at[p]
        remote(block, block, sems.at[0, k], sems.at[1, p], (p, n.row)).wait()


def swap_clip(n, src, dst, sems):
    for k, p in enumerate(n.clip_peer):
        remote(src.at[p], dst.at[n.clip], sems.at[0, k], sems.at[1, n.clip], (p, n.row)).start()


def swap_clip_wait(n, src, dst, sems):
    for k, p in enumerate(n.clip_peer):
        remote(src.at[p], dst.at[p], sems.at[0, k], sems.at[1, p], (p, n.row)).wait()


def skipped(n, z, p, relayed):
    if not relayed or not n.line:
        return None
    return jnp.logical_and(n.clip // 2 + p // 2 == 3, jnp.logical_not(n.inner))


def unless(skip, work):
    if skip is None:
        work()
    else:
        pl.when(jnp.logical_not(skip))(work)


def weight_send(n, z, buf, sems, relayed=False):
    mine = buf.at[n.clip]
    remote(mine, mine, sems.at[0, 0], sems.at[1, n.clip], (n.sib, n.row)).start()
    for k, p in enumerate(n.core_peer):
        copy = remote(mine, mine, sems.at[0, 1 + k], sems.at[1, n.clip], (p, n.row))
        unless(skipped(n, z, p, relayed), copy.start)


def weight_relay(n, z, buf, sems):
    if n.line:

        @pl.when(n.inner)
        def _():
            block = buf.at[n.far_end]
            remote(block, block, sems.at[0, 0], sems.at[1, n.far_end], (n.far_end, n.row)).wait_recv()
            remote(block, block, sems.at[0, z.C - 1], sems.at[1, n.far_end], (n.near_end, n.row)).start()


def weight_forward(n, z, buf, sems, relayed=False):
    for k, p in enumerate(n.core_peer):
        block = buf.at[p]
        known = jnp.logical_and(n.inner, p == n.far_end) if relayed and n.line else None
        unless(known, remote(block, block, sems.at[0, 1 + k], sems.at[1, p], (p, n.row)).wait_recv)
        remote(block, block, sems.at[0, z.C // 2 + k], sems.at[1, p], (n.sib, n.row)).start()


def weight_wait(n, z, buf, sems, relayed=False):
    block = buf.at[n.sib]
    remote(block, block, sems.at[0, 0], sems.at[1, n.sib], (n.sib, n.row)).wait()
    for k, p in enumerate(n.core_peer):
        j = (p // 2) * 2 + n.sib % 2
        block = buf.at[j]
        remote(block, block, sems.at[0, 1 + k], sems.at[1, j], (n.sib, n.row)).wait_recv()
        unless(skipped(n, z, p, relayed), remote(block, block, sems.at[0, 1 + k], sems.at[1, j], (n.sib, n.row)).wait_send)
        remote(block, block, sems.at[0, z.C // 2 + k], sems.at[1, j], (n.sib, n.row)).wait_send()
    if relayed and n.line:
        pl.when(n.inner)(remote(block, block, sems.at[0, z.C - 1], sems.at[1, n.sib], (n.sib, n.row)).wait_send)


def flat(x):
    return x.reshape((-1, x.shape[-1]))


def normed(x):
    centre = x - jnp.mean(x, -1, keepdims=True)
    rstd = lax.rsqrt(jnp.mean(centre * centre, -1, keepdims=True) + norm_eps)
    return centre * rstd, rstd


def norm_pull(n_hat, rstd, scale, grad):
    d_shift = jnp.sum(grad, 0, keepdims=True)
    d_scale = jnp.sum(grad * n_hat, 0, keepdims=True)
    dn = grad * (1.0 + scale)
    dx = rstd * (dn - jnp.mean(dn, -1, keepdims=True) - n_hat * jnp.mean(dn * n_hat, -1, keepdims=True))
    return dx, d_shift, d_scale


def vec(n, which, frame):
    return n.mod[which, pl.ds(frame, 1), :]


def frame_rows(z, c, i):
    return pl.ds(pl.multiple_of((c * z.CF + i) * z.LT, z.LT), z.LT)


def tables(n, c):
    x = n.tab[c]
    lane = lax.broadcasted_iota(jnp.int32, x.shape, 1)
    y = pltpu.roll(x, 64, 1)
    sin = jnp.where(lane < 64, y, x)
    return jnp.where(lane < 64, x, y), jnp.where(lane % HSIZE < HSIZE // 2, -sin, sin)


def turn(x, cos, sin):
    lane = lax.broadcasted_iota(jnp.int32, x.shape, 1)
    other = jnp.where(lane % HSIZE < HSIZE // 2, pltpu.roll(x, 128 - HSIZE // 2, 1), pltpu.roll(x, HSIZE // 2, 1))
    return x * cos + other * sin


def gelu_parts(x):
    k = math.sqrt(2.0 / math.pi)
    t = jnp.tanh(k * (x + 0.044715 * (x * x * x)))
    value = 0.5 * x * (1.0 + t)
    slope = 0.5 * (1.0 + t) + 0.5 * x * (1.0 - t * t) * (k * (1.0 + 3 * 0.044715 * (x * x)))
    return value, slope


def causal(z):
    a = (lax.broadcasted_iota(jnp.int32, (z.W, z.W), 0) % z.CT) // z.LT
    b = (lax.broadcasted_iota(jnp.int32, (z.W, z.W), 1) % z.CT) // z.LT
    return a, b


def after(z, c, more):
    if z.N > 1:
        pl.when(c > 0)(lambda: more(c - 1))


def last(z, c, more):
    if z.N > 1:
        pl.when(c == 0)(lambda: more(z.N - 1))


def phase_level(n, z):
    for name in HELD:
        hold(n, name).start()
    n.lv[n.clip] = n.w_level[...].astype(bf16)
    n.ea[n.clip] = n.emb[...]
    pw, hr = D // z.R, z.DR // z.R
    n.pq[n.row, n.clip] = n.w_patch[:, pl.ds(pl.multiple_of(n.row * pw, pw), pw)].astype(n.pq.dtype)
    n.hq[n.row, n.clip] = n.w_head[pl.ds(pl.multiple_of(n.row * hr, hr), hr), :].astype(n.hq.dtype)
    enter(n, z)
    share_clip(n, n.ea, n.ea_s)
    share_clip(n, n.lv, n.lv_s)
    share_clip(n, n.pq.at[n.row], n.pq_s)
    for name in ("wp", "wo", "wg", "wd"):
        hold(n, name).wait()
    for k in range(3):
        n.Wp[n.clip, :, k * z.HW : (k + 1) * z.HW] = n.wp[k].astype(bf16)
    n.Wo[n.clip] = jnp.transpose(n.wo[...]).astype(bf16)
    weight_send(n, z, n.Wo, n.Wo_s)
    tiles = z.FH // 128
    for t in range(tiles):
        for k in range(2):
            at = k * z.FH + t * 128
            n.Wg[n.clip, :, at : at + 128] = n.wg[pl.ds(2 * t + k, z.DR, stride=2 * tiles), :].astype(bf16)
    n.Wd[n.clip] = jnp.transpose(n.wd[...]).astype(bf16)
    share_clip_wait(n, n.ea, n.ea_s)
    share_clip_wait(n, n.lv, n.lv_s)
    pre = dot_nn(flat(n.ea[...]), flat(n.lv[...]))
    n.pre[...] = pre
    cond = (pre * (1.0 / (1.0 + jnp.exp(-pre)))).astype(bf16)
    n.cond[...] = cond
    hold(n, "w_adapt").wait()
    part = dot_nn(cond, n.w_adapt[...].astype(bf16))
    for p in range(z.R):
        for i in range(z.C):
            block = part[i * PAD : i * PAD + z.F, p * z.aw : (p + 1) * z.aw]
            n.pa[p, i * z.F : (i + 1) * z.F, :] = block
    swap_row(n, n.pa, n.ra, n.ra_s)
    share_clip_wait(n, n.pq.at[n.row], n.pq_s)
    share_row(n, n.pq, n.pr_s)
    swap_row_wait(n, n.pa, n.ra, n.ra_s)
    total = n.pa[n.row]
    for p in n.row_peer:
        total = total + n.ra[p]
    n.rs[...] = jnp.zeros_like(n.rs)
    for i in range(z.C):
        n.rs[i, : z.F, :] = total[i * z.F : (i + 1) * z.F]
    n.rb[n.clip] = n.rs[n.clip]
    swap_clip(n, n.rs, n.rb, n.rb_s)
    weight_send(n, z, n.Wp, n.Wp_s)
    share_row_wait(n, n.pq, n.pr_s)
    for name in ("inputs", "tab", "noise", "fw"):
        hold(n, name).wait()
    patch = jnp.concatenate([flat(n.pq[r]) for r in range(z.R)], -1).astype(bf16)
    for c in range(z.N):
        rows = slice(c * z.CT, (c + 1) * z.CT)
        n.stream[rows, :] = dot_nn(n.inputs[rows, :], patch)
    send_hat(n, z, 0)
    swap_clip_wait(n, n.rs, n.rb, n.rb_s)
    for i in range(z.C):
        n.ab[n.row, i * z.F : (i + 1) * z.F, :] = n.rb[i, : z.F, :]
    share_row(n, n.ab, n.ab_s)
    share_clip(n, n.hq.at[n.row], n.hq_s)
    weight_send(n, z, n.Wg, n.Wg_s, True)
    weight_send(n, z, n.Wd, n.Wd_s)
    for c in range(1, z.N):
        send_hat(n, z, c)
        gather_more(n, n.one, n.one_s, c - 1)
    n.mod[...] = jnp.zeros_like(n.mod)
    share_row_wait(n, n.ab, n.ab_s)
    for i in range(z.C):
        for r in range(z.R):
            col = i * z.AW + r * z.aw
            n.mod[col // D, : z.F, col % D : col % D + z.aw] = n.ab[r, i * z.F : (i + 1) * z.F, :]


def send_hat(n, z, c):
    def frame(i, _):
        hat, unused = normed(n.stream[frame_rows(z, c, i), :])
        n.one[c, n.row, pl.ds(pl.multiple_of(i * z.LT, z.LT), z.LT), :] = hat.astype(bf16)
        return 0

    lax.fori_loop(0, z.CF, frame, 0)
    gather_row(n, n.one, n.one_s, c)


def modulate_chunk(n, z, c):
    def frame(step, _):
        p, i = step // z.CF, step % z.CF
        f = c * z.CF + i
        rows = pl.ds(pl.multiple_of(i * z.LT, z.LT), z.LT)
        y = n.one[c, p, rows, :].astype(f32) * (1.0 + vec(n, 1, f)) + vec(n, 0, f)
        n.one[c, p, rows, :] = y.astype(bf16)
        return 0

    lax.fori_loop(0, z.R * z.CF, frame, 0)


def phase_attend(n, z):
    queries = 384 if z.W % 384 == 0 else z.W
    parts = z.W // queries
    weight_forward(n, z, n.Wp, n.Wp_s)
    weight_wait(n, z, n.Wp, n.Wp_s)

    def chunk(c, _):
        if z.N == 1:
            gather_more(n, n.one, n.one_s, c)
        gather_row_wait(n, n.one, n.one_s, c)
        modulate_chunk(n, z, c)
        x = flat(n.one[c])
        pr = dot_nn(x, flat(n.Wp[...]))
        cos, sin = tables(n, c)
        for which in range(3):
            dest = (n.q, n.k, n.v)[which]
            for g in range(z.HW // 128):
                at = which * z.HW + g * 128
                y = pr[:, at : at + 128]
                if which < 2:
                    y = turn(y, cos, sin)
                if which == 0:
                    y = y * HSIZE**-0.5
                y = y.astype(bf16)
                for s in range(128 // HSIZE):
                    dest[g * (128 // HSIZE) + s, c] = y[:, s * HSIZE : (s + 1) * HSIZE]

        def heads(past):
            def head(step, _):
                h, u = step // parts, step % parts
                at = pl.ds(pl.multiple_of(u * queries, queries), queries)
                q = n.q[h, past, at, :]
                s = dot_nt(q, n.k[h, past])
                a = (lax.broadcasted_iota(jnp.int32, s.shape, 0) + u * queries) % z.CT // z.LT
                b = lax.broadcasted_iota(jnp.int32, s.shape, 1) % z.CT // z.LT
                scores = [dot_nt(q, n.k[h, j]) for j in range(past)] + [jnp.where(b <= a, s, -1e30)]
                m = functools.reduce(jnp.maximum, [jnp.max(s, -1, keepdims=True) for s in scores])
                exps = [jnp.exp(s - m) for s in scores]
                total = sum(jnp.sum(e, -1, keepdims=True) for e in exps)
                o = sum(dot_nn(e.astype(bf16), n.v[h, j]) for j, e in enumerate(exps))
                n.oh[h, at, :] = o / total
                lse = jnp.broadcast_to(m + jnp.log(total), (queries, 128))
                n.lse[h, past, :, at] = jnp.transpose(lse)[:8]
                return 0

            lax.fori_loop(0, z.HD * parts, head, 0)

        for past in range(z.N):
            pl.when(c == past)(functools.partial(heads, past))

        @pl.when(c == 0)
        def _():
            weight_forward(n, z, n.Wo, n.Wo_s)
            weight_wait(n, z, n.Wo, n.Wo_s)

        att = jnp.concatenate([n.oh[h] for h in range(z.HD)], -1)
        n.att[c] = att
        n.sb[c] = dot_nt(att.astype(bf16), flat(n.Wo[...])).astype(bf16).reshape(z.R, z.CT, D)
        last(z, c, lambda d: gather_more(n, n.one, n.one_s, d))
        scatter_row(n, n.sb, n.rsr, n.br_s, c)
        pl.when(c == (z.N - 1) // 2)(lambda: weight_relay(n, z, n.Wg, n.Wg_s))
        after(z, c, lambda d: scatter_more(n, n.sb, n.rsr, n.br_s, d))
        return 0

    lax.fori_loop(0, z.N, chunk, 0)


def summed(n, z, c, i):
    rows = pl.ds(pl.multiple_of(i * z.LT, z.LT), z.LT)
    total = n.sb[c, n.row, rows, :].astype(f32)
    for k in range(n.arrivals):
        total = total + n.rsr[c, k, rows, :].astype(f32)
    return total


def phase_two(n, z):
    def chunk(c, _):
        if z.N == 1:
            scatter_more(n, n.sb, n.rsr, n.br_s, c)
        scatter_row_wait(n, n.sb, n.rsr, n.br_s, c)

        def frame(i, _):
            f = c * z.CF + i
            rows = frame_rows(z, c, i)
            branch = summed(n, z, c, i)
            n.branch[rows, :] = branch
            mid = n.stream[rows, :] + vec(n, 2, f) * branch
            hat, unused = normed(mid)
            y = hat * (1.0 + vec(n, 4, f)) + vec(n, 3, f)
            n.two[c, n.row, pl.ds(pl.multiple_of(i * z.LT, z.LT), z.LT), :] = y.astype(bf16)
            return 0

        lax.fori_loop(0, z.CF, frame, 0)
        last(z, c, lambda d: scatter_more(n, n.sb, n.rsr, n.br_s, d))
        gather_row(n, n.two, n.two_s, c)
        after(z, c, lambda d: gather_more(n, n.two, n.two_s, d))
        return 0

    lax.fori_loop(0, z.N, chunk, 0)


def phase_feed(n, z):
    share_clip_wait(n, n.hq.at[n.row], n.hq_s)
    share_row(n, n.hq, n.hr_s)
    weight_forward(n, z, n.Wg, n.Wg_s, True)
    weight_wait(n, z, n.Wg, n.Wg_s, True)
    tile = 256

    def chunk(c, _):
        if z.N == 1:
            gather_more(n, n.two, n.two_s, c)
        gather_row_wait(n, n.two, n.two_s, c)

        def column(t, _):
            at = pl.ds(pl.multiple_of(t * tile, tile), tile)
            up_at = pl.ds(pl.multiple_of(z.FH + t * tile, tile), tile)
            x = flat(n.two[c])
            gate = dot_nn(x, flat(n.Wg[:, :, at]))
            up = dot_nn(x, flat(n.Wg[:, :, up_at]))
            value, unused = gelu_parts(gate)
            n.act[c, :, at] = (value * up).astype(bf16)
            n.gu[c, :, at] = gate.astype(bf16)
            n.gu[c, :, up_at] = up.astype(bf16)
            return 0

        lax.fori_loop(0, z.FH // tile, column, 0)

        @pl.when(c == 0)
        def _():
            weight_forward(n, z, n.Wd, n.Wd_s)
            weight_wait(n, z, n.Wd, n.Wd_s)

        slabs = tile // z.DR

        def output(t, _):
            y = dot_nt(n.act[c], flat(n.Wd[pl.ds(t * slabs, slabs)]))
            at = pl.ds(pl.multiple_of(t * tile, tile), tile)
            n.sb[c, :, :, at] = y.astype(bf16).reshape(z.R, z.CT, tile)
            return 0

        lax.fori_loop(0, D // tile, output, 0)
        last(z, c, lambda d: gather_more(n, n.two, n.two_s, d))
        scatter_row(n, n.sb, n.rsr, n.fd_s, c)
        after(z, c, lambda d: scatter_more(n, n.sb, n.rsr, n.fd_s, d))
        return 0

    lax.fori_loop(0, z.N, chunk, 0)


def phase_top(n, z):
    share_row_wait(n, n.hq, n.hr_s)
    hr = z.DR // z.R
    for i in range(z.C):
        for r in range(z.R):
            n.Wh[i, r * hr : (r + 1) * hr, :] = n.hq[r, i].astype(bf16)
    n.ghead[...] = jnp.zeros_like(n.ghead)
    n.loss[...] = jnp.zeros_like(n.loss)
    n.weight[...] = jnp.sum(n.fw[...].reshape(z.T // 8, 8, z.PF), 0) * (1.0 / z.PF)
    n.gad[...] = jnp.zeros_like(n.gad)

    def chunk(c, _):
        if z.N == 1:
            scatter_more(n, n.sb, n.rsr, n.fd_s, c)
        scatter_row_wait(n, n.sb, n.rsr, n.fd_s, c)

        def ahead(i, _):
            f = c * z.CF + i
            rows = frame_rows(z, c, i)
            here = pl.ds(pl.multiple_of(i * z.LT, z.LT), z.LT)
            feed = summed(n, z, c, i)
            mid = n.stream[rows, :] + vec(n, 2, f) * n.branch[rows, :]
            n.feed[here, :] = feed
            hat, rstd = normed(mid + vec(n, 5, f) * feed)
            n.hat[here, :] = hat
            n.rstd[here, :] = jnp.broadcast_to(rstd, (z.LT, 128))
            n.end[here, :] = (hat * (1.0 + vec(n, 7, f)) + vec(n, 6, f)).astype(bf16)
            return 0

        lax.fori_loop(0, z.CF, ahead, 0)
        rows = pl.ds(pl.multiple_of(c * z.CT, z.CT), z.CT)
        missed = dot_nn(n.end[...], flat(n.Wh[...])) - n.noise[rows, :]
        weight = n.fw[rows, :]
        n.loss[...] += jnp.sum((weight * (missed * missed)).reshape(z.CT // 8, 8, z.PF), 0)
        gp = ((2.0 / z.PF) * weight * missed).astype(bf16)
        n.ghead[...] += dot_tn(n.end[...], gp)
        n.gend[...] = dot_nt(gp, flat(n.Wh[...]))

        def back(i, _):
            f = c * z.CF + i
            rows = frame_rows(z, c, i)
            here = pl.ds(pl.multiple_of(i * z.LT, z.LT), z.LT)
            dx, d_shift, d_scale = norm_pull(n.hat[here, :], n.rstd[here, :1], vec(n, 7, f), n.gend[here, :])
            n.gad[6, pl.ds(f, 1), :] = d_shift
            n.gad[7, pl.ds(f, 1), :] = d_scale
            n.gad[5, pl.ds(f, 1), :] = jnp.sum(dx * n.feed[here, :], 0, keepdims=True)
            n.gmid[rows, :] = dx
            n.gf[c, n.row, here, :] = (dx * vec(n, 5, f)).astype(bf16)
            return 0

        lax.fori_loop(0, z.CF, back, 0)
        last(z, c, lambda d: scatter_more(n, n.sb, n.rsr, n.fd_s, d))
        gather_row(n, n.gf, n.gf_s, c)
        after(z, c, lambda d: gather_more(n, n.gf, n.gf_s, d))
        return 0

    lax.fori_loop(0, z.N, chunk, 0)


def run(body, z, cid, ins, anys, outs, scratch, export, vmem):
    names = list(ins) + list(anys) + list(outs) + list(scratch)

    def kernel(*refs):
        n = types.SimpleNamespace(**dict(zip(names, refs)))
        place(n, z)
        body(n, z)

    result = pl.pallas_call(
        kernel,
        out_shape=[jax.ShapeDtypeStruct(s, d) for s, d in outs.values()],
        in_specs=[pl.BlockSpec(memory_space=pltpu.VMEM)] * len(ins) + [pl.BlockSpec(memory_space=pl.ANY)] * len(anys),
        out_specs=[pl.BlockSpec(memory_space=pl.ANY if k in export else pltpu.VMEM) for k in outs],
        scratch_shapes=list(scratch.values()),
        compiler_params=pltpu.CompilerParams(collective_id=cid, has_side_effects=True, vmem_limit_bytes=vmem),
    )(*ins.values(), *anys.values())
    return dict(zip(outs, result))


KEPT = ("one", "two", "gf", "Wp", "Wo", "Wg", "Wd", "q", "k", "v", "att", "lse", "gu", "act", "stream", "branch", "gmid", "mod")


HELD = ("wp", "wo", "w_adapt", "wg", "wd", "inputs", "tab", "noise", "fw")


def hold(n, name):
    return pltpu.make_async_copy(getattr(n, name + "_i"), getattr(n, name), n.in_s.at[HELD.index(name)])


def forward_body(n, z):
    def export(*names):
        for name in names:
            i = KEPT.index(name)
            pltpu.make_async_copy(getattr(n, name), getattr(n, name + "_o"), n.ex_s.at[i]).start()

    phase_level(n, z)
    export("mod", "stream")
    phase_attend(n, z)
    export("one", "Wp", "Wo", "q", "k", "v", "att", "lse")
    phase_two(n, z)
    export("branch")
    phase_feed(n, z)
    export("two", "Wg", "Wd", "gu", "act")
    phase_top(n, z)
    export("gmid")
    gather_more(n, n.gf, n.gf_s, z.N - 1)
    for c in range(z.N):
        gather_row_wait(n, n.gf, n.gf_s, c)
    export("gf")
    for i, name in enumerate(KEPT):
        pltpu.make_async_copy(getattr(n, name), getattr(n, name + "_o"), n.ex_s.at[i]).wait()


def shapes_of(z):
    rowed = (z.N, z.R, z.CT, D)
    return dict(
        one=(rowed, bf16),
        two=(rowed, bf16),
        gf=(rowed, bf16),
        gb=(rowed, bf16),
        sb=(rowed, bf16),
        rsr=((z.N, z.R - 1, z.CT, D), bf16),
        Wp=((z.C, z.DR, 3 * z.HW), bf16),
        Wo=((z.C, z.DR, z.HW), bf16),
        Wg=((z.C, z.DR, 2 * z.FH), bf16),
        Wd=((z.C, z.DR, z.FH), bf16),
        Wh=((z.C, z.DR, z.PF), bf16),
        q=((z.HD, z.N, z.W, HSIZE), bf16),
        k=((z.HD, z.N, z.W, HSIZE), bf16),
        v=((z.HD, z.N, z.W, HSIZE), bf16),
        att=((z.N, z.W, z.HW), f32),
        oh=((z.HD, z.W, HSIZE), f32),
        lse=((z.HD, z.N, 8, z.W), f32),
        gu=((z.N, z.W, 2 * z.FH), bf16),
        act=((z.N, z.W, z.FH), bf16),
        stream=((z.T, D), f32),
        branch=((z.T, D), f32),
        gmid=((z.T, D), f32),
        mod=((VECTORS, PAD, D), f32),
        gad=((VECTORS, PAD, D), f32),
        ghead=((D, z.PF), f32),
        loss=((8, z.PF), f32),
        weight=((8, z.PF), f32),
        pre=((z.C * PAD, z.LW), f32),
        cond=((z.C * PAD, z.LW), bf16),
        lv=((z.C, z.LR, z.LW), bf16),
        ea=((z.C, PAD, TF), bf16),
        pq=((z.R, z.C, z.PF // z.C, D // z.R), f32 if z.PF // z.C % 16 else bf16),
        hq=((z.R, z.C, z.DR // z.R, z.PF), f32 if z.DR // z.R % 16 else bf16),
        pa=((z.R, z.C * z.F, z.aw), f32),
        ra=((z.R, z.C * z.F, z.aw), f32),
        rs=((z.C, PAD, z.aw), f32),
        rb=((z.C, PAD, z.aw), f32),
        ab=((z.R, z.C * z.F, z.aw), f32),
        feed=((z.CT, D), f32),
        hat=((z.CT, D), f32),
        rstd=((z.CT, 128), f32),
        end=((z.CT, D), bf16),
        gend=((z.CT, D), f32),
    )


def vm(shapes, names):
    return {k: pltpu.VMEM(*shapes[k]) for k in names}


def forward_call(z, ins):
    sh = shapes_of(z)
    direct = ("gad", "ghead", "loss", "weight", "pre", "cond", "ea")
    outs = {k: sh[k] for k in direct}
    outs.update({k + "_o": sh[k] for k in KEPT})
    rest = ["Wh", "oh", "sb", "rsr", "lv", "pq", "hq", "pa", "ra", "rs", "rb", "ab", "feed", "hat", "rstd", "end", "gend"]
    scratch = vm(sh, list(KEPT) + rest)
    dma = pltpu.SemaphoreType.DMA
    for k in ("ea_s", "lv_s", "pq_s", "rb_s", "hq_s", "Wp_s", "Wo_s", "Wg_s", "Wd_s"):
        scratch[k] = dma((2, z.C))
    for k in ("ra_s", "ab_s", "pr_s", "hr_s"):
        scratch[k] = dma((2, z.R))
    for k in ("one_s", "br_s", "two_s", "fd_s", "gf_s"):
        scratch[k] = dma((2, z.N, max(6, z.R)))
    scratch["ex_s"] = dma((len(KEPT),))
    scratch["in_s"] = dma((len(HELD),))
    scratch.update({k: pltpu.VMEM(ins[k].shape, ins[k].dtype) for k in HELD})
    anys = {k + "_i": ins[k] for k in HELD}
    ins = {k: v for k, v in ins.items() if k not in HELD}
    got = run(forward_body, z, 0, ins, anys, outs, scratch, [k + "_o" for k in KEPT], 60 << 20)
    return {(k[:-2] if k.endswith("_o") else k): v for k, v in got.items()}


def forward_inputs(z, a):
    alpha_bar, frame_weight = noise_plan(a["levels"])
    latents = a["latents"].reshape(z.F, z.LT, z.PF)
    noise = a["noise"].reshape(z.F, z.LT, z.PF)
    noisy = jnp.sqrt(alpha_bar)[0, :, None, None] * latents + jnp.sqrt(1.0 - alpha_bar)[0, :, None, None] * noise
    emb = level_embedding(a["levels"][0], TF // 2).astype(bf16)
    return {
        "emb": jnp.pad(emb, ((0, PAD - z.F), (0, 0))),
        "w_level": a["w_level"],
        "w_patch": a["w_patch"],
        "w_head": a["w_head"],
        "w_adapt": a["w_adapt"],
        "wp": jnp.transpose(a["w_project"], (1, 0, 2)),
        "wo": a["w_output"],
        "wg": packed(a["w_gateup"]),
        "wd": a["w_down"],
        "inputs": noisy.astype(bf16).reshape(z.T, z.PF),
        "noise": noise.reshape(z.T, z.PF),
        "fw": jnp.broadcast_to(frame_weight[0][:, None, None], (z.F, z.LT, z.PF)).reshape(z.T, z.PF),
        "tab": jnp.asarray(rotary_consts(z)),
    }


def fetch(n, name):
    i = (LOADED + LATER).index(name)
    return pltpu.make_async_copy(getattr(n, name + "_i"), getattr(n, name), n.in_s.at[i])


def phase_pull_feed(n, z):
    tile = 256
    for name in ("Wd", "gu", "gf"):
        fetch(n, name).wait()

    def chunk(s, _):
        c = z.N - 1 - s
        def column(t, _):
            at = pl.ds(pl.multiple_of(t * tile, tile), tile)
            up_at = pl.ds(pl.multiple_of(z.FH + t * tile, tile), tile)
            da = dot_nn(flat(n.gf[c]), flat(n.Wd[:, :, at]))
            value, slope = gelu_parts(n.gu[c, :, at].astype(f32))
            up = n.gu[c, :, up_at].astype(f32)
            n.gu[c, :, at] = (da * up * slope).astype(bf16)
            n.gu[c, :, up_at] = (da * value).astype(bf16)
            return 0

        lax.fori_loop(0, z.FH // tile, column, 0)

        @pl.when(s == 0)
        def _():
            fetch(n, "Wg").wait()

        slabs = tile // z.DR

        def output(t, _):
            y = dot_nt(n.gu[c], flat(n.Wg[pl.ds(t * slabs, slabs)]))
            at = pl.ds(pl.multiple_of(t * tile, tile), tile)
            n.sb[c, :, :, at] = y.astype(bf16).reshape(z.R, z.CT, tile)
            return 0

        lax.fori_loop(0, D // tile, output, 0)
        scatter_row(n, n.sb, n.rsr, n.gt_s, c)
        after(z, s, lambda d: scatter_more(n, n.sb, n.rsr, n.gt_s, z.N - 1 - d))
        return 0

    lax.fori_loop(0, z.N, chunk, 0)


def weight_grad(n, z, left, right, into):
    half = n.tb.shape[0]
    width = right.shape[-1]
    tile = next(t for t in (512, 256, 128) if width % t == 0)
    slabs = half // z.DR
    for part in range(D // half):
        for c in range(z.N):
            block = left[c, :, :, part * half : (part + 1) * half]
            n.tb[:, c * z.W : (c + 1) * z.W] = jnp.transpose(flat(block))

        def column(t, _):
            at = pl.ds(pl.multiple_of(t * tile, tile), tile)
            y = dot_nn(n.tb[...], flat(right[:, :, at]).astype(bf16))
            into[part * slabs : (part + 1) * slabs, :, at] = y.astype(bf16).reshape(slabs, z.DR, tile)
            return 0

        lax.fori_loop(0, width // tile, column, 0)


def reduce_one(n, z, part, sx, sems):
    for k in range(z.C // 2):
        j = (n.sib + 2 * k) % z.C
        remote(part.at[j], sx.at[j // 2], sems.at[0, k], sems.at[1, j // 2], (n.sib, n.row)).start()


def reduce_two(n, z, part, sx, sems, rx, more, width, relayed):
    for k in range(z.C // 2):
        j = (n.clip + 2 * k) % z.C
        mine = (n.sib + 2 * k) % z.C
        remote(part.at[mine], sx.at[j // 2], sems.at[0, k], sems.at[1, j // 2], (n.sib, n.row)).wait()
        part[j] = (part[j].astype(f32) + sx[j // 2].astype(f32)).astype(bf16)
        if k:
            back = z.C // 2 - k - 1
            at = slice(0, width)
            copy = remote(part.at[j, :, at], rx.at[back, :, at], more.at[0, k], more.at[1, back], (j, n.row))
            if relayed:
                skip = skipped(n, z, j, True)
                hold = jnp.logical_and(n.inner, k == 2)
                pl.when(jnp.logical_not(jnp.logical_or(skip, hold)))(copy.start)
                pl.when(skip)(remote(part.at[j], n.Xg, n.Xg_s.at[0], n.Xg_s.at[1], (n.relay_to, n.row)).start)
            else:
                copy.start()


def reduce_relay(n, z):
    if n.line:

        @pl.when(n.inner)
        def _():
            j = (n.clip + 4) % z.C
            remote(n.Wg.at[j], n.Xg, n.Xg_s.at[0], n.Xg_s.at[1], (j, n.row)).wait_recv()
            n.Wg[j] = (n.Wg[j].astype(f32) + n.Xg[...].astype(f32)).astype(bf16)
            back = z.C // 2 - 3
            remote(n.Wg.at[j], n.Rg.at[back], n.Rg_s.at[0, 2], n.Rg_s.at[1, back], (j, n.row)).start()


def reduce_late(n, z):
    at = slice(2 * z.HW, 3 * z.HW)
    for k in range(1, z.C // 2):
        j = (n.clip + 2 * k) % z.C
        back = z.C // 2 - k - 1
        remote(n.Wp.at[j, :, at], n.Rp.at[back, :, at], n.Rv_s.at[0, k], n.Rv_s.at[1, back], (j, n.row)).start()


def reduce_three(n, z, part, rx, more, put, late, relayed):
    total = part[n.clip].astype(f32)
    for k in range(1, z.C // 2):
        j = (n.clip + 2 * k) % z.C
        at = slice(0, 2 * z.HW) if late else slice(0, part.shape[2])
        copy = remote(part.at[j, :, at], rx.at[k - 1, :, at], more.at[0, k], more.at[1, k - 1], (j, n.row))
        skip = skipped(n, z, j, relayed)
        unless(skip, copy.wait)
        if skip is not None:
            pl.when(skip)(remote(part.at[j], n.Xg, n.Xg_s.at[0], n.Xg_s.at[1], (n.relay_to, n.row)).wait_send)
        if late:
            at = slice(2 * z.HW, 3 * z.HW)
            remote(part.at[j, :, at], rx.at[k - 1, :, at], n.Rv_s.at[0, k], n.Rv_s.at[1, k - 1], (j, n.row)).wait()
        total = total + rx[k - 1].astype(f32)
    put(total)
    n.squares[...] += fold(total)


def fold(x):
    x = x * x
    total = x[:, :128]
    for i in range(1, x.shape[1] // 128):
        total = total + x[:, i * 128 : (i + 1) * 128]
    return jnp.sum(total.reshape(x.shape[0] // 8, 8, 128), 0)


def phase_pull_two(n, z):
    for name in ("stream", "branch", "gmid") + LATER:
        fetch(n, name).wait()

    def chunk(s, _):
        c = z.N - 1 - s
        scatter_row_wait(n, n.sb, n.rsr, n.gt_s, c)

        def frame(i, _):
            f = c * z.CF + i
            rows = frame_rows(z, c, i)
            branch = n.branch[rows, :]
            hat, rstd = normed(n.stream[rows, :] + vec(n, 2, f) * branch)
            dx, d_shift, d_scale = norm_pull(hat, rstd, vec(n, 4, f), summed(n, z, c, i))
            n.gad[3, pl.ds(f, 1), :] = d_shift
            n.gad[4, pl.ds(f, 1), :] = d_scale
            mid = n.gmid[rows, :] + dx
            n.gmid[rows, :] = mid
            n.gad[2, pl.ds(f, 1), :] = jnp.sum(mid * branch, 0, keepdims=True)
            n.gb[c, n.row, pl.ds(pl.multiple_of(i * z.LT, z.LT), z.LT), :] = (mid * vec(n, 2, f)).astype(bf16)
            return 0

        lax.fori_loop(0, z.CF, frame, 0)
        gather_row(n, n.gb, n.gb_s, c)
        pl.when(s == 0)(lambda: reduce_middle(n, z, "d"))
        after(z, s, lambda d: gather_more(n, n.gb, n.gb_s, z.N - 1 - d))
        return 0

    lax.fori_loop(0, z.N, chunk, 0)


def phase_pull_attend(n, z):
    for name in ("Wo", "q", "k", "v", "att", "lse"):
        fetch(n, name).wait()
    n.dkv[...] = jnp.zeros_like(n.dkv)
    queries = 384 if z.W % 384 == 0 else z.W
    parts = z.W // queries

    def chunk(s, _):
        c = z.N - 1 - s
        if z.N == 1:
            gather_more(n, n.gb, n.gb_s, c)
        gather_row_wait(n, n.gb, n.gb_s, c)
        do = dot_nn(flat(n.gb[c]), flat(n.Wo[...])).astype(bf16)
        for h in range(z.HD):
            mine = do[:, h * HSIZE : (h + 1) * HSIZE]
            n.do[h] = mine
            delta = jnp.sum(mine.astype(f32) * n.att[c, :, h * HSIZE : (h + 1) * HSIZE], -1, keepdims=True)
            n.delta[h] = jnp.transpose(jnp.broadcast_to(delta, (z.W, 128)))[:8]
        pl.when(s == 0)(lambda: reduce_middle(n, z, "g"))

        def head(step, _):
            h, u = step // parts, step % parts
            at = pl.ds(pl.multiple_of(u * queries, queries), queries)
            q, do = n.q[h, c, at, :], n.do[h, at, :]
            lse, delta = n.lse[h, c, :, at][:1], n.delta[h, :, at][:1]

            def block(j, masked):
                k, v = n.k[h, j], n.v[h, j]
                p = jnp.exp(dot_nt(k, q) - lse)
                if masked:
                    a = lax.broadcasted_iota(jnp.int32, p.shape, 0)
                    b = lax.broadcasted_iota(jnp.int32, p.shape, 1) + u * queries
                    p = jnp.where((a % z.CT) // z.LT <= (b % z.CT) // z.LT, p, 0.0)
                dv = dot_nn(p.astype(bf16), do)
                ds = (p * (dot_nt(v, do) - delta)).astype(bf16)
                n.dkv[h, j] += jnp.concatenate([dot_nn(ds, q), dv], -1)
                return dot_tn(ds, k)

            dq = block(c, True)
            n.dq[h, at, :] = lax.fori_loop(0, c, lambda j, dq: dq + block(j, False), dq)
            return 0

        lax.fori_loop(0, z.HD * parts, head, 0)
        last(z, s, lambda d: gather_more(n, n.gb, n.gb_s, z.N - 1 - d))
        pl.when(s == z.N // 2)(lambda: early_row(n, z))
        pl.when(s == z.N // 2)(lambda: reduce_relay(n, z))
        pl.when(s == z.N - 1)(lambda: early_clip(n, z))
        per = 128 // HSIZE
        cos, sin = tables(n, c)
        for g in range(z.HW // 128):
            y = jnp.concatenate([n.dq[g * per + s] for s in range(per)], -1)
            y = turn(y, cos, -sin) * HSIZE**-0.5
            n.gp[c, :, g * 128 : (g + 1) * 128] = y.astype(bf16)
        pl.when(s == 0)(fetch(n, "Wp").wait)
        project_chunk(n, z, c)
        after(z, s, lambda d: scatter_more(n, n.sb, n.rsr, n.go_s, z.N - 1 - d))
        return 0

    lax.fori_loop(0, z.N, chunk, 0)


def project_chunk(n, z, c):
    per = 128 // HSIZE
    tile = 256
    slabs = tile // z.DR
    cos, sin = tables(n, c)
    for g in range(z.HW // 128):
        at = z.HW + g * 128
        y = jnp.concatenate([n.dkv[g * per + h, c][:, :HSIZE] for h in range(per)], -1)
        n.gp[c, :, at : at + 128] = turn(y, cos, -sin).astype(bf16)
        at = 2 * z.HW + g * 128
        y = jnp.concatenate([n.dkv[g * per + h, c][:, HSIZE:] for h in range(per)], -1)
        n.gp[c, :, at : at + 128] = y.astype(bf16)

    def output(t, _):
        y = dot_nt(n.gp[c], flat(n.Wp[pl.ds(t * slabs, slabs)]))
        at = pl.ds(pl.multiple_of(t * tile, tile), tile)
        n.sb[c, :, :, at] = y.astype(bf16).reshape(z.R, z.CT, tile)
        return 0

    lax.fori_loop(0, D // tile, output, 0)
    scatter_row(n, n.sb, n.rsr, n.go_s, c)


def phase_pull_one(n, z):
    def chunk(s, _):
        c = z.N - 1 - s
        scatter_row_wait(n, n.sb, n.rsr, n.go_s, c)

        def frame(i, _):
            f = c * z.CF + i
            rows = frame_rows(z, c, i)
            hat, rstd = normed(n.stream[rows, :])
            dx, d_shift, d_scale = norm_pull(hat, rstd, vec(n, 1, f), summed(n, z, c, i))
            n.gad[0, pl.ds(f, 1), :] = d_shift
            n.gad[1, pl.ds(f, 1), :] = d_scale
            n.gb[c, n.row, pl.ds(pl.multiple_of(i * z.LT, z.LT), z.LT), :] = (n.gmid[rows, :] + dx).astype(bf16)
            return 0

        lax.fori_loop(0, z.CF, frame, 0)
        return 0

    lax.fori_loop(0, z.N, chunk, 0)


def row_total(n, src, dst, cut):
    total = src[n.row, cut].astype(f32)
    for p in n.row_peer:
        total = total + dst[p, cut].astype(f32)
    return total


def swap_row_cut(n, src, dst, sems, cut):
    for k, p in enumerate(n.row_peer):
        remote(src.at[p, cut], dst.at[n.row, cut], sems.at[0, k], sems.at[1, n.row], (n.clip, p)).start()


def swap_row_cut_wait(n, src, dst, sems, cut):
    for k, p in enumerate(n.row_peer):
        remote(src.at[p, cut], dst.at[p, cut], sems.at[0, k], sems.at[1, p], (n.clip, p)).wait()


def is_late(z, clip):
    return clip < z.C // 4


def swap_owner(n, z, late):
    for k, p in enumerate(n.clip_peer):
        copy = remote(n.ca.at[p], n.da.at[n.clip], n.ca_s.at[0, k], n.ca_s.at[1, n.clip], (p, n.row))
        pl.when(is_late(z, p) == late)(copy.start)


def swap_owner_wait(n, z):
    for k, p in enumerate(n.clip_peer):
        remote(n.ca.at[p], n.da.at[p], n.ca_s.at[0, k], n.ca_s.at[1, p], (p, n.row)).wait_recv()


def swap_owner_sent(n, z):
    for k, p in enumerate(n.clip_peer):
        remote(n.ca.at[p], n.da.at[p], n.ca_s.at[0, k], n.ca_s.at[1, p], (p, n.row)).wait_send()


def owner_share(n, z):
    swap_owner_wait(n, z)
    n.da[n.clip] = n.ca[n.clip]
    n.ea2[n.row] = flat(n.da[...])
    share_row(n, n.ea2, n.ea2_s)


def owner_grads(n, z):
    share_row_wait(n, n.ea2, n.ea2_s)
    low = jnp.concatenate([n.ea2[r] for r in range(z.R)], -1)
    n.gc[...] = dot_nt(low, n.w_adapt[...].astype(bf16)).reshape(z.C, PAD, z.LW)
    swap_clip(n, n.gc, n.gd, n.gc_s)
    gadapt = dot_tn(n.cond[...], low)
    n.gadapt[...] = gadapt
    n.squares[...] += fold(gadapt)


def take_columns(n, z, owners):
    for r in range(z.R):
        for i in owners:
            col = i * z.AW + r * z.aw
            n.xa[r, i] = n.gad[col // D, :, col % D : col % D + z.aw]


def early_row(n, z):
    hr = z.DR // z.R
    take_columns(n, z, range(z.C // 4, z.C))
    for r in range(z.R):
        for i in range(z.C):
            at = i * z.DR + r * hr
            n.xh[r, i] = n.ghead[at : at + hr, :].astype(n.xh.dtype)
    swap_row_cut(n, n.xa, n.ya, n.xa_s, pl.ds(z.C // 4, z.C - z.C // 4))
    swap_row(n, n.xh, n.yh, n.xh_s)


def early_clip(n, z):
    cut = pl.ds(z.C // 4, z.C - z.C // 4)
    swap_row_cut_wait(n, n.xa, n.ya, n.xa_s, cut)
    swap_row_wait(n, n.xh, n.yh, n.xh_s)
    n.ca[cut] = row_total(n, n.xa, n.ya, cut).astype(bf16)
    n.ch[...] = row_total(n, n.xh, n.yh, slice(None)).astype(n.ch.dtype)
    swap_owner(n, z, False)
    swap_clip(n, n.ch, n.dh, n.ch_s)
    n.dh[n.clip] = n.ch[n.clip]


def phase_small(n, z):
    pr, hr = z.PF // z.C, z.DR // z.R
    pw = D // z.R
    late = is_late(z, n.clip)
    early = jnp.logical_not(late)
    cut = pl.ds(0, z.C // 4)
    take_columns(n, z, range(z.C // 4))
    swap_row_cut(n, n.xa, n.ya, n.xb_s, cut)
    gpatch = dot_tn(n.inputs[...], jnp.concatenate([n.gb[c, n.row] for c in range(z.N)], 0))
    for r in range(z.R):
        n.xp[r] = gpatch[:, r * pw : (r + 1) * pw].astype(bf16)
    swap_row(n, n.xp, n.yp, n.xp_s)
    pl.when(early)(lambda: owner_share(n, z))
    swap_clip_wait(n, n.ch, n.dh, n.ch_s)
    sh = n.dh[0].astype(f32)
    for i in range(1, z.C):
        sh = sh + n.dh[i].astype(f32)
    n.eh[n.row] = sh
    share_row(n, n.eh, n.eh_s)
    swap_row_cut_wait(n, n.xa, n.ya, n.xb_s, cut)
    n.ca[cut] = row_total(n, n.xa, n.ya, cut).astype(bf16)
    swap_owner(n, z, True)
    swap_row_wait(n, n.xp, n.yp, n.xp_s)
    n.cp[...] = row_total(n, n.xp, n.yp, slice(None)).reshape(z.C, pr, pw).astype(n.cp.dtype)
    swap_clip(n, n.cp, n.dp, n.cp_s)
    n.dp[n.clip] = n.cp[n.clip]
    pl.when(early)(lambda: owner_grads(n, z))
    reduce_late(n, z)
    pl.when(late)(lambda: owner_share(n, z))
    reduce_end(n, z, "d")
    pl.when(late)(lambda: owner_grads(n, z))
    swap_owner_sent(n, z)
    swap_clip_wait(n, n.cp, n.dp, n.cp_s)
    sp = n.dp[0].astype(f32)
    for i in range(1, z.C):
        sp = sp + n.dp[i].astype(f32)
    n.ep[n.row] = sp
    share_row(n, n.ep, n.ep_s)
    n.squares[...] += fold(sp) + fold(sh)
    reduce_end(n, z, "g")
    swap_clip_wait(n, n.gc, n.gd, n.gc_s)
    total = n.gc[n.clip]
    for p in n.clip_peer:
        total = total + n.gd[p]
    pre = n.pre[pl.ds(pl.multiple_of(n.clip * PAD, PAD), PAD), :]
    sig = 1.0 / (1.0 + jnp.exp(-pre))
    n.gl[n.clip] = (total * (sig * (1.0 + pre * (1.0 - sig)))).astype(bf16)
    share_clip(n, n.gl, n.gl_s)
    reduce_end(n, z, "o")
    reduce_end(n, z, "p")
    share_row_wait(n, n.eh, n.eh_s)
    share_row_wait(n, n.ep, n.ep_s)
    for r in range(z.R):
        n.gpatch[:, r * pw : (r + 1) * pw] = n.ep[r]
        n.gheads[r * hr : (r + 1) * hr, :] = n.eh[r]
    share_clip_wait(n, n.gl, n.gl_s)
    n.glv[...] = dot_tn(flat(n.ea[...]), flat(n.gl[...]))
    glevel = n.glv[pl.ds(pl.multiple_of(n.clip * z.LR, z.LR), z.LR), :]
    n.glevel[...] = glevel
    n.squares[...] += fold(glevel)


def phase_stats(n, z):
    lines = [jnp.sum(ref[...], 0, keepdims=True) for ref in (n.squares, n.loss, n.weight)]
    n.sa[n.row] = jnp.concatenate(lines + [jnp.zeros((5, 128), f32)], 0)
    share_row(n, n.sa, n.sa_s)
    share_row_wait(n, n.sa, n.sa_s)
    total = n.sa[0]
    for r in range(1, z.R):
        total = total + n.sa[r]
    n.sc[n.clip] = total
    share_clip(n, n.sc, n.sc_s)
    share_clip_wait(n, n.sc, n.sc_s)
    total = n.sc[0]
    for i in range(1, z.C):
        total = total + n.sc[i]
    n.stats[...] = total


LOADED = ("Wd", "gu", "gf", "Wg", "stream", "branch", "gmid", "act", "two", "Wo", "q", "k", "v", "att", "lse", "Wp", "one")
LATER = ("mod", "gad", "tab", "ghead", "w_adapt", "inputs", "cond", "ea", "pre")


def reduce_start(n, z, x):
    reduce_one(n, z, getattr(n, "W" + x), getattr(n, "S" + x), getattr(n, "S" + x + "_s"))


def reduce_middle(n, z, x):
    part, rx = getattr(n, "W" + x), getattr(n, "R" + x)
    width = 2 * z.HW if x == "p" else part.shape[2]
    reduce_two(n, z, part, getattr(n, "S" + x), getattr(n, "S" + x + "_s"), rx, getattr(n, "R" + x + "_s"), width, x == "g" and n.line)


def reduce_end(n, z, x):
    def put(total):
        if x == "p":
            for k in range(3):
                n.Gp[k] = total[:, k * z.HW : (k + 1) * z.HW]
        elif x == "g":
            tiles = z.FH // 128
            for t in range(tiles):
                for k in range(2):
                    at = k * z.FH + t * 128
                    n.Gg[pl.ds(2 * t + k, z.DR, stride=2 * tiles), :] = total[:, at : at + 128]
        else:
            getattr(n, "G" + x)[...] = jnp.transpose(total)

    reduce_three(n, z, getattr(n, "W" + x), getattr(n, "R" + x), getattr(n, "R" + x + "_s"), put, x == "p", x == "g")


def backward_body(n, z):
    for name in LOADED + LATER:
        if name not in ("one", "two"):
            fetch(n, name).start()
    n.squares[...] = jnp.zeros_like(n.squares)
    if n.line:
        for k, p in enumerate(n.core_peer):

            @pl.when(skipped(n, z, p, True))
            def _():
                n.Rg[k] = jnp.zeros_like(n.Rg[k])

    enter(n, z)
    phase_pull_feed(n, z)
    fetch(n, "act").wait()
    weight_grad(n, z, n.gf, n.act, n.Wd)
    load_two = pltpu.make_async_copy(n.two_i, n.gf, n.in_s.at[LOADED.index("two")])
    load_two.start()
    reduce_start(n, z, "d")
    scatter_more(n, n.sb, n.rsr, n.gt_s, 0)
    phase_pull_two(n, z)
    load_two.wait()
    weight_grad(n, z, n.gf, n.gu, n.Wg)
    load_one = pltpu.make_async_copy(n.one_i, n.gf, n.in_s.at[LOADED.index("one")])
    load_one.start()
    reduce_start(n, z, "g")
    phase_pull_attend(n, z)
    load_one.wait()
    weight_grad(n, z, n.gf, n.gp, n.Wp)
    scatter_more(n, n.sb, n.rsr, n.go_s, 0)
    reduce_start(n, z, "p")
    weight_grad(n, z, n.gb, n.att, n.Wo)
    reduce_start(n, z, "o")
    reduce_middle(n, z, "p")
    reduce_middle(n, z, "o")
    phase_pull_one(n, z)
    phase_small(n, z)
    phase_stats(n, z)


def backward_call(z, kept, ins):
    sh = shapes_of(z)
    pr, hr, pw = z.PF // z.C, z.DR // z.R, D // z.R
    head_type = f32 if hr % 16 else bf16
    patch_type = f32 if pr % 16 else bf16
    widths = {"p": 3 * z.HW, "o": z.HW, "g": 2 * z.FH, "d": z.FH}
    outs = {
        "Gp": ((3, z.DR, z.HW), f32),
        "Go": ((z.HW, z.DR), f32),
        "Gg": ((z.DR * 2 * z.FH // 128, 128), f32),
        "Gd": ((z.FH, z.DR), f32),
    }
    outs.update(
        gpatch=((pr, D), f32),
        gheads=((z.DR, z.PF), f32),
        gadapt=((z.LW, z.AW), f32),
        glevel=((z.LR, z.LW), f32),
        stats=((8, 128), f32),
    )
    anys = {k + "_i": kept[k] for k in LOADED}
    anys.update({k + "_i": ins[k] for k in LATER})
    scratch = vm(sh, [k for k in LOADED if k not in ("one", "two")] + ["gb", "sb", "rsr"])
    scratch.update({k: pltpu.VMEM(ins[k].shape, ins[k].dtype) for k in LATER})
    ins = {k: v for k, v in ins.items() if k not in LATER}
    for x, w in widths.items():
        scratch["S" + x] = pltpu.VMEM((z.C // 2, z.DR, w), bf16)
        scratch["R" + x] = pltpu.VMEM((z.C // 2 - 1, z.DR, w), bf16)
    extra = dict(
        tb=((D // max(2, z.W // 192), z.N * z.W), bf16),
        do=((z.HD, z.W, HSIZE), bf16),
        delta=((z.HD, 8, z.W), f32),
        dq=((z.HD, z.W, HSIZE), f32),
        dkv=((z.HD, z.N, z.W, 2 * HSIZE), f32),
        gp=((z.N, z.W, 3 * z.HW), bf16),
        squares=((8, 128), f32),
        xa=((z.R, z.C, PAD, z.aw), f32),
        ya=((z.R, z.C, PAD, z.aw), f32),
        xp=((z.R, z.PF, pw), bf16),
        yp=((z.R, z.PF, pw), bf16),
        xh=((z.R, z.C, hr, z.PF), head_type),
        yh=((z.R, z.C, hr, z.PF), head_type),
        ca=((z.C, PAD, z.aw), bf16),
        da=((z.C, PAD, z.aw), bf16),
        cp=((z.C, pr, pw), patch_type),
        dp=((z.C, pr, pw), patch_type),
        ch=((z.C, hr, z.PF), head_type),
        dh=((z.C, hr, z.PF), head_type),
        ea2=((z.R, z.C * PAD, z.aw), bf16),
        ep=((z.R, pr, pw), f32),
        eh=((z.R, hr, z.PF), f32),
        gc=((z.C, PAD, z.LW), f32),
        gd=((z.C, PAD, z.LW), f32),
        gl=((z.C, PAD, z.LW), bf16),
        glv=((TF, z.LW), f32),
        sa=((z.R, 8, 128), f32),
        sc=((z.C, 8, 128), f32),
    )
    scratch.update(vm(extra, extra))
    dma = pltpu.SemaphoreType.DMA
    if z.C == 8:
        scratch["Xg"] = pltpu.VMEM((z.DR, 2 * z.FH), bf16)
        scratch["Xg_s"] = dma((2,))
    scratch["Rv_s"] = dma((2, z.C // 2))
    scratch["in_s"] = dma((len(LOADED + LATER),))
    for x in widths:
        scratch["S" + x + "_s"] = dma((2, z.C // 2))
        scratch["R" + x + "_s"] = dma((2, z.C // 2))
    for k in ("gt_s", "gb_s", "go_s"):
        scratch[k] = dma((2, z.N, max(6, z.R)))
    for k in ("xa_s", "xb_s", "xp_s", "xh_s", "ea2_s", "ep_s", "eh_s", "sa_s"):
        scratch[k] = dma((2, z.R))
    for k in ("ca_s", "cp_s", "ch_s", "gc_s", "gl_s", "sc_s"):
        scratch[k] = dma((2, z.C))
    return run(backward_body, z, 1, ins, anys, outs, scratch, (), 64 << 20)


WEIGHTS = ("patch", "level", "adapt", "project", "output", "gateup", "down", "head")


def packed(x):
    rows, pair, width = x.shape
    return jnp.transpose(x.reshape(rows, pair, width // 128, 128), (0, 2, 1, 3)).reshape(-1, 128)


def unpacked(x, shape):
    rows, pair, width = shape
    return jnp.transpose(x.reshape(rows, width // 128, pair, 128), (0, 2, 1, 3)).reshape(shape)


def to_kernel(values):
    values = list(values)
    values[3] = jnp.transpose(values[3], (1, 0, 2))
    values[5] = packed(values[5])
    return values


def from_kernel(values, gateup_shape):
    values = list(values)
    values[3] = jnp.transpose(values[3], (1, 0, 2))
    values[5] = unpacked(values[5], gateup_shape)
    return values


def adam_kernel(pf, stats, *refs):
    grads, masters, firsts, seconds = (refs[8 * i : 8 * i + 8] for i in range(4))
    scalars = refs[32:35]
    news, means, squares = (refs[35 + 8 * i : 43 + 8 * i] for i in range(3))
    weight_sum = jnp.sum(stats[2:3])
    grad_norm = jnp.sqrt(jnp.full((8, 128), jnp.sum(stats[0:1]))) / weight_sum
    factor = jnp.minimum(1.0, clip_level / (grad_norm + 1e-06)) / weight_sum
    scalars[0][0, 0] = jnp.sum(stats[1:2]) / pf
    scalars[1][0, 0] = weight_sum
    scalars[2][0, 0] = jnp.max(grad_norm)
    factor = factor[:1, :1]
    for g, m, f, s, new, mean, square in zip(grads, masters, firsts, seconds, news, means, squares):
        grad = g[...] * factor
        first_new = beta_one * f[...] + (1.0 - beta_one) * grad
        second_new = beta_two * s[...] + (1.0 - beta_two) * grad * grad
        first_hat = first_new * (1.0 / (1.0 - beta_one**STEP))
        second_hat = second_new * (1.0 / (1.0 - beta_two**STEP))
        master = m[...]
        new[...] = master - learn_rate * (first_hat / (jnp.sqrt(second_hat) + adam_eps) + decay_rate * master)
        mean[...] = first_new
        square[...] = second_new


def adam_call(z, stats, grads, masters, firsts, seconds):
    steps = 2
    split = (None, None, 0, 1, 0, 0, 0, 0)

    def spec(x, axis):
        if axis is None:
            return pl.BlockSpec(x.shape, lambda i: (0,) * x.ndim)
        block = tuple(d // steps if k == axis else d for k, d in enumerate(x.shape))
        return pl.BlockSpec(block, lambda i: tuple(i if k == axis else 0 for k in range(x.ndim)))

    specs = [spec(x, axis) for x, axis in zip(masters, split)]
    shapes = [jax.ShapeDtypeStruct(x.shape, f32) for x in masters]
    scalar = jax.ShapeDtypeStruct((1, 1), f32)
    result = pl.pallas_call(
        functools.partial(adam_kernel, z.PF),
        grid=(steps,),
        out_shape=[scalar] * 3 + shapes * 3,
        in_specs=[pl.BlockSpec(stats.shape, lambda i: (0, 0))] + specs * 4,
        out_specs=[pl.BlockSpec((1, 1), lambda i: (0, 0), memory_space=pltpu.SMEM)] * 3 + specs * 3,
        compiler_params=pltpu.CompilerParams(vmem_limit_bytes=64 << 20),
    )(stats, *grads, *masters, *firsts, *seconds)
    return result[:3], result[3:11], result[11:19], result[19:27]


def on_device(latents, noise, levels, *weights):
    masters, firsts, seconds = weights[:8], weights[8:16], weights[16:]
    a = dict(zip(["w_" + k for k in WEIGHTS], masters))
    a.update(latents=latents, noise=noise, levels=levels)
    z = sizes_of(latents, lax.axis_size("clip"), lax.axis_size("row"))
    ins = forward_inputs(z, a)
    kept = forward_call(z, ins)
    back = {k: kept[k] for k in ("gad", "ghead", "loss", "weight", "pre", "cond", "ea", "mod")}
    back.update({k: ins[k] for k in ("w_adapt", "inputs", "tab")})
    g = backward_call(z, kept, back)
    grads = (g["gpatch"], g["glevel"], g["gadapt"], g["Gp"], g["Go"], g["Gg"], g["Gd"], g["gheads"])
    scalars, *results = adam_call(z, g["stats"], grads, *(to_kernel(x) for x in (masters, firsts, seconds)))
    results = [from_kernel(x, masters[5].shape) for x in results]
    return tuple(x.reshape(()) for x in scalars) + tuple(x for result in results for x in result)


def solution(mesh):
    tokens = P("clip", None, "row", None, None)
    by_clip = P("clip", None)
    weights = (by_clip, P("clip", "row"), P("row", "clip"), P("clip", None, "row"), P("row", "clip"))
    weights = weights + (P("clip", None, "row"), P("row", "clip"), by_clip)
    return jax.shard_map(
        on_device,
        mesh=mesh,
        in_specs=(tokens, tokens, by_clip) + weights * 3,
        out_specs=(P(), P(), P()) + weights * 3,
        check_vma=False,
    )
```
